32 devices in a mesh: dp: 8 (over z, core), aa: 2 (over x), ba: 2 (over y).
Axes of the slice: x: 2, y: 2, z: 4, core: 2. Of those that a mesh axis runs over, the one named last changes fastest.
Arguments:
- frames: bfloat16 [32, 1024, 512], P(('dp', 'aa', 'ba')), may hold values from -6 to 6
- segment_ids: int32 [32, 1024], P(('dp', 'aa', 'ba')), may hold values from 0 to 3, never falling along the last dimension, each value on 1 to 512 neighbouring positions
- cotangent: bfloat16 [32, 1024, 512], P(('dp', 'aa', 'ba')), may hold values from -30 to 30
- first_gain: bfloat16 [512], replicated, may hold values from 0.25 to 1.75
- first_shift: bfloat16 [512], replicated, may hold values from -2.5 to 2.5
- query_weight: bfloat16 [512, 512], P(None, ('aa', 'ba')), may hold values from -0.5 to 0.5
- query_bias: bfloat16 [512], P(('aa', 'ba')), may hold values from -2.5 to 2.5
- key_weight: bfloat16 [512, 512], P(None, ('aa', 'ba')), may hold values from -0.25 to 0.25
- value_weight: bfloat16 [512, 512], P(None, ('aa', 'ba')), may hold values from -0.25 to 0.25
- value_bias: bfloat16 [512], P(('aa', 'ba')), may hold values from -2.5 to 2.5
- out_weight: bfloat16 [512, 512], P(('aa', 'ba')), may hold values from -0.75 to 0.75
- out_bias: bfloat16 [512], replicated, may hold values from -2.5 to 2.5
- second_gain: bfloat16 [512], replicated, may hold values from 0.25 to 1.75
- second_shift: bfloat16 [512], replicated, may hold values from -2.5 to 2.5
- up_weight: bfloat16 [512, 2048], P(None, ('aa', 'ba')), may hold values from -0.25 to 0.25
- up_bias: bfloat16 [2048], P(('aa', 'ba')), may hold values from -2.5 to 2.5
- down_weight: bfloat16 [2048, 512], P(('aa', 'ba')), may hold values from -0.125 to 0.125
- down_bias: bfloat16 [512], replicated, may hold values from -2.5 to 2.5
Outputs:
- layer_output: bfloat16 [32, 1024, 512], P(('dp', 'aa', 'ba'))
- frames_delta: bfloat16 [32, 1024, 512], P(('dp', 'aa', 'ba'))
- first_gain_delta: float32 [512], replicated
- first_shift_delta: float32 [512], replicated
- query_weight_delta: float32 [512, 512], P(None, ('aa', 'ba'))
- query_bias_delta: float32 [512], P(('aa', 'ba'))
- key_weight_delta: float32 [512, 512], P(None, ('aa', 'ba'))
- value_weight_delta: float32 [512, 512], P(None, ('aa', 'ba'))
- value_bias_delta: float32 [512], P(('aa', 'ba'))
- out_weight_delta: float32 [512, 512], P(('aa', 'ba'))
- out_bias_delta: float32 [512], replicated
- second_gain_delta: float32 [512], replicated
- second_shift_delta: float32 [512], replicated
- up_weight_delta: float32 [512, 2048], P(None, ('aa', 'ba'))
- up_bias_delta: float32 [2048], P(('aa', 'ba'))
- down_weight_delta: float32 [2048, 512], P(('aa', 'ba'))
- down_bias_delta: float32 [512], replicated
The draws below stay inside these ranges and needn't reach their ends.
Inputs may be any that keep to these rules, and one draw needn't show every extreme that they name: `segment_ids`: in each window the clip numbers never fall and every number from 0 to 3 appears; each clip covers 1 to 512 frames and one clip exactly 512.
All inputs are finite; a program needn't handle non-finite values.
Results may differ from the reference program's by a relative error of at most 0.02.
Values may be sent and summed in bfloat16 or wider, within the bound.
No kernel may reach another device: no remote copies, remote signals or barrier semaphores. Data moves between devices by JAX's collectives and lax.ppermute only.
A program may use at most 256 MiB of HBM per device.

```python
import math
import jax
import jax.numpy as jnp
import numpy as np
from jax import lax

D = 512
HEADS = 8
HEAD_DIM = 64
FF = 2048
L = 1024
SEGS = 4
WINDOWS = 32


def draw_cotangent(key, part):
    key = jax.random.fold_in(key, 7)
    place = jnp.arange(WINDOWS, dtype=jnp.float32) / max(WINDOWS - 1, 1)
    rising = (1.0 + 2.0 * place)[:, None, None]
    drawn = jax.random.truncated_normal(key, -4.0, 4.0, (WINDOWS, L, D), jnp.float32) * rising
    return jnp.clip(drawn, -30.0, 30.0).astype(jnp.bfloat16)


def levels(rng, dims, cuts, low, high):
    factor_of = 1.0
    for axis_at, shards_of in cuts:
        steps = jax.random.uniform(jax.random.fold_in(jax.random.fold_in(rng, 6), axis_at), (shards_of,), jnp.float32, low / len(cuts), high / len(cuts))
        factor_of = factor_of * jnp.repeat(jnp.exp(steps), dims[axis_at] // shards_of).reshape((-1,) + (1,) * (len(dims) - 1 - axis_at))
    return factor_of


def profile(amount, total, bound, slope):
    weights = [(1 << 20) // math.isqrt(rank ** slope) + 1 for rank in range(2, amount + 1)]
    rest, given = total - bound - (amount - 1), [1] * (amount - 1)
    while rest > 0:
        free = [i for i in range(amount - 1) if given[i] < bound]
        pool, left = sum([weights[i] for i in free]), rest
        for i in free:
            extra = min(bound - given[i], max(1, left * weights[i] // pool), rest)
            given[i] = given[i] + extra
            rest = rest - extra
    return np.array([bound] + given)


def ragged(rng, amount, total, limit, skew):
    if amount == 2:
        one = jax.random.randint(rng, (), max(1, total - limit), min(limit, total - 1) + 1)
        return jnp.stack([one, total - one])
    sizes = jnp.asarray(profile(amount, total, limit, skew), jnp.int32)
    twos = (amount - 1) // 2
    source_of, taker = sizes[1:1 + 2 * twos:2], sizes[2:2 + 2 * twos:2]
    margin = jnp.minimum(source_of - 1, limit - taker)
    shifted = jax.random.randint(jax.random.fold_in(rng, 1), (twos,), 0, 1 << 20) % (margin + 1)
    sizes = sizes.at[1:1 + 2 * twos:2].set(source_of - shifted).at[2:2 + 2 * twos:2].set(taker + shifted)
    return sizes[jax.random.permutation(jax.random.fold_in(rng, 2), amount)]


def gaussian(own_key, extent, deviation, bound, shards=(), kind=jnp.bfloat16):
    values = jax.random.normal(own_key, extent, jnp.float32) * deviation
    if len(shards) > 0:
        values = levels(own_key, extent, shards, -0.22, 0.18) * values
    return jnp.clip(values, min=-bound, max=bound).astype(kind)


def setup_inputs(seed: int = 0) -> dict:
    streams_of = jax.random.split(jax.random.key(seed), 19)
    frames = gaussian(streams_of[0], (WINDOWS, L, D), 1.0, 6.0, ((0, 32),))
    segment_ids = jax.vmap(lambda own: jnp.searchsorted(jnp.cumsum(ragged(own, SEGS, L, L // 2, 0)), jnp.arange(L), side="right"))(jax.random.split(streams_of[1], WINDOWS)).reshape((WINDOWS, L)).astype(jnp.int32)
    cotangent = draw_cotangent(jax.random.fold_in(streams_of[18], 71), 0)
    first_gain = jnp.clip(1.0 + 0.15 * jax.random.normal(streams_of[3], (D,), jnp.float32), 0.25, 1.75).astype(jnp.bfloat16)
    first_shift = gaussian(streams_of[4], (D,), 0.3, 2.5)
    query_weight = gaussian(streams_of[5], (D, D), (D // 4) ** -0.5, 0.5, ((1, 4),))
    query_bias = gaussian(streams_of[6], (D,), 0.3, 2.5, ((0, 4),))
    key_weight = gaussian(streams_of[7], (D, D), D ** -0.5, 0.25, ((1, 4),))
    value_weight = gaussian(streams_of[8], (D, D), D ** -0.5, 0.25, ((1, 4),))
    value_bias = gaussian(streams_of[9], (D,), 0.3, 2.5, ((0, 4),))
    out_weight = gaussian(streams_of[10], (D, D), (D // 8) ** -0.5, 0.75, ((0, 4),))
    out_bias = gaussian(streams_of[11], (D,), 0.3, 2.5)
    second_gain = jnp.clip(1.0 + 0.15 * jax.random.normal(streams_of[12], (D,), jnp.float32), 0.25, 1.75).astype(jnp.bfloat16)
    second_shift = gaussian(streams_of[13], (D,), 0.3, 2.5)
    up_weight = gaussian(streams_of[14], (D, FF), D ** -0.5, 0.25, ((1, 4),))
    up_bias = gaussian(streams_of[15], (FF,), 0.3, 2.5, ((0, 4),))
    down_weight = gaussian(streams_of[16], (FF, D), FF ** -0.5, 0.125, ((0, 4),))
    down_bias = gaussian(streams_of[17], (D,), 0.3, 2.5)
    return {"frames": frames, "segment_ids": segment_ids, "cotangent": cotangent, "first_gain": first_gain, "first_shift": first_shift, "query_weight": query_weight, "query_bias": query_bias, "key_weight": key_weight, "value_weight": value_weight, "value_bias": value_bias, "out_weight": out_weight, "out_bias": out_bias, "second_gain": second_gain, "second_shift": second_shift, "up_weight": up_weight, "up_bias": up_bias, "down_weight": down_weight, "down_bias": down_bias}


EPSILON = 1e-05
MASKED = -1e+30

@jax.custom_vjp
def low(v):
    return lax.optimization_barrier(v.astype(jnp.bfloat16)).astype(jnp.float32)

@jax.custom_vjp
def low_back(v):
    return v

def low_keep(v):
    return (low(v), None)

def low_pass(kept, grad):
    return (grad,)

def back_keep(v):
    return (v, None)

def back_low(kept, grad):
    return (low(grad),)
low.defvjp(low_keep, low_pass)
low_back.defvjp(back_keep, back_low)

def matmul(left, right):
    return jnp.dot(left, right, precision=lax.Precision.HIGHEST, preferred_element_type=jnp.float32)

def layer_norm(values, gain, shift):
    centre = lax.optimization_barrier(jnp.mean(values, axis=-1, keepdims=True))
    offset = values - centre
    spread = lax.optimization_barrier(jnp.mean(offset * offset, axis=-1, keepdims=True))
    return offset * lax.rsqrt(spread + EPSILON) * gain + shift

def window_layer(params, frame_rows, labels):
    gain_one, shift_one, query_weight, query_bias, key_weight, value_weight, value_bias, out_weight, out_bias, gain_two, shift_two, up_weight, up_bias, down_weight, down_bias = params
    normed = low(layer_norm(frame_rows, gain_one, shift_one))
    query = low(low_back(HEAD_DIM ** (-0.5) * (matmul(normed, query_weight) + query_bias)))
    keys = low(low_back(matmul(normed, key_weight)))
    values = low(low_back(matmul(normed, value_weight) + value_bias))
    query_heads = query.reshape(L, HEADS, HEAD_DIM)
    key_heads = keys.reshape(L, HEADS, HEAD_DIM)
    value_heads = values.reshape(L, HEADS, HEAD_DIM)
    raw_scores = jnp.einsum('qhd,khd->hqk', query_heads, key_heads, precision=lax.Precision.HIGHEST)
    same_clip = labels[:, None] == labels[None, :]
    scores = jnp.where(same_clip[None, :, :], low_back(raw_scores), MASKED)
    row_peak = lax.optimization_barrier(jnp.max(scores, axis=-1, keepdims=True))
    raised = jnp.exp(scores - row_peak)
    key_weights = raised / lax.optimization_barrier(jnp.sum(raised, axis=-1, keepdims=True))
    mixed = jnp.einsum('hqk,khd->qhd', low(key_weights), value_heads, precision=lax.Precision.HIGHEST)
    mixed = low(low_back(mixed.reshape(L, D)))
    inner = frame_rows + low_back(matmul(mixed, out_weight) + out_bias)
    normed_two = low(layer_norm(inner, gain_two, shift_two))
    up_linear = low_back(matmul(normed_two, up_weight) + up_bias)
    activated = low(jax.nn.gelu(up_linear, approximate=False))
    return inner + low_back(matmul(activated, down_weight) + down_bias)

def all_windows(params, frames_all, labels_all):
    layer = jax.checkpoint(window_layer)

    def window_step(state_in, window_item):
        return (state_in, layer(params, window_item[0], window_item[1]))
    unused, outputs = lax.scan(window_step, jnp.zeros((), jnp.float32), (frames_all, labels_all))
    return outputs

def reference(frames, segment_ids, cotangent, first_gain, first_shift, query_weight, query_bias, key_weight, value_weight, value_bias, out_weight, out_bias, second_gain, second_shift, up_weight, up_bias, down_weight, down_bias):
    params = (first_gain.astype(jnp.float32), first_shift.astype(jnp.float32), query_weight.astype(jnp.float32), query_bias.astype(jnp.float32), key_weight.astype(jnp.float32), value_weight.astype(jnp.float32), value_bias.astype(jnp.float32), out_weight.astype(jnp.float32), out_bias.astype(jnp.float32), second_gain.astype(jnp.float32), second_shift.astype(jnp.float32), up_weight.astype(jnp.float32), up_bias.astype(jnp.float32), down_weight.astype(jnp.float32), down_bias.astype(jnp.float32))
    frames_wide = frames.astype(jnp.float32)

    def forward(param_set, inputs):
        return all_windows(param_set, inputs, segment_ids)
    outputs, backward = jax.vjp(forward, params, frames_wide)
    param_deltas, frames_delta = backward(cotangent.astype(jnp.float32))
    return (outputs.astype(jnp.bfloat16), frames_delta.astype(jnp.bfloat16), param_deltas[0], param_deltas[1], param_deltas[2], param_deltas[3], param_deltas[4], param_deltas[5], param_deltas[6], param_deltas[7], param_deltas[8], param_deltas[9], param_deltas[10], param_deltas[11], param_deltas[12], param_deltas[13], param_deltas[14])
```

```python
import functools

import jax
import jax.numpy as jnp
from jax import lax
from jax.experimental import pallas as pl
from jax.experimental.pallas import tpu as pltpu
from jax.sharding import PartitionSpec as P

HEAD_DIM = 64
PAIR = 2 * HEAD_DIM
BLOCK = 128
ROWS = 256
EPSILON = 1e-05
MASKED = -1e30
SPANS = (2, 3, 4, 5, 6, 8)

F32 = jnp.float32
BF16 = jnp.bfloat16
NN = (((1,), (0,)), ((), ()))
NT = (((1,), (1,)), ((), ()))
TN = (((0,), (0,)), ((), ()))
VMEM = pl.BlockSpec(memory_space=pltpu.VMEM)
SMEM = pl.BlockSpec(memory_space=pltpu.SMEM)
LIMIT = 60 * 1024 * 1024


def dot(left, right, dims=NN):
    return lax.dot_general(left, right, dims, preferred_element_type=F32)


def call(body, out_shape, in_specs, scratch, flops, *args):
    moved = sum(a.size * a.dtype.itemsize for a in args)
    moved += sum(o.size * o.dtype.itemsize for o in out_shape)
    return pl.pallas_call(
        body,
        out_shape=out_shape,
        in_specs=in_specs,
        out_specs=[VMEM] * len(out_shape),
        scratch_shapes=scratch,
        compiler_params=pltpu.CompilerParams(vmem_limit_bytes=LIMIT),
        cost_estimate=pl.CostEstimate(flops=int(flops), bytes_accessed=int(moved), transcendentals=0),
    )(*args)


def shape(dims, dtype):
    return jax.ShapeDtypeStruct(dims, dtype)


def centred(values):
    centre = jnp.mean(values, axis=-1, keepdims=True)
    offset = values - centre
    spread = jnp.mean(offset * offset, axis=-1, keepdims=True)
    scale = lax.rsqrt(spread + EPSILON)
    return offset * scale, scale


def lane_of(dims):
    return lax.broadcasted_iota(jnp.int32, dims, 1)


def key_range(lab_s, at, blocks):
    first = lab_s[0, at * BLOCK]
    last = lab_s[0, at * BLOCK + BLOCK - 1]
    low = jnp.int32(0)
    high = jnp.int32(blocks)
    for b in range(blocks):
        low += (lab_s[0, b * BLOCK + BLOCK - 1] < first).astype(jnp.int32)
        high -= (lab_s[0, b * BLOCK] > last).astype(jnp.int32)
    return low, high - low


def each_query_block(lab_s, blocks, body):
    spans = [s for s in SPANS if s < blocks] + [blocks]

    def step(at, carry):
        low, count = key_range(lab_s, at, blocks)
        under = 0
        for span in spans:
            base = jnp.minimum(low, blocks - span)

            @pl.when((count > under) & (count <= span))
            def _():
                body(at, base, span)

            under = span
        return carry

    lax.fori_loop(0, blocks, step, 0)


def fill_heads(rows_at, wide, masked_to, pair):
    lane = lane_of(wide.shape)
    zero = jnp.zeros_like(wide)
    for part in range(wide.shape[0] // BLOCK):
        piece = wide[part * BLOCK : (part + 1) * BLOCK]
        for head in range(2):
            keep = (lane[:BLOCK] < HEAD_DIM) if head == 0 else (lane[:BLOCK] >= HEAD_DIM)
            at = 2 * rows_at + (2 * part + head) * BLOCK
            masked_to[pair, pl.ds(at, BLOCK), :PAIR] = jnp.where(keep, piece, zero[:BLOCK])


def attend_kernel(groups, first, *refs):
    refs = list(refs)
    lab_s, lab_c, x_ref = refs[:3]
    refs = refs[3:]
    if first:
        gain, shift = refs[:2]
        refs = refs[2:]
    weights, biases = refs[:groups], refs[groups : 2 * groups]
    refs = refs[2 * groups :]
    if first:
        normed_ref, normed_t = refs[:2]
        refs = refs[2:]
    qkv = refs[:groups]
    mixed_ref, mixed_t, lse_ref, qm, ke, vt = refs[groups:]
    length = x_ref.shape[0]
    blocks = length // BLOCK

    def prepare(tile, carry):
        at = pl.multiple_of(tile * ROWS, ROWS)
        rows = pl.ds(at, ROWS)
        if first:
            xhat, _ = centred(x_ref[rows, :].astype(F32))
            x = (xhat * gain[...] + shift[...]).astype(BF16)
            normed_ref[rows, :] = x
            normed_t[:, rows] = x.T
        else:
            x = x_ref[rows, :]
        same = lane_of((ROWS, BLOCK)) == lab_c[rows, :]
        hot = jnp.where(same, 1.0, 0.0).astype(BF16)
        cold = jnp.where(same, 0.0, MASKED).astype(BF16)
        for g in range(groups):
            y = dot(x, weights[g][...]) + biases[g][...]
            q = (y[:, :PAIR] * HEAD_DIM ** (-0.5)).astype(BF16)
            k = y[:, PAIR : 2 * PAIR].astype(BF16)
            v = y[:, 2 * PAIR :].astype(BF16)
            qkv[g][rows, :PAIR] = q
            qkv[g][rows, PAIR : 2 * PAIR] = k
            qkv[g][rows, 2 * PAIR :] = v
            fill_heads(at, q, qm, g)
            for part in range(ROWS // BLOCK):
                for head in range(2):
                    to = pl.ds(2 * at + (2 * part + head) * BLOCK, BLOCK)
                    qm[g, to, PAIR:] = hot[part * BLOCK : (part + 1) * BLOCK]
            ke[g, rows, :PAIR] = k
            ke[g, rows, PAIR:] = cold
            vt[g, :, rows] = v.T
        return carry

    lax.fori_loop(0, length // ROWS, prepare, 0)

    def body(at, base, span):
        keys = pl.ds(pl.multiple_of(base * BLOCK, BLOCK), span * BLOCK)
        rows = pl.ds(pl.multiple_of(at * BLOCK, BLOCK), BLOCK)
        both = pl.ds(pl.multiple_of(at * 2 * BLOCK, 2 * BLOCK), 2 * BLOCK)
        for g in range(groups):
            scores = dot(ke[g, keys, :], qm[g, both, :], NT)
            peak = jnp.max(scores, axis=0, keepdims=True)
            raised = jnp.exp(scores - peak)
            total = jnp.sum(raised, axis=0, keepdims=True)
            out = dot(vt[g, :, keys], raised.astype(BF16)) * (1.0 / total)
            out = jnp.concatenate([out[:HEAD_DIM, :BLOCK], out[HEAD_DIM:, BLOCK:]], axis=0)
            mixed_t[g * PAIR : (g + 1) * PAIR, rows] = out.astype(BF16)
            mixed_ref[rows, g * PAIR : (g + 1) * PAIR] = out.T.astype(BF16)
            lse = peak + jnp.log(total)
            lse_ref[2 * g : 2 * g + 1, rows] = lse[:, :BLOCK]
            lse_ref[2 * g + 1 : 2 * g + 2, rows] = lse[:, BLOCK:]

    each_query_block(lab_s, blocks, body)


def attend(lab_s, lab_c, x, norm, weights, biases):
    groups = len(weights)
    length, width = x.shape
    first = norm is not None
    outs = [shape((length, width), BF16), shape((width, length), BF16)] if first else []
    outs += [shape((length, 3 * PAIR), BF16)] * groups
    outs += [
        shape((length, groups * PAIR), BF16),
        shape((groups * PAIR, length), BF16),
        shape((2 * groups, length), F32),
    ]
    args = [lab_s, lab_c, x] + (list(norm) if first else []) + list(weights) + list(biases)
    scratch = [
        pltpu.VMEM((groups, 2 * length, 2 * PAIR), BF16),
        pltpu.VMEM((groups, length, 2 * PAIR), BF16),
        pltpu.VMEM((groups, PAIR, length), BF16),
    ]
    flops = groups * (2 * length * width * 3 * PAIR + 8 * length * length * PAIR)
    got = call(
        functools.partial(attend_kernel, groups, first),
        outs,
        [SMEM] + [VMEM] * (len(args) - 1),
        scratch,
        flops,
        *args,
    )
    head = got[:2] if first else []
    got = got[len(head) :]
    return head, got[:groups], got[groups], got[groups + 1], got[groups + 2]


def join_kernel(parts, frames, bias, gain, shift, *refs):
    mixed, weights = refs[:parts], refs[parts : 2 * parts]
    inner_ref, normed_ref, normed_t = refs[2 * parts :]

    def step(tile, carry):
        rows = pl.ds(pl.multiple_of(tile * ROWS, ROWS), ROWS)
        inner = frames[rows, :].astype(F32) + bias[...]
        for m, w in zip(mixed, weights):
            inner += dot(m[rows, :], w[...])
        inner_ref[rows, :] = inner
        xhat, _ = centred(inner)
        normed = (xhat * gain[...] + shift[...]).astype(BF16)
        normed_ref[rows, :] = normed
        normed_t[:, rows] = normed.T
        return carry

    lax.fori_loop(0, frames.shape[0] // ROWS, step, 0)


def join(frames, bias, gain, shift, mixed, weights):
    length, width = frames.shape
    args = [frames, bias, gain, shift] + list(mixed) + list(weights)
    return call(
        functools.partial(join_kernel, len(mixed)),
        [shape((length, width), F32), shape((length, width), BF16), shape((width, length), BF16)],
        [VMEM] * len(args),
        [],
        2 * length * width * width,
        *args,
    )


def gelu_both(u):
    falling = jnp.exp(u * u * -0.5)
    t = 1.0 / (1.0 + jnp.abs(u) * (0.3275911 * 0.5**0.5))
    poly = 0.5 * 1.061405429
    for c in (-1.453152027, 1.421413741, -0.284496736, 0.254829592):
        poly = poly * t + 0.5 * c
    tail = poly * t * falling
    phi = jnp.where(u >= 0.0, 1.0 - tail, tail)
    return u * phi, phi + u * falling * (0.5 / jnp.pi) ** 0.5


def feed_kernel(groups, last, *refs):
    refs = list(refs)
    normed, normed_t, cot, cot_t, out_in, two_in = refs[:6]
    ups, up_biases, downs = (refs[6 + i * groups : 6 + (i + 1) * groups] for i in range(3))
    refs = refs[6 + 3 * groups :]
    out_ref, two_ref = refs[:2]
    up_deltas = refs[2 : 2 + groups]
    down_deltas = refs[2 + groups : 2 + 2 * groups]
    bias_deltas = refs[2 + 2 * groups : 2 + 3 * groups]
    act_s, delta_s = refs[2 + 3 * groups :]
    length = normed.shape[0]
    for g in range(groups):
        bias_deltas[g][...] = jnp.zeros_like(bias_deltas[g])

        def step(tile, carry):
            rows = pl.ds(pl.multiple_of(tile * ROWS, ROWS), ROWS)
            u = dot(normed[rows, :], ups[g][...]) + up_biases[g][...]
            back = dot(cot[rows, :], downs[g][...], NT)
            act, slope = gelu_both(u)
            act = act.astype(BF16)
            delta = (back * slope).astype(BF16)
            act_s[rows, :] = act
            delta_s[rows, :] = delta
            source_out, source_two = (out_in, two_in) if g == 0 else (out_ref, two_ref)
            out_ref[rows, :] = source_out[rows, :] + dot(act, downs[g][...])
            fresh = dot(delta, ups[g][...], NT)
            if g == 0 and two_in is out_in:
                two_ref[rows, :] = fresh
            else:
                two_ref[rows, :] = source_two[rows, :] + fresh
            bias_deltas[g][...] += jnp.sum(delta.astype(F32), axis=0, keepdims=True)
            return carry

        lax.fori_loop(0, length // ROWS, step, 0)
        up_deltas[g][...] = dot(normed_t[...], delta_s[...]).astype(BF16)
        down_deltas[g][...] = dot(cot_t[...], act_s[...]).T.astype(BF16)


def feed(normed, normed_t, cot, cot_t, out_sum, two_sum, ups, up_biases, downs):
    groups = len(ups)
    length, width = normed.shape
    hidden = ups[0].shape[1]
    args = [normed, normed_t, cot, cot_t, out_sum, two_sum] + list(ups) + list(up_biases) + list(downs)
    outs = [shape((length, width), F32)] * 2
    outs += [shape((width, hidden), BF16)] * groups
    outs += [shape((hidden, width), BF16)] * groups
    outs += [shape((1, hidden), F32)] * groups
    got = call(
        functools.partial(feed_kernel, groups, False),
        outs,
        [VMEM] * len(args),
        [pltpu.VMEM((length, hidden), BF16)] * 2,
        12 * groups * length * width * hidden,
        *args,
    )
    return (
        got[0],
        got[1],
        got[2 : 2 + groups],
        got[2 + groups : 2 + 2 * groups],
        got[2 + 2 * groups :],
    )


def turn_kernel(parts, inner_ref, out_ref, down_bias, two_ref, cot, gain, *refs):
    mixed, mixed_t, weights = (refs[i * parts : (i + 1) * parts] for i in range(3))
    refs = refs[3 * parts :]
    layer_ref, delta_ref, sums_ref, inner_rows = refs[:4]
    branch_s = refs[-1]
    out_deltas, delta_mixed = refs[4 : 4 + parts], refs[4 + parts : 4 + 2 * parts]
    length, width = inner_ref.shape
    sums_ref[...] = jnp.zeros_like(sums_ref)
    features = sum(m.shape[1] for m in mixed)
    heads = features // HEAD_DIM

    def step(tile, carry):
        rows = pl.ds(pl.multiple_of(tile * ROWS, ROWS), ROWS)
        inner = inner_ref[rows, :]
        layer_ref[rows, :] = (inner + out_ref[rows, :] + down_bias[...]).astype(BF16)
        xhat, scale = centred(inner)
        two = two_ref[rows, :]
        dy = cot[rows, :].astype(F32)
        e = two * gain[...]
        lean = jnp.mean(e, axis=-1, keepdims=True)
        pull = jnp.mean(e * xhat, axis=-1, keepdims=True)
        delta = dy + scale * (e - lean - xhat * pull)
        delta_ref[rows, :] = delta
        branch = delta.astype(BF16)
        branch_s[rows, :] = branch
        sums_ref[0:1, :] += jnp.sum(two * xhat, axis=0, keepdims=True)
        sums_ref[1:2, :] += jnp.sum(two, axis=0, keepdims=True)
        sums_ref[2:3, :] += jnp.sum(branch.astype(F32), axis=0, keepdims=True)
        sums_ref[3:4, :] += jnp.sum(dy, axis=0, keepdims=True)
        head_at = 0
        for m, w, dm in zip(mixed, weights, delta_mixed):
            back = dot(branch, w[...], NT).astype(BF16)
            dm[rows, :] = back
            product = back.astype(F32) * m[rows, :].astype(F32)
            high = product.astype(BF16)
            low = (product - high.astype(F32)).astype(BF16)
            here = m.shape[1] // HEAD_DIM
            dims = (2 * here, m.shape[1])
            picks = lax.broadcasted_iota(jnp.int32, dims, 0) == lane_of(dims) // HEAD_DIM
            ones = jnp.where(picks, 1.0, 0.0).astype(BF16)
            sums = dot(ones, high, NT) + dot(ones, low, NT)
            inner_rows[head_at : head_at + here, rows] = sums[:here]
            head_at += here
        return carry

    lax.fori_loop(0, length // ROWS, step, 0)
    for mt, od in zip(mixed_t, out_deltas):
        od[...] = dot(mt[...], branch_s[...]).astype(BF16)


def turn(inner, out_sum, down_bias, two_sum, cot, gain, mixed, mixed_t, weights):
    length, width = inner.shape
    parts = len(mixed)
    args = [inner, out_sum, down_bias, two_sum, cot, gain]
    args += list(mixed) + list(mixed_t) + list(weights)
    features = sum(m.shape[1] for m in mixed)
    outs = [
        shape((length, width), BF16),
        shape((length, width), F32),
        shape((8, width), F32),
        shape((features // HEAD_DIM, length), F32),
    ]
    outs += [shape(w.shape, BF16) for w in weights]
    outs += [shape(m.shape, BF16) for m in mixed]
    got = call(
        functools.partial(turn_kernel, parts),
        outs,
        [VMEM] * len(args),
        [pltpu.VMEM((length, width), BF16)],
        4 * length * width * width,
        *args,
    )
    return got[0], got[1], got[2], got[3], got[4 : 4 + parts], got[4 + parts :]


def attend_back_kernel(groups, dm_at, lab_s, lab_c, normed_t, lse_ref, inner_ref, *refs):
    qkv, dms = refs[:groups], refs[groups : 2 * groups]
    refs = refs[2 * groups :]
    deltas, changes, sums = (refs[i * groups : (i + 1) * groups] for i in range(3))
    qm, ke, ve, dmm, kt, dk, dv = refs[3 * groups :]
    length = normed_t.shape[1]
    blocks = length // BLOCK

    def prepare(tile, carry):
        at = pl.multiple_of(tile * ROWS, ROWS)
        rows = pl.ds(at, ROWS)
        same = lane_of((ROWS, BLOCK)) == lab_c[rows, :]
        hot = jnp.where(same, 1.0, 0.0).astype(BF16)
        cold = jnp.where(same, 0.0, MASKED).astype(BF16)
        for g in range(groups):
            q = qkv[g][rows, :PAIR]
            k = qkv[g][rows, PAIR : 2 * PAIR]
            fill_heads(at, q, qm, g)
            for part in range(ROWS // BLOCK):
                for head in range(2):
                    to = pl.ds(2 * at + (2 * part + head) * BLOCK, BLOCK)
                    qm[g, to, PAIR:] = hot[part * BLOCK : (part + 1) * BLOCK]
            fill_heads(at, dms[g][rows, :], dmm, g)
            ke[g, rows, :PAIR] = k
            ke[g, rows, PAIR:] = cold
            ve[g, rows, :] = qkv[g][rows, 2 * PAIR :]
            kt[g, :, rows] = k.T
            dk[g, rows, :] = jnp.zeros((ROWS, PAIR), F32)
            dv[g, rows, :] = jnp.zeros((ROWS, PAIR), F32)
        return carry

    lax.fori_loop(0, length // ROWS, prepare, 0)

    def body(at, base, span):
        rows = pl.ds(pl.multiple_of(at * BLOCK, BLOCK), BLOCK)
        both = pl.ds(pl.multiple_of(at * 2 * BLOCK, 2 * BLOCK), 2 * BLOCK)
        for g in range(groups):
            queries = qm[g, both, :]
            downs = dmm[g, both, :]
            lse = jnp.concatenate([lse_ref[2 * g : 2 * g + 1, rows], lse_ref[2 * g + 1 : 2 * g + 2, rows]], axis=1)
            pull = jnp.concatenate([inner_ref[2 * g : 2 * g + 1, rows], inner_ref[2 * g + 1 : 2 * g + 2, rows]], axis=1)
            dqt = jnp.zeros((PAIR, 2 * BLOCK), F32)
            done = 0
            while done < span:
                size = min(2, span - done)
                keys = pl.ds(pl.multiple_of((base + done) * BLOCK, BLOCK), size * BLOCK)
                scores = dot(ke[g, keys, :], queries, NT)
                probs = jnp.exp(scores - lse)
                slope = dot(ve[g, keys, :], downs, NT)
                delta = (probs * (slope - pull)).astype(BF16)
                dv[g, keys, :] += dot(probs.astype(BF16), downs)
                dk[g, keys, :] += dot(delta, queries[:, :PAIR])
                dqt += dot(kt[g, :, keys], delta)
                done += size
            dqt = jnp.concatenate([dqt[:HEAD_DIM, :BLOCK], dqt[HEAD_DIM:, BLOCK:]], axis=0)
            dq = dqt.T.astype(BF16).astype(F32) * HEAD_DIM ** (-0.5)
            deltas[g][rows, :PAIR] = dq.astype(BF16)

    each_query_block(lab_s, blocks, body)
    for g in range(groups):
        deltas[g][:, PAIR : 2 * PAIR] = dk[g].astype(BF16)
        deltas[g][:, 2 * PAIR :] = dv[g].astype(BF16)
        changes[g][...] = dot(normed_t[...], deltas[g][...]).astype(BF16)
        sums[g][...] = jnp.sum(deltas[g][...].astype(F32), axis=0, keepdims=True)


def attend_back(lab_s, lab_c, normed_t, lse, inner, qkv, dms):
    groups = len(qkv)
    width, length = normed_t.shape
    args = [lab_s, lab_c, normed_t, lse, inner] + list(qkv) + list(dms)
    outs = [shape((length, 3 * PAIR), BF16)] * groups
    outs += [shape((width, 3 * PAIR), BF16)] * groups
    outs += [shape((1, 3 * PAIR), F32)] * groups
    scratch = [
        pltpu.VMEM((groups, 2 * length, 2 * PAIR), BF16),
        pltpu.VMEM((groups, length, 2 * PAIR), BF16),
        pltpu.VMEM((groups, length, PAIR), BF16),
        pltpu.VMEM((groups, 2 * length, PAIR), BF16),
        pltpu.VMEM((groups, PAIR, length), BF16),
        pltpu.VMEM((groups, length, PAIR), F32),
        pltpu.VMEM((groups, length, PAIR), F32),
    ]
    got = call(
        functools.partial(attend_back_kernel, groups, 0),
        outs,
        [SMEM] + [VMEM] * (len(args) - 1),
        scratch,
        groups * (2 * length * width * 3 * PAIR + 20 * length * length * PAIR),
        *args,
    )
    return got[:groups], got[groups : 2 * groups], got[2 * groups :]


def close_kernel(groups, frames, delta_ref, gain, *refs):
    deltas, weights = refs[:groups], refs[groups : 2 * groups]
    out_ref, sums_ref = refs[2 * groups :]
    sums_ref[...] = jnp.zeros_like(sums_ref)

    def step(tile, carry):
        rows = pl.ds(pl.multiple_of(tile * ROWS, ROWS), ROWS)
        one = jnp.zeros((ROWS, frames.shape[1]), F32)
        for d, w in zip(deltas, weights):
            one += dot(d[rows, :], w[...], NT)
        xhat, scale = centred(frames[rows, :].astype(F32))
        e = one * gain[...]
        lean = jnp.mean(e, axis=-1, keepdims=True)
        pull = jnp.mean(e * xhat, axis=-1, keepdims=True)
        out_ref[rows, :] = (delta_ref[rows, :] + scale * (e - lean - xhat * pull)).astype(BF16)
        sums_ref[0:1, :] += jnp.sum(one * xhat, axis=0, keepdims=True)
        sums_ref[1:2, :] += jnp.sum(one, axis=0, keepdims=True)
        return carry

    lax.fori_loop(0, frames.shape[0] // ROWS, step, 0)


def close(frames, delta, gain, deltas, weights):
    length, width = frames.shape
    args = [frames, delta, gain] + list(deltas) + list(weights)
    return call(
        functools.partial(close_kernel, len(deltas)),
        [shape((length, width), BF16), shape((8, width), F32)],
        [VMEM] * len(args),
        [],
        6 * length * width * width,
        *args,
    )


PLANE = ("aa", "ba")


def plane_swap(value, step, size):
    return lax.ppermute(value, PLANE, [(i, i ^ step) for i in range(size)])


def dp_swap(value, step, size):
    return lax.ppermute(value, "dp", [(i, i ^ step) for i in range(size)])


def halves(value, axis, core):
    low, high = jnp.split(value, 2, axis=axis)
    return jnp.where(core == 0, low, high), jnp.where(core == 0, high, low)


def unhalve(mine, other, axis, core):
    low = jnp.where(core == 0, mine, other)
    high = jnp.where(core == 0, other, mine)
    return jnp.concatenate([low, high], axis=axis)


def shards(
    frames,
    segment_ids,
    cotangent,
    first_gain,
    first_shift,
    query_weight,
    query_bias,
    key_weight,
    value_weight,
    value_bias,
    out_weight,
    out_bias,
    second_gain,
    second_shift,
    up_weight,
    up_bias,
    down_weight,
    down_bias,
):
    length, width = frames.shape[1:]
    planes = lax.axis_size(PLANE)
    dp_size = lax.axis_size("dp")
    core = lax.axis_index("dp") % 2
    head_cols = query_weight.shape[1]
    groups = width // PAIR
    per_group = planes // groups

    def row(v):
        return v.astype(F32)[None, :]

    qkv_half = [halves(w, 1, core) for w in (query_weight, key_weight, value_weight)]
    half_cols = head_cols // 2
    zero_bias = jnp.zeros_like(query_bias)
    bias_half = [halves(b, 0, core) for b in (query_bias, zero_bias, value_bias)]
    qkv_own = [
        jnp.concatenate(
            [jnp.concatenate([w[h] for w in qkv_half], axis=1), jnp.concatenate([b[h] for b in bias_half])[None, :]],
            axis=0,
        )
        for h in range(2)
    ]
    out_own = halves(out_weight, 0, core)
    up_own = halves(up_weight, 1, core)
    up_bias_own = halves(up_bias, 0, core)
    down_own = halves(down_weight, 0, core)

    def gathered(own):
        pieces = [own]
        for r in range(1, planes):
            near = plane_swap(own[0], r, planes)
            pieces.append((near, dp_swap(near, 1, dp_size)))
        return pieces

    qkv_pieces = gathered(qkv_own)
    out_pieces = gathered(out_own)
    up_pieces = gathered(up_own)
    up_bias_pieces = gathered(up_bias_own)
    down_pieces = gathered(down_own)

    def group_pieces(pieces, g):
        return [p for r in range(g * per_group, (g + 1) * per_group) for p in pieces[r]]

    qkv_w, qkv_b, out_w, up_w, up_b, down_w = [], [], [], [], [], []
    for g in range(groups):
        parts = group_pieces(qkv_pieces, g)
        joined = jnp.concatenate(
            [p[:, i * half_cols : (i + 1) * half_cols] for i in range(3) for p in parts], axis=1
        )
        qkv_w.append(joined[:width])
        qkv_b.append(joined[width:].astype(F32))
        out_w.append(jnp.concatenate(group_pieces(out_pieces, g), axis=0))
        up_w.append(jnp.concatenate(group_pieces(up_pieces, g), axis=1))
        up_b.append(row(jnp.concatenate(group_pieces(up_bias_pieces, g), axis=0)))
        down_w.append(jnp.concatenate(group_pieces(down_pieces, g), axis=0))

    x = frames[0]
    dy = cotangent[0]
    lab_c = segment_ids.reshape(length, 1)
    gain_one, shift_one, gain_two, shift_two = map(row, (first_gain, first_shift, second_gain, second_shift))

    (normed, normed_t), qkv0, mixed0, mixed_t0, lse0 = attend(
        segment_ids, lab_c, x, (gain_one, shift_one), qkv_w[:1], qkv_b[:1]
    )
    _, qkv1, mixed1, mixed_t1, lse1 = attend(segment_ids, lab_c, normed, None, qkv_w[1:], qkv_b[1:])
    qkv = list(qkv0) + list(qkv1)
    out_w_parts = [out_w[0], jnp.concatenate(out_w[1:], axis=0)]
    inner, normed_two, normed_two_t = join(x, row(out_bias), gain_two, shift_two, [mixed0, mixed1], out_w_parts)
    dy_t = dy.T
    zero = jnp.zeros((length, width), F32)
    out_sum, two_sum, up_d, down_d, upb_d = feed(
        normed_two, normed_two_t, dy, dy_t, zero, zero, up_w, up_b, down_w
    )
    layer, delta, sums, inner_rows, out_d, dms = turn(
        inner, out_sum, row(down_bias), two_sum, dy, gain_two, [mixed0, mixed1], [mixed_t0, mixed_t1], out_w_parts
    )
    out_delta = jnp.concatenate(out_d, axis=0)
    dm_groups = [dms[0]] + [dms[1][:, i * PAIR : (i + 1) * PAIR] for i in range(groups - 1)]
    lse = jnp.concatenate([lse0, lse1], axis=0)
    deltas, changes, change_sums = [], [], []
    for g in list(range(1, groups)) + [0]:
        d, c, s = attend_back(
            segment_ids, lab_c, normed_t, lse[2 * g : 2 * g + 2], inner_rows[2 * g : 2 * g + 2], [qkv[g]], [dm_groups[g]]
        )
        deltas.append(d[0])
        changes.append(c[0])
        change_sums.append(s[0])
    order = list(range(1, groups)) + [0]
    frames_delta, close_sums = close(x, delta, gain_one, deltas, [qkv_w[g] for g in order])
    by_group = {g: i for i, g in enumerate(order)}

    def reduced(value, axis):
        size = value.shape[axis] // (2 * planes)

        def piece(at):
            return lax.slice_in_dim(value, at * size, (at + 1) * size, axis=axis)

        mine = []
        for r in range(planes):
            mine.append(piece(2 * r) + dp_swap(piece(2 * r + 1), 1, dp_size))
        total = mine[0].astype(F32)
        for r in range(1, planes):
            total += plane_swap(mine[r], r, planes).astype(F32)
        total = total.astype(BF16)
        wide = total.astype(F32)
        for k in range(2, dp_size, 2):
            wide += dp_swap(total, k, dp_size).astype(F32)
        wide = wide.astype(BF16)
        return unhalve(wide, dp_swap(wide, 1, dp_size), axis, core).astype(F32)

    def joint(i):
        return jnp.concatenate([changes[by_group[g]][:, i * PAIR : (i + 1) * PAIR] for g in range(groups)], axis=1)

    def joint_sum(i):
        return jnp.concatenate([change_sums[by_group[g]][0, i * PAIR : (i + 1) * PAIR] for g in range(groups)], axis=0)

    query_change = reduced(joint(0), 1)
    key_change = reduced(joint(1), 1)
    value_change = reduced(joint(2), 1)
    qbias_change = reduced(joint_sum(0), 0)
    vbias_change = reduced(joint_sum(2), 0)
    out_change = reduced(out_delta, 0)
    up_change = reduced(jnp.concatenate(up_d, axis=1), 1)
    down_change = reduced(jnp.concatenate(down_d, axis=0), 0)
    upbias_change = reduced(jnp.concatenate(upb_d, axis=1)[0], 0)

    small = jnp.concatenate([close_sums[:2], sums[:4]], axis=0)
    small = small + dp_swap(small, 1, dp_size)
    total = small
    for r in range(1, planes):
        total += plane_swap(small, r, planes)
    small = total
    for k in range(2, dp_size, 2):
        total += dp_swap(small, k, dp_size)
    return (
        layer[None],
        frames_delta[None],
        total[0],
        total[1],
        query_change,
        qbias_change,
        key_change,
        value_change,
        vbias_change,
        out_change,
        total[4],
        total[2],
        total[3],
        up_change,
        upbias_change,
        down_change,
        total[5],
    )


def solution(mesh):
    rows = P(("dp", "aa", "ba"), None, None)
    cols = P(None, ("aa", "ba"))
    flat = P(("aa", "ba"))
    down = P(("aa", "ba"), None)
    placed = (
        rows, P(("dp", "aa", "ba"), None), rows, P(), P(), cols, flat, cols, cols, flat,
        down, P(), P(), P(), cols, flat, down, P(),
    )
    outs = (
        rows, rows, P(), P(), cols, flat, cols, cols, flat, down, P(), P(), P(), cols, flat, down, P(),
    )
    return jax.shard_map(shards, mesh=mesh, in_specs=placed, out_specs=outs, check_vma=False)
```

```python
import functools
import math

import jax
import jax.numpy as jnp
from jax import lax
from jax.experimental import pallas as pl
from jax.experimental.pallas import tpu as pltpu
from jax.sharding import PartitionSpec as P

HEAD_DIM = 64
PAIR = 2 * HEAD_DIM
TRIPLE = 3 * PAIR
BLOCK = 128
ROWS = 256
EXTRA = 16
EPSILON = 1e-05
MASKED = -1e30
DP = "dp"
PLANE = ("aa", "ba")

F32 = jnp.float32
BF16 = jnp.bfloat16
NN = (((1,), (0,)), ((), ()))
NT = (((1,), (1,)), ((), ()))
TN = (((0,), (0,)), ((), ()))
SPARE = 8 * 1024 * 1024
LARGE = 61 * 1024 * 1024
VMEM = pl.BlockSpec(memory_space=pltpu.VMEM)
SMEM = pl.BlockSpec(memory_space=pltpu.SMEM)
PACE = 1e6


def dot(left, right, dims=NN):
    return lax.dot_general(left, right, dims, preferred_element_type=F32)


def shape(dims, dtype):
    return jax.ShapeDtypeStruct(tuple(dims), dtype)


class Bag(dict):
    def __getattr__(self, name):
        if name not in self:
            raise AttributeError(name)
        return self[name]


jax.tree_util.register_pytree_node(
    Bag, lambda bag: (tuple(bag.values()), tuple(bag)), lambda names, values: Bag(zip(names, values))
)


def leaves(tree):
    if isinstance(tree, dict):
        tree = list(tree.values())
    if isinstance(tree, (list, tuple)):
        return [leaf for part in tree for leaf in leaves(part)]
    return [tree]


def rebuilt(tree, values):
    if isinstance(tree, dict):
        return Bag({key: rebuilt(part, values) for key, part in tree.items()})
    if isinstance(tree, (list, tuple)):
        return [rebuilt(part, values) for part in tree]
    return next(values)


def staged(body, meta, ins, outs, scratch, microseconds, kept=(), room=None):
    kept = leaves(list(kept))
    given, made = leaves(ins), leaves(outs)

    def kernel(*refs):
        table, refs = refs[0], refs[1 + len(kept) :]
        ours, refs = refs[: len(given)], refs[len(given) :]
        theirs, rest = refs[: len(made)], refs[len(made) :]
        body(table, rebuilt(ins, iter(ours)), rebuilt(outs, iter(theirs)), *rest)

    if room is None:
        room = sum(math.prod(v.shape) * jnp.dtype(v.dtype).itemsize for v in scratch) + SPARE
    got = pl.pallas_call(
        kernel,
        out_shape=made,
        in_specs=[SMEM] + [VMEM] * (len(kept) + len(given)),
        out_specs=[VMEM] * len(made),
        scratch_shapes=list(scratch),
        compiler_params=pltpu.CompilerParams(vmem_limit_bytes=room),
        cost_estimate=pl.CostEstimate(flops=1000, bytes_accessed=int(microseconds * PACE), transcendentals=0),
    )(meta, *kept, *given)
    return rebuilt(outs, iter(got))


def centred(values):
    centre = jnp.mean(values, axis=-1, keepdims=True)
    offset = values - centre
    spread = jnp.mean(offset * offset, axis=-1, keepdims=True)
    scale = lax.rsqrt(spread + EPSILON)
    return offset * scale, scale


def lane_of(dims):
    return lax.broadcasted_iota(jnp.int32, dims, 1)


def my_half(table, half):
    core = table[0, 0]
    mine = pl.ds(pl.multiple_of(core * half, half), half)
    other = pl.ds(pl.multiple_of((1 - core) * half, half), half)
    return mine, other


def scalars(core, labels):
    length = labels.shape[1]
    first_q, last_q = labels[0, ::ROWS], labels[0, ROWS - 1 :: ROWS]
    first_k, last_k = labels[0, ::BLOCK], labels[0, BLOCK - 1 :: BLOCK]
    low = jnp.sum((last_k[None, :] < first_q[:, None]).astype(jnp.int32), axis=1)
    above = jnp.sum((first_k[None, :] > last_q[:, None]).astype(jnp.int32), axis=1)
    count = length // BLOCK - above - low
    return jnp.concatenate([core.astype(jnp.int32)[None], low, count])[None]


def open_kernel(labels, places, q, k, v, o, qb, vb, *refs):
    rows, (own, other, vectors, table) = refs[:-4], refs[-4:]
    half = own.shape[0] - EXTRA
    length = labels.shape[1]
    core = places[0, 0]
    for pack, at in ((own, core), (other, 1 - core)):
        part = pl.ds(pl.multiple_of(at * half, half), half)
        for i, w in enumerate((q, k, v)):
            pack[:half, i * PAIR : (i + 1) * PAIR] = w[part, :]
        pack[:half, TRIPLE:] = o[:, part].T
        pack[half:, :] = jnp.zeros((EXTRA, 4 * PAIR), BF16)
        for i, b in ((0, qb), (2, vb)):
            wide = jnp.broadcast_to(b[...].astype(F32).reshape(1, PAIR), (EXTRA, PAIR))
            pack[half:, i * PAIR : (i + 1) * PAIR] = wide.astype(BF16)
    vectors[...] = jnp.zeros_like(vectors)
    for i, r in enumerate(rows):
        vectors[i : i + 1, :] = r[...].astype(F32).reshape(1, r.shape[0])
    table[0, 0] = core
    table[0, 15] = places[0, 1]
    queries, blocks = length // ROWS, length // BLOCK
    for at in range(queries):
        first, last = labels[0, at * ROWS], labels[0, (at + 1) * ROWS - 1]
        low, high = jnp.int32(0), jnp.int32(blocks)
        for b in range(blocks):
            low += (labels[0, (b + 1) * BLOCK - 1] < first).astype(jnp.int32)
            high -= (labels[0, b * BLOCK] > last).astype(jnp.int32)
        table[0, 1 + at] = low
        table[0, 1 + queries + at] = high - low


def opened(labels, places, q, k, v, o, qb, vb, rows):
    width = q.shape[0]
    pack = shape((width // 2 + EXTRA, 4 * PAIR), BF16)
    return pl.pallas_call(
        open_kernel,
        out_shape=[pack, pack, shape((8, width), F32), shape((1, 16), jnp.int32)],
        in_specs=[SMEM, SMEM] + [VMEM] * (6 + len(rows)),
        out_specs=[VMEM, VMEM, VMEM, SMEM],
        compiler_params=pltpu.CompilerParams(vmem_limit_bytes=LARGE),
        cost_estimate=pl.CostEstimate(flops=1000, bytes_accessed=int(2 * PACE), transcendentals=0),
    )(labels, places, q, k, v, o, qb, vb, *rows)


def each_query_block(table, length, body):
    blocks = length // BLOCK
    queries = length // ROWS

    def step(at, carry):
        low = table[0, 1 + at]
        count = table[0, 1 + queries + at]
        under = 0
        for span in range(2, blocks + 1):
            base = jnp.minimum(low, blocks - span)

            @pl.when((count > under) & (count <= span))
            def _():
                body(at, base, span)

            under = span
        return carry

    lax.fori_loop(0, queries, step, 0)


def clip_marks(labels, at):
    clip = lax.broadcasted_iota(jnp.int32, (BLOCK, ROWS), 0)
    same = clip == labels[:, pl.ds(at, ROWS)]
    hot = jnp.where(same, 1.0, 0.0).T.astype(BF16)
    cold = jnp.where(same, 0.0, MASKED).T.astype(BF16)
    return hot, cold


def split_heads(wide):
    low = lane_of(wide.shape) < HEAD_DIM
    zero = jnp.zeros_like(wide)
    return jnp.where(low, wide, zero), jnp.where(low, zero, wide)


def attend_scratch(groups, length):
    return [
        pltpu.VMEM((groups, 2 * length, 2 * PAIR), BF16),
        pltpu.VMEM((groups, length, 2 * PAIR), BF16),
        pltpu.VMEM((groups, PAIR, length), BF16),
    ]


def attend(table, labels, norm_tile, packs, qkv, mixed, lse, qm, ke, vt):
    length = qkv[0].shape[0]
    half = packs[0][0].shape[0] - EXTRA
    mine, other = my_half(table, half)
    for tile in range(length // ROWS):
        at = tile * ROWS
        rows = pl.ds(at, ROWS)
        normed = norm_tile(rows)
        hot, cold = clip_marks(labels, at)
        for g, (own, far) in enumerate(packs):
            y = dot(normed[rows, mine], own[:half, :TRIPLE])
            y += dot(normed[rows, other], far[:half, :TRIPLE])
            y += own[half:, :TRIPLE][:1].astype(F32)
            q = (y[:, :PAIR] * HEAD_DIM ** (-0.5)).astype(BF16)
            k = y[:, PAIR : 2 * PAIR].astype(BF16)
            v = y[:, 2 * PAIR :].astype(BF16)
            qkv[g][rows, :PAIR] = q
            qkv[g][rows, PAIR : 2 * PAIR] = k
            qkv[g][rows, 2 * PAIR :] = v
            for head, part in enumerate(split_heads(q)):
                to = pl.ds(2 * at + head * ROWS, ROWS)
                qm[g, to, :PAIR] = part
                qm[g, to, PAIR:] = hot
            ke[g, rows, :PAIR] = k
            ke[g, rows, PAIR:] = cold
            vt[g, :, rows] = v.T
    for out in lse:
        out[...] = jnp.zeros_like(out)

    def body(at, base, span):
        keys = pl.ds(pl.multiple_of(base * BLOCK, BLOCK), span * BLOCK)
        rows = pl.ds(pl.multiple_of(at * ROWS, ROWS), ROWS)
        for g in range(len(packs)):
            heads = []
            for head in range(2):
                queries = pl.ds(pl.multiple_of((2 * at + head) * ROWS, ROWS), ROWS)
                scores = dot(ke[g, keys, :], qm[g, queries, :], NT)
                peak = jnp.max(scores, axis=0, keepdims=True)
                raised = jnp.exp(scores - peak)
                total = jnp.sum(raised, axis=0, keepdims=True)
                values = vt[g, head * HEAD_DIM : (head + 1) * HEAD_DIM, keys]
                heads.append(dot(values, raised.astype(BF16)) * (1.0 / total))
                lse[g][head : head + 1, rows] = peak + jnp.log(total)
            mixed[g][rows, :] = jnp.concatenate(heads, axis=0).T.astype(BF16)

    each_query_block(table, length, body)


def attend_outs(groups, length):
    return Bag(
        qkv=[shape((length, TRIPLE), BF16)] * groups,
        mixed=[shape((length, PAIR), BF16)] * groups,
        lse=[shape((8, length), F32)] * groups,
    )


def feed_pack_into(pack, up, down, bias, rows, half):
    hidden = up.shape[1]
    pack[:half, :] = up[rows, :]
    for b in range(0, hidden, half):
        pack[half : 2 * half, b : b + half] = down[b : b + half, rows]
    pack[2 * half :, :] = jnp.broadcast_to(bias, (EXTRA, hidden)).astype(BF16)


def first_body(table, ins, outs, qm, ke, vt):
    vectors = ins.vectors

    def norm_tile(rows):
        xhat, _ = centred(ins.frames[rows, :].astype(F32))
        outs.xhat[rows, :] = xhat.astype(BF16)
        outs.normed[rows, :] = (xhat * vectors[0:1, :] + vectors[1:2, :]).astype(BF16)
        return outs.normed

    attend(table, ins.labels, norm_tile, [ins.pack], outs.qkv, outs.mixed, outs.lse, qm, ke, vt)
    if len(ins.feed):
        up, down = ins.feed
        half = up.shape[0] // 2
        for pack, rows in zip(outs.feed, my_half(table, half)):
            feed_pack_into(pack, up, down, vectors[6:7, :], rows, half)


def first(meta, labels, frames, vectors, pack, feed):
    length, width = frames.shape
    outs = attend_outs(1, length)
    outs.update(
        normed=shape((length, width), BF16),
        xhat=shape((length, width), BF16),
        feed=[shape((width + EXTRA, up.shape[1]), BF16) for up in feed],
    )
    ins = Bag(labels=labels, vectors=vectors, pack=list(pack), frames=frames, feed=list(feed))
    return staged(first_body, meta, ins, outs, attend_scratch(1, length), 9, room=LARGE)


def second_body(table, ins, outs, qm, ke, vt):
    attend(table, ins.labels, lambda rows: ins.normed, ins.packs, outs.qkv, outs.mixed, outs.lse, qm, ke, vt)


def second(meta, labels, normed, packs, kept):
    length, width = normed.shape
    groups = len(packs)
    ins = Bag(labels=labels, packs=[list(pair) for pair in packs], normed=normed)
    scratch = attend_scratch(groups, length)
    return staged(second_body, meta, ins, attend_outs(groups, length), scratch, 13, kept)


def join_body(table, ins, outs):
    length, width = ins.frames.shape
    half = width // 2
    vectors, inner = ins.vectors, outs.inner
    for tile in range(length // ROWS):
        rows = pl.ds(tile * ROWS, ROWS)
        for which, cols in enumerate(my_half(table, half)):
            total = ins.frames[rows, cols].astype(F32) + vectors[2:3, cols]
            for m, pack in zip(ins.mixed, ins.packs):
                total += dot(m[rows, :], pack[which][:half, TRIPLE:], NT)
            inner[rows, cols] = total
        xhat, _ = centred(inner[rows, :])
        outs.normed[rows, :] = (xhat * vectors[3:4, :] + vectors[4:5, :]).astype(BF16)


def join(meta, frames, vectors, mixed, packs, kept):
    ins = Bag(frames=frames, vectors=vectors, mixed=list(mixed), packs=[list(pair) for pair in packs])
    outs = Bag(inner=shape(frames.shape, F32), normed=shape(frames.shape, BF16))
    return staged(join_body, meta, ins, outs, [], 4, kept)


def gelu_both(u):
    falling = jnp.exp(u * u * -0.5)
    t = 1.0 / (1.0 + jnp.abs(u) * (0.3275911 * 0.5**0.5))
    poly = 0.5 * 1.061405429
    for c in (-1.453152027, 1.421413741, -0.284496736, 0.254829592):
        poly = poly * t + 0.5 * c
    tail = poly * t * falling
    phi = jnp.where(u >= 0.0, 1.0 - tail, tail)
    return u * phi, phi + u * falling * (0.5 / jnp.pi) ** 0.5


def feed_tile(rows, halves, normed, cot, own, far, act, delta_s):
    mine, other = halves
    half = own.shape[0] // 2 - EXTRA // 2
    hidden = own.shape[1]
    u = dot(normed[rows, mine], own[:half, :]) + dot(normed[rows, other], far[:half, :])
    u += own[2 * half :, :][:1].astype(F32)
    back = jnp.concatenate(
        [
            dot(cot[rows, mine], own[half : 2 * half, b : b + half], NT)
            + dot(cot[rows, other], far[half : 2 * half, b : b + half], NT)
            for b in range(0, hidden, half)
        ],
        axis=1,
    )
    active, slope = gelu_both(u)
    active = active.astype(BF16)
    act[rows, :] = active
    delta = (back * slope).astype(BF16)
    delta_s[rows, :] = delta
    out = [
        sum(dot(active[:, b : b + half], pack[half : 2 * half, b : b + half]) for b in range(0, hidden, half))
        for pack in (own, far)
    ]
    return [dot(delta, pack[:half, :], NT) for pack in (own, far)], out


def feed_deltas(halves, normed, cot, act, delta_s, keep, send):
    delta = delta_s[...]
    hidden = delta.shape[1]
    half = normed.shape[1] // 2
    total = jnp.sum(delta.astype(F32), axis=0, keepdims=True)
    for cols, pack in zip(halves[::-1], (send, keep)):
        pack[:half, :] = dot(normed[:, cols], delta, TN).astype(BF16)
        for b in range(0, hidden, half):
            pack[half : 2 * half, b : b + half] = dot(act[:, b : b + half], cot[:, cols], TN).astype(BF16)
        pack[2 * half :, :] = jnp.broadcast_to(total, (EXTRA, hidden)).astype(BF16)


def feed_body(count, table, ins, outs, *scratch):
    normed, cot = ins.normed, ins.cot
    acts, deltas = scratch[:count], scratch[count:]
    length, width = normed.shape
    halves = my_half(table, width // 2)
    for tile in range(length // ROWS):
        rows = pl.ds(tile * ROWS, ROWS)
        fresh = [
            feed_tile(rows, halves, normed, cot, own, far, acts[i], deltas[i]) for i, (own, far) in enumerate(ins.feed)
        ]
        for i, to in enumerate((outs.two, outs.out)):
            for which, cols in enumerate(halves):
                total = sum(f[i][which] for f in fresh)
                for before in ins.before:
                    total += before[i][rows, cols]
                to[rows, cols] = total
    for i in range(count):
        feed_deltas(halves, normed, cot, acts[i], deltas[i], outs.keep[i], outs.send[i])


def feed(meta, normed, cot, before, packs, kept):
    length, width = normed.shape
    hidden = packs[0][0].shape[1]
    count = len(packs)
    ins = Bag(feed=[list(pair) for pair in packs], normed=normed, cot=cot, before=before)
    pack = shape(packs[0][0].shape, BF16)
    outs = Bag(
        keep=[pack] * count, send=[pack] * count, two=shape((length, width), F32), out=shape((length, width), F32)
    )
    scratch = [pltpu.VMEM((length, hidden), BF16)] * (2 * count)
    return staged(functools.partial(feed_body, count), meta, ins, outs, scratch, 4 * count, kept)


def turn_body(table, ins, outs):
    length, width = ins.inner.shape
    half = width // 2
    mine, other = my_half(table, half)
    sums, pulls, packs = outs.sums, outs.pulls, ins.packs
    sums[...] = jnp.zeros_like(sums)
    pulls[...] = jnp.zeros_like(pulls)
    dims = (8, PAIR)
    picks = lax.broadcasted_iota(jnp.int32, dims, 0) == lane_of(dims) // HEAD_DIM
    ones = jnp.where(picks, 1.0, 0.0).astype(BF16)
    for tile in range(length // ROWS):
        rows = pl.ds(tile * ROWS, ROWS)
        inner = ins.inner[rows, :]
        outs.layer[rows, :] = (inner + ins.out[rows, :] + ins.vectors[5:6, :]).astype(BF16)
        xhat, scale = centred(inner)
        two = ins.two[rows, :]
        dy = ins.cot[rows, :].astype(F32)
        e = two * ins.vectors[3:4, :]
        lean = jnp.mean(e, axis=-1, keepdims=True)
        pull = jnp.mean(e * xhat, axis=-1, keepdims=True)
        delta = dy + scale * (e - lean - xhat * pull)
        outs.delta[rows, :] = delta
        branch = delta.astype(BF16)
        outs.branch[rows, :] = branch
        for at, part in enumerate((two * xhat, two, branch.astype(F32), dy)):
            sums[2 + at : 3 + at, :] += jnp.sum(part, axis=0, keepdims=True)
        for g, m in enumerate(ins.mixed):
            back = dot(outs.branch[rows, mine], packs[g][0][:half, TRIPLE:])
            back += dot(outs.branch[rows, other], packs[g][1][:half, TRIPLE:])
            back = back.astype(BF16)
            outs.back[g][rows, :] = back
            product = back.astype(F32) * m[rows, :].astype(F32)
            high = product.astype(BF16)
            low = (product - high.astype(F32)).astype(BF16)
            pulls[2 * g : 2 * g + 2, rows] = (dot(ones, high, NT) + dot(ones, low, NT))[:2]


def back_body(at_rows, carry, table, ins, outs, qm, ke, ve, dmm, kt, dk, dv, ds):
    groups = len(at_rows)
    length = ins.qkv[0].shape[0]
    for tile in range(length // ROWS):
        at = tile * ROWS
        rows = pl.ds(at, ROWS)
        hot, cold = clip_marks(ins.labels, at)
        for g in range(groups):
            qkv, down = ins.qkv[g], ins.back[g]
            q = qkv[rows, :PAIR]
            k = qkv[rows, PAIR : 2 * PAIR]
            for head, (part, d) in enumerate(zip(split_heads(q), split_heads(down[rows, :]))):
                to = pl.ds(2 * at + head * ROWS, ROWS)
                qm[g, to, :PAIR] = part
                qm[g, to, PAIR:] = hot
                dmm[g, to, :] = d
            ke[g, rows, :PAIR] = k
            ke[g, rows, PAIR:] = cold
            ve[g, rows, :] = qkv[rows, 2 * PAIR :]
            kt[g, :, rows] = k.T
            dk[g, rows, :] = jnp.zeros((ROWS, PAIR), F32)
            dv[g, rows, :] = jnp.zeros((ROWS, PAIR), F32)

    def body(at, base, span):
        rows = pl.ds(pl.multiple_of(at * ROWS, ROWS), ROWS)
        both = pl.ds(pl.multiple_of(at * 2 * ROWS, 2 * ROWS), 2 * ROWS)
        for g in range(groups):
            queries = qm[g, both, :]
            downs = dmm[g, both, :]
            dqt = [jnp.zeros((HEAD_DIM, ROWS), F32)] * 2
            done = 0
            while done < span:
                size = min(2, span - done)
                keys = pl.ds(pl.multiple_of((base + done) * BLOCK, BLOCK), size * BLOCK)
                probs, delta = [], []
                for head in range(2):
                    cut = slice(head * ROWS, (head + 1) * ROWS)
                    scores = dot(ke[g, keys, :], queries[cut], NT)
                    p = jnp.exp(scores - ins.lse[g][head : head + 1, rows])
                    slope = dot(ve[g, keys, :], downs[cut], NT)
                    at_row = at_rows[g] + head
                    d = (p * (slope - ins.pulls[at_row : at_row + 1, rows])).astype(BF16)
                    probs.append(p.astype(BF16))
                    delta.append(d)
                    dqt[head] += dot(kt[g, head * HEAD_DIM : (head + 1) * HEAD_DIM, keys], d)
                dv[g, keys, :] += dot(jnp.concatenate(probs, axis=1), downs)
                dk[g, keys, :] += dot(jnp.concatenate(delta, axis=1), queries[:, :PAIR])
                done += size
            dq = jnp.concatenate(dqt, axis=0).T.astype(BF16).astype(F32) * HEAD_DIM ** (-0.5)
            ds[g, rows, :PAIR] = dq.astype(BF16)

    each_query_block(table, length, body)
    half = ins.normed.shape[1] // 2
    halves = my_half(table, half)
    for g in range(groups):
        ds[g, :, PAIR : 2 * PAIR] = dk[g].astype(BF16)
        ds[g, :, 2 * PAIR :] = dv[g].astype(BF16)
        every = ds[g]
        for cols, pack in zip(halves[::-1], (outs.send[g], outs.keep[g])):
            pack[:half, :TRIPLE] = dot(ins.normed[:, cols], every, TN).astype(BF16)
            pack[:half, TRIPLE:] = dot(ins.branch[:, cols], ins.mixed[g][...], TN).astype(BF16)
    outs.sums[...] = ins.sums[...]
    for tile in range(length // ROWS):
        rows = pl.ds(tile * ROWS, ROWS)
        for which, cols in enumerate(halves):
            part = dot(ds[0, rows, :], ins.packs[0][which][:half, :TRIPLE], NT)
            for g in range(1, groups):
                part += dot(ds[g, rows, :], ins.packs[g][which][:half, :TRIPLE], NT)
            outs.sums[0:1, cols] += jnp.sum(part * ins.xhat[rows, cols].astype(F32), axis=0, keepdims=True)
            outs.sums[1:2, cols] += jnp.sum(part, axis=0, keepdims=True)
            for before in ins.one:
                part += before[rows, cols]
            outs.one[rows, cols] = part
    for g in range(groups):
        total = jnp.sum(ds[g].astype(F32), axis=0, keepdims=True)
        total = jnp.concatenate([total, jnp.zeros((1, PAIR), F32)], axis=1)
        rest = outs.sums[...] if carry and g == 0 else jnp.zeros((8, 4 * PAIR), F32)
        extra = jnp.concatenate([jnp.broadcast_to(total, (8, 4 * PAIR)), rest], axis=0).astype(BF16)
        outs.send[g][half:, :] = extra
        outs.keep[g][half:, :] = extra


def back_scratch(groups, length):
    return [
        pltpu.VMEM((groups, 2 * length, 2 * PAIR), BF16),
        pltpu.VMEM((groups, length, 2 * PAIR), BF16),
        pltpu.VMEM((groups, length, PAIR), BF16),
        pltpu.VMEM((groups, 2 * length, PAIR), BF16),
        pltpu.VMEM((groups, PAIR, length), BF16),
        pltpu.VMEM((groups, length, PAIR), F32),
        pltpu.VMEM((groups, length, PAIR), F32),
        pltpu.VMEM((groups, length, TRIPLE), BF16),
    ]


def back_outs(groups, length, width):
    pack = shape((width // 2 + EXTRA, 4 * PAIR), BF16)
    return Bag(
        send=[pack] * groups, keep=[pack] * groups, one=shape((length, width), F32), sums=shape((8, width), F32)
    )


def back(meta, given, one, sums, part, carry, kept):
    length, width = given.normed.shape
    ins = Bag(
        labels=given.labels,
        qkv=[given.qkv[g] for g in part],
        back=[given.back[g] for g in part],
        lse=[given.lse[g] for g in part],
        pulls=given.pulls,
        normed=given.normed,
        xhat=given.xhat,
        branch=given.branch,
        mixed=[given.mixed[g] for g in part],
        packs=[list(given.packs[g]) for g in part],
        one=[one],
        sums=sums,
    )
    outs = back_outs(len(part), length, width)
    body = functools.partial(back_body, [2 * g for g in part], carry)
    return staged(body, meta, ins, outs, back_scratch(len(part), length), 8 * len(part), kept)


def turn_back_body(part, table, ins, outs, sums, *scratch):
    turned = Bag(outs.turned)
    turned.update(sums=sums)
    turn_body(table, ins.turn, turned)
    given = Bag(ins.back)
    given.update(
        back=[outs.turned.back[g] for g in part], pulls=outs.turned.pulls, branch=outs.turned.branch, one=[], sums=sums
    )
    back_body([2 * g for g in part], False, table, given, outs.back, *scratch)


def turn_back(meta, given, inner, two, out, cot, vectors, part, kept):
    length, width = inner.shape
    ins = Bag(
        turn=Bag(
            inner=inner,
            two=two,
            out=out,
            cot=cot,
            vectors=vectors,
            mixed=list(given.mixed),
            packs=[list(p) for p in given.packs],
        ),
        back=Bag(
            labels=given.labels,
            qkv=[given.qkv[g] for g in part],
            lse=[given.lse[g] for g in part],
            normed=given.normed,
            xhat=given.xhat,
            mixed=[given.mixed[g] for g in part],
            packs=[list(given.packs[g]) for g in part],
        ),
    )
    groups = len(given.mixed)
    outs = Bag(
        turned=Bag(
            layer=shape((length, width), BF16),
            pulls=shape((max(8, 2 * groups), length), F32),
            delta=shape((length, width), F32),
            branch=shape((length, width), BF16),
            back=[shape((length, PAIR), BF16)] * groups,
        ),
        back=back_outs(len(part), length, width),
    )
    scratch = [pltpu.VMEM((8, width), F32)] + back_scratch(len(part), length)
    return staged(functools.partial(turn_back_body, part), meta, ins, outs, scratch, 14, kept)


def close_body(table, ins, outs):
    length, width = ins.frames.shape
    for tile in range(length // ROWS):
        rows = pl.ds(tile * ROWS, ROWS)
        xhat, scale = centred(ins.frames[rows, :].astype(F32))
        e = ins.one[rows, :] * ins.vectors[0:1, :]
        lean = jnp.mean(e, axis=-1, keepdims=True)
        pull = jnp.mean(e * xhat, axis=-1, keepdims=True)
        outs.frames_delta[rows, :] = (ins.delta[rows, :] + scale * (e - lean - xhat * pull)).astype(BF16)


def close(meta, frames, vectors, delta, one, kept):
    ins = Bag(vectors=vectors, frames=frames, delta=delta, one=one)
    outs = Bag(frames_delta=shape(frames.shape, BF16))
    return staged(close_body, meta, ins, outs, [], 3, kept).frames_delta


def cut_body(table, ins, outs):
    size = outs.blocks[0].shape[0] - EXTRA
    rows = size * len(outs.blocks)
    place = table[0, 15]
    end = sum(p[rows:, :].astype(F32) for p in ins.pieces).astype(BF16)
    for j, block in enumerate(outs.blocks):
        at = pl.ds(pl.multiple_of(jnp.bitwise_xor(place, j) * size, size), size)
        block[:size, :] = sum(p[at, :].astype(F32) for p in ins.pieces).astype(BF16)
        block[size:, :] = end


def cut_blocks(meta, pieces, count, kept):
    rows, cols = pieces[0].shape
    block = shape(((rows - EXTRA) // count + EXTRA, cols), BF16)
    return staged(cut_body, meta, Bag(pieces=list(pieces)), Bag(blocks=[block] * count), [], 2, kept).blocks


def sum_body(table, ins, outs):
    total = sum(p[...].astype(F32) for p in ins.parts)
    size = outs.block.shape[0]
    outs.block[...] = total[:size].astype(BF16)
    outs.extra[...] = total[size:]


def sum_blocks(meta, parts, kept):
    rows, cols = parts[0].shape
    outs = Bag(block=shape((rows - EXTRA, cols), BF16), extra=shape((EXTRA, cols), F32))
    return staged(sum_body, meta, Bag(parts=list(parts)), outs, [], 1, kept)


def ordered_into(table, blocks, pack_s):
    size = blocks[0].shape[0]
    for j, block in enumerate(blocks):
        at = pl.ds(pl.multiple_of(jnp.bitwise_xor(table[0, 15], j) * size, size), size)
        pack_s[at, :] = block[...].astype(F32)


def feed_end_body(table, ins, outs, pack_s):
    width, hidden = outs.up.shape
    half = width // 2
    for cols, blocks in zip(my_half(table, half), (ins.blocks, ins.far)):
        ordered_into(table, blocks, pack_s)
        outs.up[cols, :] = pack_s[:half, :]
        for b in range(0, hidden, half):
            outs.down[b : b + half, cols] = pack_s[half:, b : b + half]
    outs.bias[...] = ins.extra[0:1, :].reshape(hidden)


def feed_end(meta, blocks, far, extra, width, hidden):
    ins = Bag(blocks=list(blocks), far=list(far), extra=extra)
    outs = Bag(up=shape((width, hidden), F32), down=shape((hidden, width), F32), bias=shape((hidden,), F32))
    return staged(feed_end_body, meta, ins, outs, [pltpu.VMEM((width, hidden), F32)], 3)


def out_end_body(table, ins, outs, pack_s):
    half = pack_s.shape[0]
    for cols, blocks in zip(my_half(table, half), (ins.blocks, ins.far)):
        ordered_into(table, blocks, pack_s)
        for i, to in enumerate((outs.query, outs.key, outs.value)):
            to[cols, :] = pack_s[:, i * PAIR : (i + 1) * PAIR]
        outs.out[:, cols] = pack_s[:, TRIPLE:].T
    row = ins.extra[0:1, :]
    outs.query_bias[...] = row[:, :PAIR].reshape(PAIR)
    outs.value_bias[...] = row[:, 2 * PAIR : TRIPLE].reshape(PAIR)
    for i, to in enumerate(outs.small):
        to[...] = ins.small[8 + i : 9 + i, :].reshape(to.shape[0])


def out_end(meta, blocks, far, extra, small):
    width = small.shape[1]
    ins = Bag(blocks=list(blocks), far=list(far), extra=extra, small=small)
    outs = Bag(
        query=shape((width, PAIR), F32),
        key=shape((width, PAIR), F32),
        value=shape((width, PAIR), F32),
        out=shape((PAIR, width), F32),
        query_bias=shape((PAIR,), F32),
        value_bias=shape((PAIR,), F32),
        small=[shape((width,), F32)] * 6,
    )
    return staged(out_end_body, meta, ins, outs, [pltpu.VMEM((width // 2, 4 * PAIR), F32)], 2)


def plane_swap(value, step, size):
    return lax.ppermute(value, PLANE, [(i, i ^ step) for i in range(size)])


def dp_swap(value, step, size):
    return lax.ppermute(value, DP, [(i, i ^ step) for i in range(size)])


def to_blocks(value, half):
    rows = value.shape[0]
    if rows >= half:
        return jnp.concatenate(jnp.split(value, rows // half, axis=0), axis=1)
    return jnp.concatenate(jnp.split(value, half // rows, axis=1), axis=0)


def from_blocks(value, half):
    cols = value.shape[1]
    if cols >= half:
        return jnp.concatenate(jnp.split(value, cols // half, axis=1), axis=0)
    return jnp.concatenate(jnp.split(value, half // cols, axis=0), axis=1)


def extra_row(value):
    return jnp.pad(value[None], ((0, EXTRA - 1), (0, 0)))


def qkvo_pack(half_at, half, query, key, value, out, query_bias, value_bias):
    parts = [lax.dynamic_slice_in_dim(w, half_at, half, axis=0) for w in (query, key, value)]
    parts.append(lax.dynamic_slice_in_dim(out, half_at, half, axis=1).T)
    zero = jnp.zeros_like(query_bias)
    bias = jnp.concatenate([query_bias, zero, value_bias, zero])
    return jnp.concatenate([jnp.concatenate(parts, axis=1), extra_row(bias)], axis=0)


def feed_pack(half_at, half, up, up_bias, down):
    top = lax.dynamic_slice_in_dim(up, half_at, half, axis=0)
    low = to_blocks(lax.dynamic_slice_in_dim(down, half_at, half, axis=1), half)
    return jnp.concatenate([top, low, extra_row(up_bias)], axis=0)


def qkvo_join(shards):
    if len(shards) == 1:
        return shards[0]
    quarters = [jnp.split(s, 4, axis=1) for s in shards]
    return jnp.concatenate([q[i] for i in range(4) for q in quarters], axis=1)


def qkvo_cut(pack, count):
    if count == 1:
        return [pack]
    pieces = jnp.split(pack, 4 * count, axis=1)
    return [jnp.concatenate([pieces[i * count + s] for i in range(4)], axis=1) for s in range(count)]


def feed_join(shards, half):
    if len(shards) == 1:
        return shards[0]
    top = jnp.concatenate([s[:half] for s in shards], axis=1)
    low = jnp.concatenate([from_blocks(s[half : 2 * half], half) for s in shards], axis=0)
    end = jnp.concatenate([s[2 * half :] for s in shards], axis=1)
    return jnp.concatenate([top, to_blocks(low, half), end], axis=0)


def feed_cut(pack, count, half):
    if count == 1:
        return [pack]
    tops = jnp.split(pack[:half], count, axis=1)
    lows = jnp.split(from_blocks(pack[half : 2 * half], half), count, axis=0)
    ends = jnp.split(pack[2 * half :], count, axis=1)
    return [jnp.concatenate([t, to_blocks(l, half), e], axis=0) for t, l, e in zip(tops, lows, ends)]


def ordered(mine, other, core, axis):
    low = jnp.where(core == 0, mine, other)
    high = jnp.where(core == 0, other, mine)
    return jnp.concatenate([low, high], axis=axis)


def after(value, other):
    return lax.optimization_barrier((value, other))


def added(pieces):
    total = pieces[0].astype(F32)
    for piece in pieces[1:]:
        total += piece.astype(F32)
    return total.astype(BF16)


def z_swaps(pack, dp_size):
    return [pack] + [dp_swap(pack, k, dp_size) for k in range(2, dp_size, 2)]


def z_blocks(pack, dp_at, dp_size):
    rows, z_size = pack.shape[0] - EXTRA, dp_size // 2
    size = rows // z_size
    z_at = dp_at // 2

    def block(at):
        return jnp.concatenate([lax.dynamic_slice_in_dim(pack, at * size, size, axis=0), pack[rows:]], axis=0)

    return [block(z_at ^ k) for k in range(z_size)]


def from_z(blocks, dp_at, dp_size):
    stack = jnp.stack(blocks)
    z_at, z_size = dp_at // 2, dp_size // 2
    return jnp.concatenate([stack[z_at ^ j] for j in range(z_size)], axis=0)


def shards(
    frames,
    segment_ids,
    cotangent,
    first_gain,
    first_shift,
    query_weight,
    query_bias,
    key_weight,
    value_weight,
    value_bias,
    out_weight,
    out_bias,
    second_gain,
    second_shift,
    up_weight,
    up_bias,
    down_weight,
    down_bias,
):
    length, width = frames.shape[1:]
    half = width // 2
    planes = lax.axis_size(PLANE)
    dp_size = lax.axis_size(DP)
    dp_at = lax.axis_index(DP)
    core = dp_at % 2
    groups = width // PAIR
    per_group = planes // groups
    alone = per_group == 1
    x, dy, labels = frames[0], cotangent[0], segment_ids
    group_of = [range(g * per_group, (g + 1) * per_group) for g in range(groups)]
    last = groups - 1
    middle = list(range(1, last))
    peers = list(range(1, planes))
    late = [r for g in middle for r in group_of[g]]
    soon = list(group_of[last])
    rest = [r for r in group_of[0] if r]
    rows = (first_gain, first_shift, out_bias, second_gain, second_shift, down_bias)

    def far_half(near):
        return {r: dp_swap(v, 1, dp_size) for r, v in near.items()}

    def out_pair(g):
        return qkvo_join([near[r] for r in group_of[g]]), qkvo_join([far[r] for r in group_of[g]])

    def feed_pair(g):
        return feed_join([feed_near[r] for r in group_of[g]], half), feed_join([feed_far[r] for r in group_of[g]], half)

    if alone:
        places = jnp.stack([core, dp_at // 2]).astype(jnp.int32)[None]
        own, other, vectors, meta = opened(
            labels,
            places,
            query_weight,
            key_weight,
            value_weight,
            out_weight,
            query_bias,
            value_bias,
            (*rows, up_bias),
        )
        near = {r: plane_swap(own, r, planes) for r in peers}
        one = first(meta, labels, x, vectors, (own, other), (up_weight, down_weight))
        near, one = after(near, one)
        far = far_half(near)
        feed_own, feed_other = one.feed
    else:
        meta = scalars(core, labels)
        zero = jnp.zeros((width,), F32)
        vectors = jnp.stack([v.astype(F32) for v in rows] + [zero] * 2)
        own, other = (
            qkvo_pack(c * half, half, query_weight, key_weight, value_weight, out_weight, query_bias, value_bias)
            for c in (core, 1 - core)
        )
        near = {r: plane_swap(own, r, planes) for r in peers}
        far = far_half(near)
        feed_own, feed_other = (feed_pack(c * half, half, up_weight, up_bias, down_weight) for c in (core, 1 - core))
    near[0], far[0] = own, other
    qkvo = [out_pair(g) for g in range(groups)]
    if not alone:
        one = first(meta, labels, x, vectors, qkvo[0], ())
    feed_near, feed_far = {0: feed_own}, {0: feed_other}
    feed_soon = {r: plane_swap(feed_own, r, planes) for r in soon + rest}
    two = second(meta, labels, one.normed, qkvo[1:], ())
    feed_soon, two = after(feed_soon, two)
    feed_near.update(feed_soon)
    feed_far.update(far_half(feed_soon))
    mixed, qkv, lse = one.mixed + two.mixed, one.qkv + two.qkv, one.lse + two.lse
    held = [two.qkv, two.lse, one.normed]
    joined = join(meta, x, vectors, mixed, qkvo, held)
    feed_far, joined = after(feed_far, joined)
    feed_own, feed_soon = after(feed_own, feed_soon)
    feed_near.update({r: plane_swap(feed_own, r, planes) for r in late})

    def chip_sum(keep, far_send):
        return (keep.astype(F32) + far_send.astype(F32)).astype(BF16)

    def across(send):
        return dp_swap(send, 1, dp_size)

    def spread(pack, g, cut):
        return [plane_swap(p, r, planes) if r else p for r, p in zip(group_of[g], cut(pack))]

    def cut_feed(pack):
        return feed_cut(pack, per_group, half)

    def cut_qkvo(pack):
        return qkvo_cut(pack, per_group)

    held += [joined.inner, two.mixed, qkvo]
    three = feed(meta, joined.normed, dy, (), [feed_pair(last), feed_pair(0)], held)
    feed_late, three = after({r: feed_near[r] for r in late}, three)
    feed_near.update(feed_late)
    feed_far.update(far_half(feed_late))
    far_sends = [across(s) for s in three.send]
    middle_packs, far_sends = after([feed_pair(g) for g in middle], far_sends)
    feed_here = spread(chip_sum(three.keep[0], far_sends[0]), last, cut_feed)
    feed_here += spread(chip_sum(three.keep[1], far_sends[1]), 0, cut_feed)
    four = feed(meta, joined.normed, dy, [[three.two, three.out]], middle_packs, held)
    far_sends = [across(s) for s in four.send]
    two_sum, far_sends = after(four.two, far_sends)
    for i, g in enumerate(middle):
        feed_here += spread(chip_sum(four.keep[i], far_sends[i]), g, cut_feed)

    def along_z(parts):
        return [dp_swap(p, 2 * k, dp_size) if k else p for k, p in enumerate(parts)]

    def z_cut(pieces, kept):
        if alone:
            return cut_blocks(meta, pieces, dp_size // 2, kept)
        return z_blocks(added(pieces), dp_at, dp_size)

    given = Bag(labels=labels, normed=one.normed, xhat=one.xhat, qkv=qkv, lse=lse, mixed=mixed, packs=qkvo)
    got = turn_back(meta, given, joined.inner, two_sum, four.out, dy, vectors, [last], held)
    turned = got.turned
    given.update(pulls=turned.pulls, branch=turned.branch, back=turned.back)
    held = [two.qkv, two.lse, one.normed, mixed, qkvo, turned.back, turned.branch]
    got = got.back
    feed_here, got = after(feed_here, got)
    far_send = across(got.send[0])
    fed_parts = z_cut(feed_here, held + [got.one])
    labels, (fed_parts, far_send) = after(labels, (fed_parts, far_send))
    given.update(labels=labels)
    fed_parts = along_z(fed_parts)
    out_here = spread(chip_sum(got.keep[0], far_send), last, cut_qkvo)

    got = back(meta, given, got.one, got.sums, middle, False, held)
    (out_here, fed_parts), got = after((out_here, fed_parts), got)
    far_sends = [across(s) for s in got.send]
    fed_sum = sum_blocks(meta, fed_parts, held + [got.one])
    labels, (fed_sum, far_sends) = after(labels, (fed_sum, far_sends))
    given.update(labels=labels)
    fed_blocks = z_swaps(fed_sum.block, dp_size)
    for i, g in enumerate(middle):
        out_here += spread(chip_sum(got.keep[i], far_sends[i]), g, cut_qkvo)

    got = back(meta, given, got.one, got.sums, [0], alone, held)
    (out_here, fed_blocks), got = after((out_here, fed_blocks), got)
    far_send = across(got.send[0])
    if alone:
        out_parts = z_cut(out_here + [got.keep[0], far_send], [])
    else:
        out_here += spread(chip_sum(got.keep[0], far_send), 0, cut_qkvo)
        out_parts = z_cut(out_here, [])
    vectors, out_parts = after(vectors, out_parts)
    out_parts = along_z(out_parts)
    frames_delta = close(meta, x, vectors, turned.delta, got.one, [])
    fed_far = [across(b) for b in fed_blocks]
    out_parts, (frames_delta, fed_far) = after(out_parts, (frames_delta, fed_far))
    out_sum = sum_blocks(meta, out_parts, [])
    out_blocks = z_swaps(out_sum.block, dp_size)
    total = out_sum.extra if alone else got.sums
    step = 1
    while step < planes:
        total += plane_swap(total, step, planes)
        step *= 2
    if not alone:
        for step in range(1, dp_size.bit_length() - 1):
            total += dp_swap(total, 1 << step, dp_size)
        total += across(total)
    out_far = [across(b) for b in out_blocks]
    if alone:
        ended = feed_end(meta, fed_blocks, fed_far, fed_sum.extra, width, up_weight.shape[1])
        up_change, down_change, upbias_change = ended.up, ended.down, ended.bias
        ended = out_end(meta, out_blocks, out_far, out_sum.extra, total)
        query_change, key_change, value_change, out_change = ended.query, ended.key, ended.value, ended.out
        qbias_change, vbias_change, total = ended.query_bias, ended.value_bias, ended.small
    else:
        fed_near, fed_far = from_z(fed_blocks, dp_at, dp_size), from_z(fed_far, dp_at, dp_size)
        up_change = ordered(fed_near[:half], fed_far[:half], core, 0).astype(F32)
        down_change = ordered(from_blocks(fed_near[half:], half), from_blocks(fed_far[half:], half), core, 1)
        down_change = down_change.astype(F32)
        upbias_change = fed_sum.extra[0]
        out_near, out_far = from_z(out_blocks, dp_at, dp_size), from_z(out_far, dp_at, dp_size)
        qkvo_change = ordered(out_near, out_far, core, 0).astype(F32)
        query_change, key_change, value_change, out_change = jnp.split(qkvo_change, 4, axis=1)
        qbias_change, _, vbias_change, _ = jnp.split(out_sum.extra[0], 4)
        out_change = out_change.T
    return (
        turned.layer[None],
        frames_delta[None],
        total[0],
        total[1],
        query_change,
        qbias_change,
        key_change,
        value_change,
        vbias_change,
        out_change,
        total[4],
        total[2],
        total[3],
        up_change,
        upbias_change,
        down_change,
        total[5],
    )


def solution(mesh):
    rows = P((DP, *PLANE), None, None)
    cols = P(None, PLANE)
    flat = P(PLANE)
    down = P(PLANE, None)
    every = P()
    placed = (
        rows, P((DP, *PLANE), None), rows, every, every, cols, flat, cols, cols, flat,
        down, every, every, every, cols, flat, down, every,
    )
    outs = (
        rows, rows, every, every, cols, flat, cols, cols, flat, down, every, every, every, cols, flat, down, every,
    )
    return jax.shard_map(shards, mesh=mesh, in_specs=placed, out_specs=outs, check_vma=False)
```

```python
import functools
import math

import jax
import jax.numpy as jnp
from jax import lax
from jax.experimental import pallas as pl
from jax.experimental.pallas import tpu as pltpu
from jax.sharding import PartitionSpec as P

HEAD_DIM = 64
PAIR = 2 * HEAD_DIM
TRIPLE = 3 * PAIR
BLOCK = 128
ROWS = 256
EXTRA = 16
EPSILON = 1e-05
MASKED = -1e30
SPANS = (3, 5, 6, 8)
DP = "dp"
PLANE = ("aa", "ba")

F32 = jnp.float32
BF16 = jnp.bfloat16
NN = (((1,), (0,)), ((), ()))
NT = (((1,), (1,)), ((), ()))
TN = (((0,), (0,)), ((), ()))
SPARE = 8 * 1024 * 1024
LARGE = 61 * 1024 * 1024
VMEM = pl.BlockSpec(memory_space=pltpu.VMEM)
SMEM = pl.BlockSpec(memory_space=pltpu.SMEM)
PACE = 1e6


def dot(left, right, dims=NN):
    return lax.dot_general(left, right, dims, preferred_element_type=F32)


def shape(dims, dtype):
    return jax.ShapeDtypeStruct(tuple(dims), dtype)


class Bag(dict):
    def __getattr__(self, name):
        if name not in self:
            raise AttributeError(name)
        return self[name]


jax.tree_util.register_pytree_node(
    Bag, lambda bag: (tuple(bag.values()), tuple(bag)), lambda names, values: Bag(zip(names, values))
)


def leaves(tree):
    if isinstance(tree, dict):
        tree = list(tree.values())
    if isinstance(tree, (list, tuple)):
        return [leaf for part in tree for leaf in leaves(part)]
    return [tree]


def rebuilt(tree, values):
    if isinstance(tree, dict):
        return Bag({key: rebuilt(part, values) for key, part in tree.items()})
    if isinstance(tree, (list, tuple)):
        return [rebuilt(part, values) for part in tree]
    return next(values)


def staged(body, meta, ins, outs, scratch, microseconds, kept=(), room=None):
    kept = leaves(list(kept))
    given, made = leaves(ins), leaves(outs)

    def kernel(*refs):
        table, refs = refs[0], refs[1 + len(kept) :]
        ours, refs = refs[: len(given)], refs[len(given) :]
        theirs, rest = refs[: len(made)], refs[len(made) :]
        body(table, rebuilt(ins, iter(ours)), rebuilt(outs, iter(theirs)), *rest)

    if room is None:
        room = sum(math.prod(v.shape) * jnp.dtype(v.dtype).itemsize for v in scratch) + SPARE
    got = pl.pallas_call(
        kernel,
        out_shape=made,
        in_specs=[SMEM] + [VMEM] * (len(kept) + len(given)),
        out_specs=[VMEM] * len(made),
        scratch_shapes=list(scratch),
        compiler_params=pltpu.CompilerParams(vmem_limit_bytes=room),
        cost_estimate=pl.CostEstimate(flops=1000, bytes_accessed=int(microseconds * PACE), transcendentals=0),
    )(meta, *kept, *given)
    return rebuilt(outs, iter(got))


def centred(values):
    centre = jnp.mean(values, axis=-1, keepdims=True)
    offset = values - centre
    spread = jnp.mean(offset * offset, axis=-1, keepdims=True)
    scale = lax.rsqrt(spread + EPSILON)
    return offset * scale, scale


def lane_of(dims):
    return lax.broadcasted_iota(jnp.int32, dims, 1)


def my_half(table, half):
    core = table[0, 0]
    mine = pl.ds(pl.multiple_of(core * half, half), half)
    other = pl.ds(pl.multiple_of((1 - core) * half, half), half)
    return mine, other


def scalars(core, labels):
    length = labels.shape[1]
    first_q, last_q = labels[0, ::ROWS], labels[0, ROWS - 1 :: ROWS]
    first_k, last_k = labels[0, ::BLOCK], labels[0, BLOCK - 1 :: BLOCK]
    low = jnp.sum((last_k[None, :] < first_q[:, None]).astype(jnp.int32), axis=1)
    above = jnp.sum((first_k[None, :] > last_q[:, None]).astype(jnp.int32), axis=1)
    count = length // BLOCK - above - low
    return jnp.concatenate([core.astype(jnp.int32)[None], low, count])[None]


def open_kernel(labels, places, q, k, v, o, qb, vb, *refs):
    rows, (own, other, vectors, table) = refs[:-4], refs[-4:]
    half = own.shape[0] - EXTRA
    length = labels.shape[1]
    core = places[0, 0]
    for pack, at in ((own, core), (other, 1 - core)):
        part = pl.ds(pl.multiple_of(at * half, half), half)
        for i, w in enumerate((q, k, v)):
            pack[:half, i * PAIR : (i + 1) * PAIR] = w[part, :]
        pack[:half, TRIPLE:] = o[:, part].T
        pack[half:, :] = jnp.zeros((EXTRA, 4 * PAIR), BF16)
        for i, b in ((0, qb), (2, vb)):
            wide = jnp.broadcast_to(b[...].astype(F32).reshape(1, PAIR), (EXTRA, PAIR))
            pack[half:, i * PAIR : (i + 1) * PAIR] = wide.astype(BF16)
    vectors[...] = jnp.zeros_like(vectors)
    for i, r in enumerate(rows):
        vectors[i : i + 1, :] = r[...].astype(F32).reshape(1, r.shape[0])
    table[0, 0] = core
    table[0, 15] = places[0, 1]
    queries, blocks = length // ROWS, length // BLOCK
    for at in range(queries):
        first, last = labels[0, at * ROWS], labels[0, (at + 1) * ROWS - 1]
        low, high = jnp.int32(0), jnp.int32(blocks)
        for b in range(blocks):
            low += (labels[0, (b + 1) * BLOCK - 1] < first).astype(jnp.int32)
            high -= (labels[0, b * BLOCK] > last).astype(jnp.int32)
        table[0, 1 + at] = low
        table[0, 1 + queries + at] = high - low


def opened(labels, places, q, k, v, o, qb, vb, rows):
    width = q.shape[0]
    pack = shape((width // 2 + EXTRA, 4 * PAIR), BF16)
    return pl.pallas_call(
        open_kernel,
        out_shape=[pack, pack, shape((8, width), F32), shape((1, 16), jnp.int32)],
        in_specs=[SMEM, SMEM] + [VMEM] * (6 + len(rows)),
        out_specs=[VMEM, VMEM, VMEM, SMEM],
        compiler_params=pltpu.CompilerParams(vmem_limit_bytes=LARGE),
        cost_estimate=pl.CostEstimate(flops=1000, bytes_accessed=int(2 * PACE), transcendentals=0),
    )(labels, places, q, k, v, o, qb, vb, *rows)


def each_query_block(table, length, body, spans):
    blocks = length // BLOCK
    queries = length // ROWS

    def step(at, carry):
        low = table[0, 1 + at]
        count = table[0, 1 + queries + at]
        under = 0
        for span in [s for s in spans if s < blocks] + [blocks]:
            base = jnp.minimum(low, blocks - span)

            @pl.when((count > under) & (count <= span))
            def _():
                body(at, base, span)

            under = span
        return carry

    lax.fori_loop(0, queries, step, 0)


def clip_marks(labels, at):
    clip = lax.broadcasted_iota(jnp.int32, (BLOCK, ROWS), 0)
    same = clip == labels[:, pl.ds(at, ROWS)]
    hot = jnp.where(same, 1.0, 0.0).T.astype(BF16)
    cold = jnp.where(same, 0.0, MASKED).T.astype(BF16)
    return hot, cold


def split_heads(wide):
    low = lane_of(wide.shape) < HEAD_DIM
    zero = jnp.zeros_like(wide)
    return jnp.where(low, wide, zero), jnp.where(low, zero, wide)


def attend_scratch(groups, length):
    return [
        pltpu.VMEM((groups, 2 * length, 2 * PAIR), BF16),
        pltpu.VMEM((groups, length, 2 * PAIR), BF16),
        pltpu.VMEM((groups, PAIR, length), BF16),
        pltpu.VMEM((2 * groups, length, ROWS), BF16),
    ]


def attend(table, labels, norm_tile, packs, qkv, mixed, lse, qm, ke, vt, probs):
    length = qkv[0].shape[0]
    half = packs[0][0].shape[0] - EXTRA
    mine, other = my_half(table, half)
    for tile in range(length // ROWS):
        at = tile * ROWS
        rows = pl.ds(at, ROWS)
        normed = norm_tile(rows)
        hot, cold = clip_marks(labels, at)
        for g, (own, far) in enumerate(packs):
            y = dot(normed[rows, mine], own[:half, :TRIPLE])
            y += dot(normed[rows, other], far[:half, :TRIPLE])
            y += own[half:, :TRIPLE][:1].astype(F32)
            q = (y[:, :PAIR] * HEAD_DIM ** (-0.5)).astype(BF16)
            k = y[:, PAIR : 2 * PAIR].astype(BF16)
            v = y[:, 2 * PAIR :].astype(BF16)
            qkv[g][rows, :PAIR] = q
            qkv[g][rows, PAIR : 2 * PAIR] = k
            qkv[g][rows, 2 * PAIR :] = v
            for head, part in enumerate(split_heads(q)):
                to = pl.ds(2 * at + head * ROWS, ROWS)
                qm[g, to, :PAIR] = part
                qm[g, to, PAIR:] = hot
            ke[g, rows, :PAIR] = k
            ke[g, rows, PAIR:] = cold
            vt[g, :, rows] = v.T
    for out in lse:
        out[...] = jnp.zeros_like(out)

    def body(at, base, span):
        keys = pl.ds(pl.multiple_of(base * BLOCK, BLOCK), span * BLOCK)
        rows = pl.ds(pl.multiple_of(at * ROWS, ROWS), ROWS)
        scale = []
        for g in range(len(packs)):
            for head in range(2):
                queries = pl.ds(pl.multiple_of((2 * at + head) * ROWS, ROWS), ROWS)
                scores = dot(ke[g, keys, :], qm[g, queries, :], NT)
                peak = jnp.max(scores, axis=0, keepdims=True)
                raised = jnp.exp(scores - peak)
                total = jnp.sum(raised, axis=0, keepdims=True)
                probs[2 * g + head, : span * BLOCK, :] = raised.astype(BF16)
                lse[g][head : head + 1, rows] = peak + jnp.log(total)
                scale.append(1.0 / total)
        for g in range(len(packs)):
            heads = []
            for head in range(2):
                values = vt[g, head * HEAD_DIM : (head + 1) * HEAD_DIM, keys]
                heads.append(dot(values, probs[2 * g + head, : span * BLOCK, :]) * scale[2 * g + head])
            mixed[g][rows, :] = jnp.concatenate(heads, axis=0).T.astype(BF16)

    each_query_block(table, length, body, SPANS)


def attend_outs(groups, length):
    return Bag(
        qkv=[shape((length, TRIPLE), BF16)] * groups,
        mixed=[shape((length, PAIR), BF16)] * groups,
        lse=[shape((8, length), F32)] * groups,
    )


def feed_pack_into(pack, up, down, bias, rows, half):
    hidden = up.shape[1]
    pack[:half, :] = up[rows, :]
    for b in range(0, hidden, half):
        pack[half : 2 * half, b : b + half] = down[b : b + half, rows]
    pack[2 * half :, :] = jnp.broadcast_to(bias, (EXTRA, hidden)).astype(BF16)


def first_body(table, ins, outs, *scratch):
    vectors = ins.vectors

    def norm_tile(rows):
        xhat, _ = centred(ins.frames[rows, :].astype(F32))
        outs.xhat[rows, :] = xhat.astype(BF16)
        outs.normed[rows, :] = (xhat * vectors[0:1, :] + vectors[1:2, :]).astype(BF16)
        return outs.normed

    attend(table, ins.labels, norm_tile, [ins.pack], outs.qkv, outs.mixed, outs.lse, *scratch)
    if len(ins.feed):
        up, down = ins.feed
        half = up.shape[0] // 2
        for pack, rows in zip(outs.feed, my_half(table, half)):
            feed_pack_into(pack, up, down, vectors[6:7, :], rows, half)


def first(meta, labels, frames, vectors, pack, feed):
    length, width = frames.shape
    outs = attend_outs(1, length)
    outs.update(
        normed=shape((length, width), BF16),
        xhat=shape((length, width), BF16),
        feed=[shape((width + EXTRA, up.shape[1]), BF16) for up in feed],
    )
    ins = Bag(labels=labels, vectors=vectors, pack=list(pack), frames=frames, feed=list(feed))
    return staged(first_body, meta, ins, outs, attend_scratch(1, length), 9, room=LARGE)


def second_body(table, ins, outs, *scratch):
    attend(table, ins.labels, lambda rows: ins.normed, ins.packs, outs.qkv, outs.mixed, outs.lse, *scratch)


def second(meta, labels, normed, packs, kept):
    length, width = normed.shape
    groups = len(packs)
    ins = Bag(labels=labels, packs=[list(pair) for pair in packs], normed=normed)
    scratch = attend_scratch(groups, length)
    return staged(second_body, meta, ins, attend_outs(groups, length), scratch, 13, kept)


def join_body(table, ins, outs):
    length, width = ins.frames.shape
    half = width // 2
    vectors, inner = ins.vectors, outs.inner
    for tile in range(length // ROWS):
        rows = pl.ds(tile * ROWS, ROWS)
        for which, cols in enumerate(my_half(table, half)):
            total = ins.frames[rows, cols].astype(F32) + vectors[2:3, cols]
            for m, pack in zip(ins.mixed, ins.packs):
                total += dot(m[rows, :], pack[which][:half, TRIPLE:], NT)
            inner[rows, cols] = total
        xhat, _ = centred(inner[rows, :])
        outs.normed[rows, :] = (xhat * vectors[3:4, :] + vectors[4:5, :]).astype(BF16)


def join(meta, frames, vectors, mixed, packs, kept):
    ins = Bag(frames=frames, vectors=vectors, mixed=list(mixed), packs=[list(pair) for pair in packs])
    outs = Bag(inner=shape(frames.shape, F32), normed=shape(frames.shape, BF16))
    return staged(join_body, meta, ins, outs, [], 4, kept)


def gelu_both(u):
    falling = jnp.exp(u * u * -0.5)
    t = 1.0 / (1.0 + jnp.abs(u) * (0.3275911 * 0.5**0.5))
    poly = 0.5 * 1.061405429
    for c in (-1.453152027, 1.421413741, -0.284496736, 0.254829592):
        poly = poly * t + 0.5 * c
    tail = poly * t * falling
    phi = jnp.where(u >= 0.0, 1.0 - tail, tail)
    return u * phi, phi + u * falling * (0.5 / jnp.pi) ** 0.5


def feed_tile(rows, halves, normed, cot, own, far):
    mine, other = halves
    half = own.shape[0] // 2 - EXTRA // 2
    hidden = own.shape[1]
    u = dot(normed[rows, mine], own[:half, :]) + dot(normed[rows, other], far[:half, :])
    back = [
        dot(cot[rows, mine], own[half : 2 * half, b : b + half], NT)
        + dot(cot[rows, other], far[half : 2 * half, b : b + half], NT)
        for b in range(0, hidden, half)
    ]
    return u + own[2 * half :, :][:1].astype(F32), jnp.concatenate(back, axis=1)


def feed_turn(rows, u, back, act, delta_s):
    active, slope = gelu_both(u)
    act[rows, :] = active.astype(BF16)
    delta_s[rows, :] = (back * slope).astype(BF16)


def feed_out(rows, halves, packs, acts, deltas, before, two, out):
    half = packs[0][0].shape[0] // 2 - EXTRA // 2
    hidden = packs[0][0].shape[1]
    for which, cols in enumerate(halves):
        total = sum(dot(d[rows, :], p[which][:half, :], NT) for d, p in zip(deltas, packs))
        for b in before:
            total += b[0][rows, cols]
        two[rows, cols] = total
        total = sum(
            dot(a[rows, b : b + half], p[which][half : 2 * half, b : b + half])
            for a, p in zip(acts, packs)
            for b in range(0, hidden, half)
        )
        for b in before:
            total += b[1][rows, cols]
        out[rows, cols] = total


def feed_deltas(halves, normed, cot, act, delta_s, keep, send):
    delta = delta_s[...]
    hidden = delta.shape[1]
    half = normed.shape[1] // 2
    total = jnp.sum(delta.astype(F32), axis=0, keepdims=True)
    for cols, pack in zip(halves[::-1], (send, keep)):
        pack[:half, :] = dot(normed[:, cols], delta, TN).astype(BF16)
        for b in range(0, hidden, half):
            pack[half : 2 * half, b : b + half] = dot(act[:, b : b + half], cot[:, cols], TN).astype(BF16)
        pack[2 * half :, :] = jnp.broadcast_to(total, (EXTRA, hidden)).astype(BF16)


def feed_body(count, table, ins, outs, *scratch):
    normed, cot = ins.normed, ins.cot
    acts, deltas = scratch[:count], scratch[count:]
    length, width = normed.shape
    halves = my_half(table, width // 2)
    tiles = [pl.ds(at, ROWS) for at in range(0, length, ROWS)]
    late = None
    for rows in tiles + [None]:
        if rows is not None:
            fresh = [feed_tile(rows, halves, normed, cot, *pair) for pair in ins.feed]
        if late is not None:
            feed_out(late, halves, ins.feed, acts, deltas, ins.before, outs.two, outs.out)
        if rows is not None:
            for (u, back), act, delta in zip(fresh, acts, deltas):
                feed_turn(rows, u, back, act, delta)
        late = rows
    for i in range(count):
        feed_deltas(halves, normed, cot, acts[i], deltas[i], outs.keep[i], outs.send[i])


def feed(meta, normed, cot, before, packs, kept):
    length, width = normed.shape
    hidden = packs[0][0].shape[1]
    count = len(packs)
    ins = Bag(feed=[list(pair) for pair in packs], normed=normed, cot=cot, before=before)
    pack = shape(packs[0][0].shape, BF16)
    outs = Bag(
        keep=[pack] * count, send=[pack] * count, two=shape((length, width), F32), out=shape((length, width), F32)
    )
    scratch = [pltpu.VMEM((length, hidden), BF16)] * (2 * count)
    return staged(functools.partial(feed_body, count), meta, ins, outs, scratch, 4 * count, kept)


def turn_body(table, ins, outs):
    length, width = ins.inner.shape
    half = width // 2
    mine, other = my_half(table, half)
    sums, pulls, packs = outs.sums, outs.pulls, ins.packs
    sums[...] = jnp.zeros_like(sums)
    pulls[...] = jnp.zeros_like(pulls)
    dims = (8, PAIR)
    picks = lax.broadcasted_iota(jnp.int32, dims, 0) == lane_of(dims) // HEAD_DIM
    ones = jnp.where(picks, 1.0, 0.0).astype(BF16)
    for tile in range(length // ROWS):
        rows = pl.ds(tile * ROWS, ROWS)
        inner = ins.inner[rows, :]
        outs.layer[rows, :] = (inner + ins.out[rows, :] + ins.vectors[5:6, :]).astype(BF16)
        xhat, scale = centred(inner)
        two = ins.two[rows, :]
        dy = ins.cot[rows, :].astype(F32)
        e = two * ins.vectors[3:4, :]
        lean = jnp.mean(e, axis=-1, keepdims=True)
        pull = jnp.mean(e * xhat, axis=-1, keepdims=True)
        delta = dy + scale * (e - lean - xhat * pull)
        outs.delta[rows, :] = delta
        branch = delta.astype(BF16)
        outs.branch[rows, :] = branch
        for at, part in enumerate((two * xhat, two, branch.astype(F32), dy)):
            sums[2 + at : 3 + at, :] += jnp.sum(part, axis=0, keepdims=True)
        for g, m in enumerate(ins.mixed):
            back = dot(outs.branch[rows, mine], packs[g][0][:half, TRIPLE:])
            back += dot(outs.branch[rows, other], packs[g][1][:half, TRIPLE:])
            back = back.astype(BF16)
            outs.back[g][rows, :] = back
            product = back.astype(F32) * m[rows, :].astype(F32)
            high = product.astype(BF16)
            low = (product - high.astype(F32)).astype(BF16)
            pulls[2 * g : 2 * g + 2, rows] = (dot(ones, high, NT) + dot(ones, low, NT))[:2]


def back_body(at_rows, carry, table, ins, outs, qm, ke, ve, dmm, kt, dk, dv, ds, probs, tilts):
    groups = len(at_rows)
    length = ins.qkv[0].shape[0]
    blocks = length // BLOCK
    for tile in range(length // ROWS):
        at = tile * ROWS
        rows = pl.ds(at, ROWS)
        hot, cold = clip_marks(ins.labels, at)
        for g in range(groups):
            qkv, down = ins.qkv[g], ins.back[g]
            q = qkv[rows, :PAIR]
            k = qkv[rows, PAIR : 2 * PAIR]
            for head, (part, d) in enumerate(zip(split_heads(q), split_heads(down[rows, :]))):
                to = pl.ds(2 * at + head * ROWS, ROWS)
                qm[g, to, :PAIR] = part
                qm[g, to, PAIR:] = hot
                dmm[g, to, :] = d
            ke[g, rows, :PAIR] = k
            ke[g, rows, PAIR:] = cold
            ve[g, rows, :] = qkv[rows, 2 * PAIR :]
            kt[g, :, rows] = k.T
            dk[g, rows, :] = jnp.zeros((ROWS, PAIR), F32)
            dv[g, rows, :] = jnp.zeros((ROWS, PAIR), F32)

    def body(at, base, span):
        rows = pl.ds(pl.multiple_of(at * ROWS, ROWS), ROWS)
        both = pl.ds(pl.multiple_of(at * 2 * ROWS, 2 * ROWS), 2 * ROWS)
        queries = [qm[g, both, :] for g in range(groups)]
        downs = [dmm[g, both, :] for g in range(groups)]
        dqt = [[jnp.zeros((HEAD_DIM, ROWS), F32)] * 2 for _ in range(groups)]
        items = [(g, done, min(2, span - done)) for g in range(groups) for done in range(0, span, 2)]

        def weigh(slot, g, done, size):
            keys = pl.ds(pl.multiple_of((base + done) * BLOCK, BLOCK), size * BLOCK)
            for head in range(2):
                cut = slice(head * ROWS, (head + 1) * ROWS)
                scores = dot(ke[g, keys, :], queries[g][cut], NT)
                slope = dot(ve[g, keys, :], downs[g][cut], NT)
                p = jnp.exp(scores - ins.lse[g][head : head + 1, rows])
                at_row = at_rows[g] + head
                delta = p * (slope - ins.pulls[at_row : at_row + 1, rows])
                probs[slot, : size * BLOCK, cut] = p.astype(BF16)
                tilts[slot, : size * BLOCK, cut] = delta.astype(BF16)

        def gather(slot, g, done, size):
            keys = pl.ds(pl.multiple_of((base + done) * BLOCK, BLOCK), size * BLOCK)
            part = slice(0, size * BLOCK)
            dv[g, keys, :] += dot(probs[slot, part, :], downs[g])
            dk[g, keys, :] += dot(tilts[slot, part, :], queries[g][:, :PAIR])
            for head in range(2):
                cut = slice(head * ROWS, (head + 1) * ROWS)
                wide = kt[g, head * HEAD_DIM : (head + 1) * HEAD_DIM, keys]
                dqt[g][head] += dot(wide, tilts[slot, part, cut])

        for i, item in enumerate(items):
            weigh(i % 2, *item)
            if i:
                gather((i - 1) % 2, *items[i - 1])
        gather((len(items) - 1) % 2, *items[-1])
        for g in range(groups):
            dq = jnp.concatenate(dqt[g], axis=0).T.astype(BF16).astype(F32) * HEAD_DIM ** (-0.5)
            ds[g, rows, :PAIR] = dq.astype(BF16)

    each_query_block(table, length, body, range(2, blocks))
    half = ins.normed.shape[1] // 2
    halves = my_half(table, half)
    for g in range(groups):
        ds[g, :, PAIR : 2 * PAIR] = dk[g].astype(BF16)
        ds[g, :, 2 * PAIR :] = dv[g].astype(BF16)
        every = ds[g]
        for cols, pack in zip(halves[::-1], (outs.send[g], outs.keep[g])):
            pack[:half, :TRIPLE] = dot(ins.normed[:, cols], every, TN).astype(BF16)
            pack[:half, TRIPLE:] = dot(ins.branch[:, cols], ins.mixed[g][...], TN).astype(BF16)
    outs.sums[...] = ins.sums[...]
    for tile in range(length // ROWS):
        rows = pl.ds(tile * ROWS, ROWS)
        for which, cols in enumerate(halves):
            part = dot(ds[0, rows, :], ins.packs[0][which][:half, :TRIPLE], NT)
            for g in range(1, groups):
                part += dot(ds[g, rows, :], ins.packs[g][which][:half, :TRIPLE], NT)
            outs.sums[0:1, cols] += jnp.sum(part * ins.xhat[rows, cols].astype(F32), axis=0, keepdims=True)
            outs.sums[1:2, cols] += jnp.sum(part, axis=0, keepdims=True)
            for before in ins.one:
                part += before[rows, cols]
            outs.one[rows, cols] = part
    for g in range(groups):
        total = jnp.sum(ds[g].astype(F32), axis=0, keepdims=True)
        total = jnp.concatenate([total, jnp.zeros((1, PAIR), F32)], axis=1)
        rest = outs.sums[...] if carry and g == 0 else jnp.zeros((8, 4 * PAIR), F32)
        extra = jnp.concatenate([jnp.broadcast_to(total, (8, 4 * PAIR)), rest], axis=0).astype(BF16)
        outs.send[g][half:, :] = extra
        outs.keep[g][half:, :] = extra


def back_scratch(groups, length):
    return [
        pltpu.VMEM((groups, 2 * length, 2 * PAIR), BF16),
        pltpu.VMEM((groups, length, 2 * PAIR), BF16),
        pltpu.VMEM((groups, length, PAIR), BF16),
        pltpu.VMEM((groups, 2 * length, PAIR), BF16),
        pltpu.VMEM((groups, PAIR, length), BF16),
        pltpu.VMEM((groups, length, PAIR), F32),
        pltpu.VMEM((groups, length, PAIR), F32),
        pltpu.VMEM((groups, length, TRIPLE), BF16),
        pltpu.VMEM((2, 2 * BLOCK, 2 * ROWS), BF16),
        pltpu.VMEM((2, 2 * BLOCK, 2 * ROWS), BF16),
    ]


def back_outs(groups, length, width):
    pack = shape((width // 2 + EXTRA, 4 * PAIR), BF16)
    return Bag(
        send=[pack] * groups, keep=[pack] * groups, one=shape((length, width), F32), sums=shape((8, width), F32)
    )


def back(meta, given, one, sums, part, carry, kept):
    length, width = given.normed.shape
    ins = Bag(
        labels=given.labels,
        qkv=[given.qkv[g] for g in part],
        back=[given.back[g] for g in part],
        lse=[given.lse[g] for g in part],
        pulls=given.pulls,
        normed=given.normed,
        xhat=given.xhat,
        branch=given.branch,
        mixed=[given.mixed[g] for g in part],
        packs=[list(given.packs[g]) for g in part],
        one=[one],
        sums=sums,
    )
    outs = back_outs(len(part), length, width)
    body = functools.partial(back_body, [2 * g for g in part], carry)
    return staged(body, meta, ins, outs, back_scratch(len(part), length), 8 * len(part), kept)


def turn_back_body(part, table, ins, outs, sums, *scratch):
    turned = Bag(outs.turned)
    turned.update(sums=sums)
    turn_body(table, ins.turn, turned)
    given = Bag(ins.back)
    given.update(
        back=[outs.turned.back[g] for g in part], pulls=outs.turned.pulls, branch=outs.turned.branch, one=[], sums=sums
    )
    back_body([2 * g for g in part], False, table, given, outs.back, *scratch)


def turn_back(meta, given, inner, two, out, cot, vectors, part, kept):
    length, width = inner.shape
    ins = Bag(
        turn=Bag(
            inner=inner,
            two=two,
            out=out,
            cot=cot,
            vectors=vectors,
            mixed=list(given.mixed),
            packs=[list(p) for p in given.packs],
        ),
        back=Bag(
            labels=given.labels,
            qkv=[given.qkv[g] for g in part],
            lse=[given.lse[g] for g in part],
            normed=given.normed,
            xhat=given.xhat,
            mixed=[given.mixed[g] for g in part],
            packs=[list(given.packs[g]) for g in part],
        ),
    )
    groups = len(given.mixed)
    outs = Bag(
        turned=Bag(
            layer=shape((length, width), BF16),
            pulls=shape((max(8, 2 * groups), length), F32),
            delta=shape((length, width), F32),
            branch=shape((length, width), BF16),
            back=[shape((length, PAIR), BF16)] * groups,
        ),
        back=back_outs(len(part), length, width),
    )
    scratch = [pltpu.VMEM((8, width), F32)] + back_scratch(len(part), length)
    return staged(functools.partial(turn_back_body, part), meta, ins, outs, scratch, 14, kept)


def close_body(table, ins, outs):
    length, width = ins.frames.shape
    for tile in range(length // ROWS):
        rows = pl.ds(tile * ROWS, ROWS)
        xhat, scale = centred(ins.frames[rows, :].astype(F32))
        e = ins.one[rows, :] * ins.vectors[0:1, :]
        lean = jnp.mean(e, axis=-1, keepdims=True)
        pull = jnp.mean(e * xhat, axis=-1, keepdims=True)
        outs.frames_delta[rows, :] = (ins.delta[rows, :] + scale * (e - lean - xhat * pull)).astype(BF16)


def close(meta, frames, vectors, delta, one, kept):
    ins = Bag(vectors=vectors, frames=frames, delta=delta, one=one)
    outs = Bag(frames_delta=shape(frames.shape, BF16))
    return staged(close_body, meta, ins, outs, [], 3, kept).frames_delta


def cut_body(table, ins, outs):
    size = outs.blocks[0].shape[0] - EXTRA
    rows = size * len(outs.blocks)
    place = table[0, 15]
    end = sum(p[rows:, :].astype(F32) for p in ins.pieces).astype(BF16)
    for j, block in enumerate(outs.blocks):
        at = pl.ds(pl.multiple_of(jnp.bitwise_xor(place, j) * size, size), size)
        block[:size, :] = sum(p[at, :].astype(F32) for p in ins.pieces).astype(BF16)
        block[size:, :] = end


def cut_blocks(meta, pieces, count, kept):
    rows, cols = pieces[0].shape
    block = shape(((rows - EXTRA) // count + EXTRA, cols), BF16)
    return staged(cut_body, meta, Bag(pieces=list(pieces)), Bag(blocks=[block] * count), [], 2, kept).blocks


def sum_body(table, ins, outs):
    total = sum(p[...].astype(F32) for p in ins.parts)
    size = outs.block.shape[0]
    outs.block[...] = total[:size].astype(BF16)
    outs.extra[...] = total[size:]


def sum_blocks(meta, parts, kept):
    rows, cols = parts[0].shape
    outs = Bag(block=shape((rows - EXTRA, cols), BF16), extra=shape((EXTRA, cols), F32))
    return staged(sum_body, meta, Bag(parts=list(parts)), outs, [], 1, kept)


def ordered_into(table, blocks, pack_s):
    size = blocks[0].shape[0]
    for j, block in enumerate(blocks):
        at = pl.ds(pl.multiple_of(jnp.bitwise_xor(table[0, 15], j) * size, size), size)
        pack_s[at, :] = block[...].astype(F32)


def feed_end_body(table, ins, outs, pack_s):
    width, hidden = outs.up.shape
    half = width // 2
    for cols, blocks in zip(my_half(table, half), (ins.blocks, ins.far)):
        ordered_into(table, blocks, pack_s)
        outs.up[cols, :] = pack_s[:half, :]
        for b in range(0, hidden, half):
            outs.down[b : b + half, cols] = pack_s[half:, b : b + half]
    outs.bias[...] = ins.extra[0:1, :].reshape(hidden)


def feed_end(meta, blocks, far, extra, width, hidden):
    ins = Bag(blocks=list(blocks), far=list(far), extra=extra)
    outs = Bag(up=shape((width, hidden), F32), down=shape((hidden, width), F32), bias=shape((hidden,), F32))
    return staged(feed_end_body, meta, ins, outs, [pltpu.VMEM((width, hidden), F32)], 3)


def out_end_body(table, ins, outs, pack_s):
    half = pack_s.shape[0]
    for cols, blocks in zip(my_half(table, half), (ins.blocks, ins.far)):
        ordered_into(table, blocks, pack_s)
        for i, to in enumerate((outs.query, outs.key, outs.value)):
            to[cols, :] = pack_s[:, i * PAIR : (i + 1) * PAIR]
        outs.out[:, cols] = pack_s[:, TRIPLE:].T
    row = ins.extra[0:1, :]
    outs.query_bias[...] = row[:, :PAIR].reshape(PAIR)
    outs.value_bias[...] = row[:, 2 * PAIR : TRIPLE].reshape(PAIR)
    for i, to in enumerate(outs.small):
        to[...] = ins.small[8 + i : 9 + i, :].reshape(to.shape[0])


def out_end(meta, blocks, far, extra, small):
    width = small.shape[1]
    ins = Bag(blocks=list(blocks), far=list(far), extra=extra, small=small)
    outs = Bag(
        query=shape((width, PAIR), F32),
        key=shape((width, PAIR), F32),
        value=shape((width, PAIR), F32),
        out=shape((PAIR, width), F32),
        query_bias=shape((PAIR,), F32),
        value_bias=shape((PAIR,), F32),
        small=[shape((width,), F32)] * 6,
    )
    return staged(out_end_body, meta, ins, outs, [pltpu.VMEM((width // 2, 4 * PAIR), F32)], 2)


def plane_swap(value, step, size):
    return lax.ppermute(value, PLANE, [(i, i ^ step) for i in range(size)])


def dp_swap(value, step, size):
    return lax.ppermute(value, DP, [(i, i ^ step) for i in range(size)])


def to_blocks(value, half):
    rows = value.shape[0]
    if rows >= half:
        return jnp.concatenate(jnp.split(value, rows // half, axis=0), axis=1)
    return jnp.concatenate(jnp.split(value, half // rows, axis=1), axis=0)


def from_blocks(value, half):
    cols = value.shape[1]
    if cols >= half:
        return jnp.concatenate(jnp.split(value, cols // half, axis=1), axis=0)
    return jnp.concatenate(jnp.split(value, half // cols, axis=0), axis=1)


def extra_row(value):
    return jnp.pad(value[None], ((0, EXTRA - 1), (0, 0)))


def qkvo_pack(half_at, half, query, key, value, out, query_bias, value_bias):
    parts = [lax.dynamic_slice_in_dim(w, half_at, half, axis=0) for w in (query, key, value)]
    parts.append(lax.dynamic_slice_in_dim(out, half_at, half, axis=1).T)
    zero = jnp.zeros_like(query_bias)
    bias = jnp.concatenate([query_bias, zero, value_bias, zero])
    return jnp.concatenate([jnp.concatenate(parts, axis=1), extra_row(bias)], axis=0)


def feed_pack(half_at, half, up, up_bias, down):
    top = lax.dynamic_slice_in_dim(up, half_at, half, axis=0)
    low = to_blocks(lax.dynamic_slice_in_dim(down, half_at, half, axis=1), half)
    return jnp.concatenate([top, low, extra_row(up_bias)], axis=0)


def qkvo_join(shards):
    if len(shards) == 1:
        return shards[0]
    quarters = [jnp.split(s, 4, axis=1) for s in shards]
    return jnp.concatenate([q[i] for i in range(4) for q in quarters], axis=1)


def qkvo_cut(pack, count):
    if count == 1:
        return [pack]
    pieces = jnp.split(pack, 4 * count, axis=1)
    return [jnp.concatenate([pieces[i * count + s] for i in range(4)], axis=1) for s in range(count)]


def feed_join(shards, half):
    if len(shards) == 1:
        return shards[0]
    top = jnp.concatenate([s[:half] for s in shards], axis=1)
    low = jnp.concatenate([from_blocks(s[half : 2 * half], half) for s in shards], axis=0)
    end = jnp.concatenate([s[2 * half :] for s in shards], axis=1)
    return jnp.concatenate([top, to_blocks(low, half), end], axis=0)


def feed_cut(pack, count, half):
    if count == 1:
        return [pack]
    tops = jnp.split(pack[:half], count, axis=1)
    lows = jnp.split(from_blocks(pack[half : 2 * half], half), count, axis=0)
    ends = jnp.split(pack[2 * half :], count, axis=1)
    return [jnp.concatenate([t, to_blocks(l, half), e], axis=0) for t, l, e in zip(tops, lows, ends)]


def ordered(mine, other, core, axis):
    low = jnp.where(core == 0, mine, other)
    high = jnp.where(core == 0, other, mine)
    return jnp.concatenate([low, high], axis=axis)


def after(value, other):
    return lax.optimization_barrier((value, other))


def added(pieces):
    total = pieces[0].astype(F32)
    for piece in pieces[1:]:
        total += piece.astype(F32)
    return total.astype(BF16)


def z_swaps(pack, dp_size):
    return [pack] + [dp_swap(pack, k, dp_size) for k in range(2, dp_size, 2)]


def z_blocks(pack, dp_at, dp_size):
    rows, z_size = pack.shape[0] - EXTRA, dp_size // 2
    size = rows // z_size
    z_at = dp_at // 2

    def block(at):
        return jnp.concatenate([lax.dynamic_slice_in_dim(pack, at * size, size, axis=0), pack[rows:]], axis=0)

    return [block(z_at ^ k) for k in range(z_size)]


def from_z(blocks, dp_at, dp_size):
    stack = jnp.stack(blocks)
    z_at, z_size = dp_at // 2, dp_size // 2
    return jnp.concatenate([stack[z_at ^ j] for j in range(z_size)], axis=0)


def shards(
    frames,
    segment_ids,
    cotangent,
    first_gain,
    first_shift,
    query_weight,
    query_bias,
    key_weight,
    value_weight,
    value_bias,
    out_weight,
    out_bias,
    second_gain,
    second_shift,
    up_weight,
    up_bias,
    down_weight,
    down_bias,
):
    length, width = frames.shape[1:]
    half = width // 2
    planes = lax.axis_size(PLANE)
    dp_size = lax.axis_size(DP)
    dp_at = lax.axis_index(DP)
    core = dp_at % 2
    groups = width // PAIR
    per_group = planes // groups
    alone = per_group == 1
    x, dy, labels = frames[0], cotangent[0], segment_ids
    group_of = [range(g * per_group, (g + 1) * per_group) for g in range(groups)]
    last = groups - 1
    middle = list(range(1, last))
    peers = list(range(1, planes))
    late = [r for g in middle for r in group_of[g]]
    soon = list(group_of[last])
    rest = [r for r in group_of[0] if r]
    rows = (first_gain, first_shift, out_bias, second_gain, second_shift, down_bias)

    def far_half(near):
        return {r: dp_swap(v, 1, dp_size) for r, v in near.items()}

    def out_pair(g):
        return qkvo_join([near[r] for r in group_of[g]]), qkvo_join([far[r] for r in group_of[g]])

    def feed_pair(g):
        return feed_join([feed_near[r] for r in group_of[g]], half), feed_join([feed_far[r] for r in group_of[g]], half)

    if alone:
        places = jnp.stack([core, dp_at // 2]).astype(jnp.int32)[None]
        own, other, vectors, meta = opened(
            labels,
            places,
            query_weight,
            key_weight,
            value_weight,
            out_weight,
            query_bias,
            value_bias,
            (*rows, up_bias),
        )
        near = {r: plane_swap(own, r, planes) for r in peers}
        one = first(meta, labels, x, vectors, (own, other), (up_weight, down_weight))
        near, one = after(near, one)
        far = far_half(near)
        feed_own, feed_other = one.feed
    else:
        meta = scalars(core, labels)
        zero = jnp.zeros((width,), F32)
        vectors = jnp.stack([v.astype(F32) for v in rows] + [zero] * 2)
        own, other = (
            qkvo_pack(c * half, half, query_weight, key_weight, value_weight, out_weight, query_bias, value_bias)
            for c in (core, 1 - core)
        )
        near = {r: plane_swap(own, r, planes) for r in peers}
        far = far_half(near)
        feed_own, feed_other = (feed_pack(c * half, half, up_weight, up_bias, down_weight) for c in (core, 1 - core))
    near[0], far[0] = own, other
    qkvo = [out_pair(g) for g in range(groups)]
    if not alone:
        one = first(meta, labels, x, vectors, qkvo[0], ())
    feed_near, feed_far = {0: feed_own}, {0: feed_other}
    feed_soon = {r: plane_swap(feed_own, r, planes) for r in soon + rest}
    two = second(meta, labels, one.normed, qkvo[1:], ())
    feed_soon, two = after(feed_soon, two)
    feed_near.update(feed_soon)
    feed_far.update(far_half(feed_soon))
    mixed, qkv, lse = one.mixed + two.mixed, one.qkv + two.qkv, one.lse + two.lse
    held = [two.qkv, two.lse, one.normed]
    joined = join(meta, x, vectors, mixed, qkvo, held)
    feed_far, joined = after(feed_far, joined)
    feed_own, feed_soon = after(feed_own, feed_soon)
    feed_near.update({r: plane_swap(feed_own, r, planes) for r in late})

    def chip_sum(keep, far_send):
        return (keep.astype(F32) + far_send.astype(F32)).astype(BF16)

    def across(send):
        return dp_swap(send, 1, dp_size)

    def spread(pack, g, cut):
        return [plane_swap(p, r, planes) if r else p for r, p in zip(group_of[g], cut(pack))]

    def cut_feed(pack):
        return feed_cut(pack, per_group, half)

    def cut_qkvo(pack):
        return qkvo_cut(pack, per_group)

    held += [joined.inner, two.mixed, qkvo]
    three = feed(meta, joined.normed, dy, (), [feed_pair(last), feed_pair(0)], held)
    feed_late, three = after({r: feed_near[r] for r in late}, three)
    feed_near.update(feed_late)
    feed_far.update(far_half(feed_late))
    far_send = across(three.send[0])
    middle_packs, far_send = after([feed_pair(g) for g in middle], far_send)
    feed_here = spread(chip_sum(three.keep[0], far_send), last, cut_feed)
    four = feed(meta, joined.normed, dy, [[three.two, three.out]], middle_packs, held)
    four, feed_here = after(four, feed_here)
    three_send, four.send[0] = after(three.send[1], four.send[0])
    far_sends = [across(s) for s in four.send]
    two_sum, far_sends = after(four.two, far_sends)
    for i, g in enumerate(middle):
        feed_here += spread(chip_sum(four.keep[i], far_sends[i]), g, cut_feed)

    def along_z(parts):
        return [dp_swap(p, 2 * k, dp_size) if k else p for k, p in enumerate(parts)]

    def z_cut(pieces, kept):
        if alone:
            return cut_blocks(meta, pieces, dp_size // 2, kept)
        return z_blocks(added(pieces), dp_at, dp_size)

    given = Bag(labels=labels, normed=one.normed, xhat=one.xhat, qkv=qkv, lse=lse, mixed=mixed, packs=qkvo)
    far_send = across(three_send)
    got = turn_back(meta, given, joined.inner, two_sum, four.out, dy, vectors, [last], held)
    turned = got.turned
    given.update(pulls=turned.pulls, branch=turned.branch, back=turned.back)
    held = [two.qkv, two.lse, one.normed, mixed, qkvo, turned.back, turned.branch]
    got = got.back
    (feed_here, far_send), got = after((feed_here, far_send), got)
    if alone:
        feed_here += [three.keep[1], far_send]
    else:
        feed_here += spread(chip_sum(three.keep[1], far_send), 0, cut_feed)
    far_send = across(got.send[0])
    fed_parts = z_cut(feed_here, held + [got.one])
    labels, (fed_parts, far_send) = after(labels, (fed_parts, far_send))
    given.update(labels=labels)
    fed_parts = along_z(fed_parts)
    out_here = spread(chip_sum(got.keep[0], far_send), last, cut_qkvo)

    got = back(meta, given, got.one, got.sums, middle, False, held)
    (out_here, fed_parts), got = after((out_here, fed_parts), got)
    far_sends = [across(s) for s in got.send]
    fed_sum = sum_blocks(meta, fed_parts, held + [got.one])
    labels, (fed_sum, far_sends) = after(labels, (fed_sum, far_sends))
    given.update(labels=labels)
    fed_blocks = z_swaps(fed_sum.block, dp_size)
    for i, g in enumerate(middle):
        out_here += spread(chip_sum(got.keep[i], far_sends[i]), g, cut_qkvo)

    got = back(meta, given, got.one, got.sums, [0], alone, held)
    (out_here, fed_blocks), got = after((out_here, fed_blocks), got)
    far_send = across(got.send[0])
    if alone:
        out_parts = z_cut(out_here + [got.keep[0], far_send], [])
    else:
        out_here += spread(chip_sum(got.keep[0], far_send), 0, cut_qkvo)
        out_parts = z_cut(out_here, [])
    (vectors, fed_blocks), out_parts = after((vectors, fed_blocks), out_parts)
    out_parts = along_z(out_parts)
    frames_delta = close(meta, x, vectors, turned.delta, got.one, [])
    fed_far = [across(b) for b in fed_blocks]
    if alone:
        fed_far = feed_end(meta, fed_blocks, fed_far, fed_sum.extra, width, up_weight.shape[1])
    out_parts, (frames_delta, fed_far) = after(out_parts, (frames_delta, fed_far))
    out_sum = sum_blocks(meta, out_parts, [])
    out_blocks = z_swaps(out_sum.block, dp_size)
    total = out_sum.extra if alone else got.sums
    step = 1
    while step < planes:
        total += plane_swap(total, step, planes)
        step *= 2
    if not alone:
        for step in range(1, dp_size.bit_length() - 1):
            total += dp_swap(total, 1 << step, dp_size)
        total += across(total)
    out_far = [across(b) for b in out_blocks]
    if alone:
        up_change, down_change, upbias_change = fed_far.up, fed_far.down, fed_far.bias
        ended = out_end(meta, out_blocks, out_far, out_sum.extra, total)
        query_change, key_change, value_change, out_change = ended.query, ended.key, ended.value, ended.out
        qbias_change, vbias_change, total = ended.query_bias, ended.value_bias, ended.small
    else:
        fed_near, fed_far = from_z(fed_blocks, dp_at, dp_size), from_z(fed_far, dp_at, dp_size)
        up_change = ordered(fed_near[:half], fed_far[:half], core, 0).astype(F32)
        down_change = ordered(from_blocks(fed_near[half:], half), from_blocks(fed_far[half:], half), core, 1)
        down_change = down_change.astype(F32)
        upbias_change = fed_sum.extra[0]
        out_near, out_far = from_z(out_blocks, dp_at, dp_size), from_z(out_far, dp_at, dp_size)
        qkvo_change = ordered(out_near, out_far, core, 0).astype(F32)
        query_change, key_change, value_change, out_change = jnp.split(qkvo_change, 4, axis=1)
        qbias_change, _, vbias_change, _ = jnp.split(out_sum.extra[0], 4)
        out_change = out_change.T
    return (
        turned.layer[None],
        frames_delta[None],
        total[0],
        total[1],
        query_change,
        qbias_change,
        key_change,
        value_change,
        vbias_change,
        out_change,
        total[4],
        total[2],
        total[3],
        up_change,
        upbias_change,
        down_change,
        total[5],
    )


def solution(mesh):
    rows = P((DP, *PLANE), None, None)
    cols = P(None, PLANE)
    flat = P(PLANE)
    down = P(PLANE, None)
    every = P()
    placed = (
        rows, P((DP, *PLANE), None), rows, every, every, cols, flat, cols, cols, flat,
        down, every, every, every, cols, flat, down, every,
    )
    outs = (
        rows, rows, every, every, cols, flat, cols, cols, flat, down, every, every, every, cols, flat, down, every,
    )
    return jax.shard_map(shards, mesh=mesh, in_specs=placed, out_specs=outs, check_vma=False)
```

```python
import functools
import math

import jax
import jax.numpy as jnp
from jax import lax
from jax.experimental import pallas as pl
from jax.experimental.pallas import tpu as pltpu
from jax.sharding import PartitionSpec as P

HEAD_DIM = 64
PAIR = 2 * HEAD_DIM
TRIPLE = 3 * PAIR
BLOCK = 128
ROWS = 256
EXTRA = 16
EPSILON = 1e-05
MASKED = -1e30
SPANS = (3, 5, 6, 8)
DP = "dp"
PLANE = ("aa", "ba")

F32 = jnp.float32
BF16 = jnp.bfloat16
NN = (((1,), (0,)), ((), ()))
NT = (((1,), (1,)), ((), ()))
TN = (((0,), (0,)), ((), ()))
SPARE = 8 * 1024 * 1024
LARGE = 61 * 1024 * 1024
VMEM = pl.BlockSpec(memory_space=pltpu.VMEM)
SMEM = pl.BlockSpec(memory_space=pltpu.SMEM)
PACE = 1e6


def dot(left, right, dims=NN):
    return lax.dot_general(left, right, dims, preferred_element_type=F32)


def shape(dims, dtype):
    return jax.ShapeDtypeStruct(tuple(dims), dtype)


class Bag(dict):
    def __getattr__(self, name):
        if name not in self:
            raise AttributeError(name)
        return self[name]


jax.tree_util.register_pytree_node(
    Bag, lambda bag: (tuple(bag.values()), tuple(bag)), lambda names, values: Bag(zip(names, values))
)


def leaves(tree):
    if isinstance(tree, dict):
        tree = list(tree.values())
    if isinstance(tree, (list, tuple)):
        return [leaf for part in tree for leaf in leaves(part)]
    return [tree]


def rebuilt(tree, values):
    if isinstance(tree, dict):
        return Bag({key: rebuilt(part, values) for key, part in tree.items()})
    if isinstance(tree, (list, tuple)):
        return [rebuilt(part, values) for part in tree]
    return next(values)


def staged(body, meta, ins, outs, scratch, microseconds, kept=(), room=None):
    kept = leaves(list(kept))
    given, made = leaves(ins), leaves(outs)

    def kernel(*refs):
        table, refs = refs[0], refs[1 + len(kept) :]
        ours, refs = refs[: len(given)], refs[len(given) :]
        theirs, rest = refs[: len(made)], refs[len(made) :]
        body(table, rebuilt(ins, iter(ours)), rebuilt(outs, iter(theirs)), *rest)

    if room is None:
        room = sum(math.prod(v.shape) * jnp.dtype(v.dtype).itemsize for v in scratch) + SPARE
    got = pl.pallas_call(
        kernel,
        out_shape=made,
        in_specs=[SMEM] + [VMEM] * (len(kept) + len(given)),
        out_specs=[VMEM] * len(made),
        scratch_shapes=list(scratch),
        compiler_params=pltpu.CompilerParams(vmem_limit_bytes=room),
        cost_estimate=pl.CostEstimate(flops=1000, bytes_accessed=int(microseconds * PACE), transcendentals=0),
    )(meta, *kept, *given)
    return rebuilt(outs, iter(got))


def centred(values):
    centre = jnp.mean(values, axis=-1, keepdims=True)
    offset = values - centre
    spread = jnp.mean(offset * offset, axis=-1, keepdims=True)
    scale = lax.rsqrt(spread + EPSILON)
    return offset * scale, scale


def lane_of(dims):
    return lax.broadcasted_iota(jnp.int32, dims, 1)


def my_half(table, half):
    core = table[0, 0]
    mine = pl.ds(pl.multiple_of(core * half, half), half)
    other = pl.ds(pl.multiple_of((1 - core) * half, half), half)
    return mine, other


def scalars(core, labels):
    length = labels.shape[1]
    first_q, last_q = labels[0, ::ROWS], labels[0, ROWS - 1 :: ROWS]
    first_k, last_k = labels[0, ::BLOCK], labels[0, BLOCK - 1 :: BLOCK]
    low = jnp.sum((last_k[None, :] < first_q[:, None]).astype(jnp.int32), axis=1)
    above = jnp.sum((first_k[None, :] > last_q[:, None]).astype(jnp.int32), axis=1)
    count = length // BLOCK - above - low
    return jnp.concatenate([core.astype(jnp.int32)[None], low, count])[None]


def open_kernel(labels, q, k, v, o, qb, vb, *refs):
    rows, (own, other, vectors, table) = refs[:-4], refs[-4:]
    half = own.shape[0] - EXTRA
    length = labels.shape[1]
    place = lax.axis_index(DP)
    core = lax.rem(place, 2)
    for pack, at in ((own, core), (other, 1 - core)):
        part = pl.ds(pl.multiple_of(at * half, half), half)
        for i, w in enumerate((q, k, v)):
            pack[:half, i * PAIR : (i + 1) * PAIR] = w[part, :]
        pack[:half, TRIPLE:] = o[:, part].T
        pack[half:, :] = jnp.zeros((EXTRA, 4 * PAIR), BF16)
        for i, b in ((0, qb), (2, vb)):
            wide = jnp.broadcast_to(b[...].astype(F32).reshape(1, PAIR), (EXTRA, PAIR))
            pack[half:, i * PAIR : (i + 1) * PAIR] = wide.astype(BF16)
    vectors[...] = jnp.zeros_like(vectors)
    for i, r in enumerate(rows):
        vectors[i : i + 1, :] = r[...].astype(F32).reshape(1, r.shape[0])
    table[0, 0] = core
    table[0, 15] = lax.div(place, 2)
    queries, blocks = length // ROWS, length // BLOCK
    for at in range(queries):
        first, last = labels[0, at * ROWS], labels[0, (at + 1) * ROWS - 1]
        low, high = jnp.int32(0), jnp.int32(blocks)
        for b in range(blocks):
            low += (labels[0, (b + 1) * BLOCK - 1] < first).astype(jnp.int32)
            high -= (labels[0, b * BLOCK] > last).astype(jnp.int32)
        table[0, 1 + at] = low
        table[0, 1 + queries + at] = high - low


def opened(labels, q, k, v, o, qb, vb, rows):
    width = q.shape[0]
    pack = shape((width // 2 + EXTRA, 4 * PAIR), BF16)
    return pl.pallas_call(
        open_kernel,
        out_shape=[pack, pack, shape((8, width), F32), shape((1, 16), jnp.int32)],
        in_specs=[SMEM] + [VMEM] * (6 + len(rows)),
        out_specs=[VMEM, VMEM, VMEM, SMEM],
        compiler_params=pltpu.CompilerParams(vmem_limit_bytes=LARGE),
        cost_estimate=pl.CostEstimate(flops=1000, bytes_accessed=int(2 * PACE), transcendentals=0),
    )(labels, q, k, v, o, qb, vb, *rows)


def each_query_block(table, length, body, spans):
    blocks = length // BLOCK
    queries = length // ROWS

    def step(at, carry):
        low = table[0, 1 + at]
        count = table[0, 1 + queries + at]
        under = 0
        for span in [s for s in spans if s < blocks] + [blocks]:
            base = jnp.minimum(low, blocks - span)

            @pl.when((count > under) & (count <= span))
            def _():
                body(at, base, span)

            under = span
        return carry

    lax.fori_loop(0, queries, step, 0)


def clip_marks(labels, at):
    clip = lax.broadcasted_iota(jnp.int32, (BLOCK, ROWS), 0)
    same = clip == labels[:, pl.ds(at, ROWS)]
    hot = jnp.where(same, 1.0, 0.0).T.astype(BF16)
    cold = jnp.where(same, 0.0, MASKED).T.astype(BF16)
    return hot, cold


def split_heads(wide):
    low = lane_of(wide.shape) < HEAD_DIM
    zero = jnp.zeros_like(wide)
    return jnp.where(low, wide, zero), jnp.where(low, zero, wide)


def attend_scratch(groups, length):
    return [
        pltpu.VMEM((groups, 2 * length, 2 * PAIR), BF16),
        pltpu.VMEM((groups, length, 2 * PAIR), BF16),
        pltpu.VMEM((2 * groups, HEAD_DIM + EXTRA, length), BF16),
        pltpu.VMEM((2 * groups, length, ROWS), BF16),
    ]


def attend(table, labels, norm_tile, packs, qkv, mixed, lse, qm, ke, vt, probs):
    length = qkv[0].shape[0]
    half = packs[0][0].shape[0] - EXTRA
    mine, other = my_half(table, half)
    for tile in range(length // ROWS):
        at = tile * ROWS
        rows = pl.ds(at, ROWS)
        normed = norm_tile(rows)
        hot, cold = clip_marks(labels, at)
        for g, (own, far) in enumerate(packs):
            y = dot(normed[rows, mine], own[:half, :TRIPLE])
            y += dot(normed[rows, other], far[:half, :TRIPLE])
            y += own[half:, :TRIPLE][:1].astype(F32)
            q = (y[:, :PAIR] * HEAD_DIM ** (-0.5)).astype(BF16)
            k = y[:, PAIR : 2 * PAIR].astype(BF16)
            v = y[:, 2 * PAIR :].astype(BF16)
            qkv[g][rows, :PAIR] = q
            qkv[g][rows, PAIR : 2 * PAIR] = k
            qkv[g][rows, 2 * PAIR :] = v
            for head, part in enumerate(split_heads(q)):
                to = pl.ds(2 * at + head * ROWS, ROWS)
                qm[g, to, :PAIR] = part
                qm[g, to, PAIR:] = hot
            ke[g, rows, :PAIR] = k
            ke[g, rows, PAIR:] = cold
            turned = v.T
            for head in range(2):
                vt[2 * g + head, :HEAD_DIM, rows] = turned[head * HEAD_DIM : (head + 1) * HEAD_DIM]
                vt[2 * g + head, HEAD_DIM:, rows] = jnp.ones((EXTRA, ROWS), BF16)
    for out in lse:
        out[...] = jnp.zeros_like(out)

    def body(at, base, span):
        keys = pl.ds(pl.multiple_of(base * BLOCK, BLOCK), span * BLOCK)
        rows = pl.ds(pl.multiple_of(at * ROWS, ROWS), ROWS)
        peaks = []
        for g in range(len(packs)):
            for head in range(2):
                queries = pl.ds(pl.multiple_of((2 * at + head) * ROWS, ROWS), ROWS)
                scores = dot(ke[g, keys, :], qm[g, queries, :], NT)
                peaks.append(jnp.max(scores, axis=0, keepdims=True))
                probs[2 * g + head, : span * BLOCK, :] = jnp.exp(scores - peaks[-1]).astype(BF16)
        for g in range(len(packs)):
            heads = []
            for head in range(2):
                out = dot(vt[2 * g + head, :, keys], probs[2 * g + head, : span * BLOCK, :])
                total = out[HEAD_DIM : HEAD_DIM + 1]
                heads.append(out[:HEAD_DIM] * (1.0 / total))
                lse[g][head : head + 1, rows] = peaks[2 * g + head] + jnp.log(total)
            mixed[g][rows, :] = jnp.concatenate(heads, axis=0).T.astype(BF16)

    each_query_block(table, length, body, SPANS)


def attend_outs(groups, length):
    return Bag(
        qkv=[shape((length, TRIPLE), BF16)] * groups,
        mixed=[shape((length, PAIR), BF16)] * groups,
        lse=[shape((8, length), F32)] * groups,
    )


def feed_pack_into(pack, up, down, bias, rows, half):
    hidden = up.shape[1]
    pack[:half, :] = up[rows, :]
    for b in range(0, hidden, half):
        pack[half : 2 * half, b : b + half] = down[b : b + half, rows]
    pack[2 * half :, :] = jnp.broadcast_to(bias, (EXTRA, hidden)).astype(BF16)


def first_body(table, ins, outs, *scratch):
    vectors = ins.vectors

    def norm_tile(rows):
        xhat, _ = centred(ins.frames[rows, :].astype(F32))
        outs.xhat[rows, :] = xhat.astype(BF16)
        outs.normed[rows, :] = (xhat * vectors[0:1, :] + vectors[1:2, :]).astype(BF16)
        return outs.normed

    attend(table, ins.labels, norm_tile, [ins.pack], outs.qkv, outs.mixed, outs.lse, *scratch)
    if len(ins.feed):
        up, down = ins.feed
        half = up.shape[0] // 2
        for pack, rows in zip(outs.feed, my_half(table, half)):
            feed_pack_into(pack, up, down, vectors[6:7, :], rows, half)


def first(meta, labels, frames, vectors, pack, feed):
    length, width = frames.shape
    outs = attend_outs(1, length)
    outs.update(
        normed=shape((length, width), BF16),
        xhat=shape((length, width), BF16),
        feed=[shape((width + EXTRA, up.shape[1]), BF16) for up in feed],
    )
    ins = Bag(labels=labels, vectors=vectors, pack=list(pack), frames=frames, feed=list(feed))
    return staged(first_body, meta, ins, outs, attend_scratch(1, length), 9, room=LARGE)


def second_body(table, ins, outs, *scratch):
    attend(table, ins.labels, lambda rows: ins.normed, ins.packs, outs.qkv, outs.mixed, outs.lse, *scratch)


def second(meta, labels, normed, packs, kept):
    length, width = normed.shape
    groups = len(packs)
    ins = Bag(labels=labels, packs=[list(pair) for pair in packs], normed=normed)
    scratch = attend_scratch(groups, length)
    return staged(second_body, meta, ins, attend_outs(groups, length), scratch, 13, kept)


def join_body(table, ins, outs, normed_s):
    length, width = ins.frames.shape
    half = width // 2
    vectors, inner = ins.vectors, outs.inner
    for tile in range(length // ROWS):
        rows = pl.ds(tile * ROWS, ROWS)
        for which, cols in enumerate(my_half(table, half)):
            total = ins.frames[rows, cols].astype(F32) + vectors[2:3, cols]
            for m, pack in zip(ins.mixed, ins.packs):
                total += dot(m[rows, :], pack[which][:half, TRIPLE:], NT)
            inner[rows, cols] = total
        xhat, _ = centred(inner[rows, :])
        normed_s[rows, :] = (xhat * vectors[3:4, :] + vectors[4:5, :]).astype(BF16)
        for which, cols in enumerate(my_half(table, half)):
            to = slice(which * half, (which + 1) * half)
            outs.normed[rows, to] = normed_s[rows, cols]
            outs.cot[rows, to] = ins.cot[rows, cols]


def join(meta, frames, vectors, mixed, packs, cot, kept):
    ins = Bag(frames=frames, vectors=vectors, mixed=list(mixed), packs=[list(pair) for pair in packs], cot=cot)
    outs = Bag(inner=shape(frames.shape, F32), normed=shape(frames.shape, BF16), cot=shape(frames.shape, BF16))
    return staged(join_body, meta, ins, outs, [pltpu.VMEM(frames.shape, BF16)], 4, kept)


def gelu_both(u):
    falling = jnp.exp(u * u * -0.5)
    t = 1.0 / (1.0 + jnp.abs(u) * (0.3275911 * 0.5**0.5))
    poly = 0.5 * 1.061405429
    for c in (-1.453152027, 1.421413741, -0.284496736, 0.254829592):
        poly = poly * t + 0.5 * c
    tail = poly * t * falling
    phi = jnp.where(u >= 0.0, 1.0 - tail, tail)
    return u * phi, phi + u * falling * (0.5 / jnp.pi) ** 0.5


def feed_body(count, table, ins, outs, up, down, act, delta):
    length, width = ins.normed.shape
    half = width // 2
    hidden = ins.feed[0][0].shape[1]
    bias = []
    for i, pair in enumerate(ins.feed):
        at = i * hidden
        bias.append(pair[0][2 * half :, :][:1].astype(F32))
        for which, pack in enumerate(pair):
            part = slice(which * half, (which + 1) * half)
            up[part, at : at + hidden] = pack[:half, :]
            for b in range(0, hidden, half):
                down[at + b : at + b + half, part] = pack[half : 2 * half, b : b + half]
    bias = jnp.concatenate(bias, axis=1)

    def outward(rows):
        for i, (grad, to) in enumerate(((True, outs.two), (False, outs.out))):
            total = dot(delta[rows, :], up[...], NT) if grad else dot(act[rows, :], down[...])
            for which, cols in enumerate(my_half(table, half)):
                part = total[:, which * half : (which + 1) * half]
                for before in ins.before:
                    part += before[i][rows, cols]
                to[rows, cols] = part

    late = None
    for rows in [pl.ds(at, ROWS) for at in range(0, length, ROWS)]:
        u = dot(ins.normed[rows, :], up[...]) + bias
        back = dot(ins.cot[rows, :], down[...], NT)
        if late is not None:
            outward(late)
        active, slope = gelu_both(u)
        act[rows, :] = active.astype(BF16)
        delta[rows, :] = (back * slope).astype(BF16)
        late = rows
    outward(late)
    for i, packs in enumerate(zip(outs.keep, outs.send)):
        mine = slice(i * hidden, (i + 1) * hidden)
        up_delta = dot(ins.normed[...], delta[:, mine], TN)
        down_delta = dot(act[:, mine], ins.cot[...], TN)
        total = jnp.sum(delta[:, mine].astype(F32), axis=0, keepdims=True)
        for which, pack in enumerate(packs):
            part = slice(which * half, (which + 1) * half)
            pack[:half, :] = up_delta[part, :].astype(BF16)
            for b in range(0, hidden, half):
                pack[half : 2 * half, b : b + half] = down_delta[b : b + half, part].astype(BF16)
            pack[2 * half :, :] = jnp.broadcast_to(total, (EXTRA, hidden)).astype(BF16)


def feed(meta, normed, cot, before, packs, kept):
    length, width = normed.shape
    hidden = packs[0][0].shape[1]
    count = len(packs)
    ins = Bag(feed=[list(pair) for pair in packs], normed=normed, cot=cot, before=before)
    pack = shape(packs[0][0].shape, BF16)
    outs = Bag(
        keep=[pack] * count, send=[pack] * count, two=shape((length, width), F32), out=shape((length, width), F32)
    )
    scratch = [
        pltpu.VMEM((width, count * hidden), BF16),
        pltpu.VMEM((count * hidden, width), BF16),
        pltpu.VMEM((length, count * hidden), BF16),
        pltpu.VMEM((length, count * hidden), BF16),
    ]
    return staged(functools.partial(feed_body, count), meta, ins, outs, scratch, 4 * count, kept)


def turn_body(table, ins, outs):
    length, width = ins.inner.shape
    half = width // 2
    mine, other = my_half(table, half)
    sums, pulls, packs = outs.sums, outs.pulls, ins.packs
    sums[...] = jnp.zeros_like(sums)
    pulls[...] = jnp.zeros_like(pulls)
    dims = (8, PAIR)
    picks = lax.broadcasted_iota(jnp.int32, dims, 0) == lane_of(dims) // HEAD_DIM
    ones = jnp.where(picks, 1.0, 0.0).astype(BF16)
    for tile in range(length // ROWS):
        rows = pl.ds(tile * ROWS, ROWS)
        inner = ins.inner[rows, :]
        outs.layer[rows, :] = (inner + ins.out[rows, :] + ins.vectors[5:6, :]).astype(BF16)
        xhat, scale = centred(inner)
        two = ins.two[rows, :]
        dy = ins.cot[rows, :].astype(F32)
        e = two * ins.vectors[3:4, :]
        lean = jnp.mean(e, axis=-1, keepdims=True)
        pull = jnp.mean(e * xhat, axis=-1, keepdims=True)
        delta = dy + scale * (e - lean - xhat * pull)
        outs.delta[rows, :] = delta
        branch = delta.astype(BF16)
        outs.branch[rows, :] = branch
        for at, part in enumerate((two * xhat, two, branch.astype(F32), dy)):
            sums[2 + at : 3 + at, :] += jnp.sum(part, axis=0, keepdims=True)
        for g, m in enumerate(ins.mixed):
            back = dot(outs.branch[rows, mine], packs[g][0][:half, TRIPLE:])
            back += dot(outs.branch[rows, other], packs[g][1][:half, TRIPLE:])
            back = back.astype(BF16)
            outs.back[g][rows, :] = back
            product = back.astype(F32) * m[rows, :].astype(F32)
            high = product.astype(BF16)
            low = (product - high.astype(F32)).astype(BF16)
            pulls[2 * g : 2 * g + 2, rows] = (dot(ones, high, NT) + dot(ones, low, NT))[:2]


def back_body(at_rows, table, ins, outs, qm, ke, ve, dmm, kt, dk, dv, ds, probs, tilts):
    groups = len(at_rows)
    length = ins.qkv[0].shape[0]
    blocks = length // BLOCK
    for tile in range(length // ROWS):
        at = tile * ROWS
        rows = pl.ds(at, ROWS)
        hot, cold = clip_marks(ins.labels, at)
        for g in range(groups):
            qkv, down = ins.qkv[g], ins.back[g]
            q = qkv[rows, :PAIR]
            k = qkv[rows, PAIR : 2 * PAIR]
            for head, (part, d) in enumerate(zip(split_heads(q), split_heads(down[rows, :]))):
                to = pl.ds(2 * at + head * ROWS, ROWS)
                qm[g, to, :PAIR] = part
                qm[g, to, PAIR:] = hot
                dmm[g, to, :] = d
            ke[g, rows, :PAIR] = k
            ke[g, rows, PAIR:] = cold
            ve[g, rows, :] = qkv[rows, 2 * PAIR :]
            kt[g, :, rows] = k.T
            dk[g, rows, :] = jnp.zeros((ROWS, PAIR), F32)
            dv[g, rows, :] = jnp.zeros((ROWS, PAIR), F32)

    def body(at, base, span):
        rows = pl.ds(pl.multiple_of(at * ROWS, ROWS), ROWS)
        both = pl.ds(pl.multiple_of(at * 2 * ROWS, 2 * ROWS), 2 * ROWS)
        queries = [qm[g, both, :] for g in range(groups)]
        downs = [dmm[g, both, :] for g in range(groups)]
        dqt = [[jnp.zeros((HEAD_DIM, ROWS), F32)] * 2 for _ in range(groups)]
        items = [(g, done, min(2, span - done)) for g in range(groups) for done in range(0, span, 2)]

        def weigh(slot, g, done, size):
            keys = pl.ds(pl.multiple_of((base + done) * BLOCK, BLOCK), size * BLOCK)
            for head in range(2):
                cut = slice(head * ROWS, (head + 1) * ROWS)
                scores = dot(ke[g, keys, :], queries[g][cut], NT)
                slope = dot(ve[g, keys, :], downs[g][cut], NT)
                p = jnp.exp(scores - ins.lse[g][head : head + 1, rows])
                at_row = at_rows[g] + head
                delta = p * (slope - ins.pulls[at_row : at_row + 1, rows])
                probs[slot, : size * BLOCK, cut] = p.astype(BF16)
                tilts[slot, : size * BLOCK, cut] = delta.astype(BF16)

        def gather(slot, g, done, size):
            keys = pl.ds(pl.multiple_of((base + done) * BLOCK, BLOCK), size * BLOCK)
            part = slice(0, size * BLOCK)
            dv[g, keys, :] += dot(probs[slot, part, :], downs[g])
            dk[g, keys, :] += dot(tilts[slot, part, :], queries[g][:, :PAIR])
            for head in range(2):
                cut = slice(head * ROWS, (head + 1) * ROWS)
                wide = kt[g, head * HEAD_DIM : (head + 1) * HEAD_DIM, keys]
                dqt[g][head] += dot(wide, tilts[slot, part, cut])

        for i, item in enumerate(items):
            weigh(i % 2, *item)
            if i:
                gather((i - 1) % 2, *items[i - 1])
        gather((len(items) - 1) % 2, *items[-1])
        for g in range(groups):
            dq = jnp.concatenate(dqt[g], axis=0).T.astype(BF16).astype(F32) * HEAD_DIM ** (-0.5)
            ds[g, rows, :PAIR] = dq.astype(BF16)

    each_query_block(table, length, body, range(2, blocks))
    half = ins.normed.shape[1] // 2
    halves = my_half(table, half)
    for g in range(groups):
        ds[g, :, PAIR : 2 * PAIR] = dk[g].astype(BF16)
        ds[g, :, 2 * PAIR :] = dv[g].astype(BF16)
        every = ds[g]
        for cols, pack in zip(halves[::-1], (outs.send[g], outs.keep[g])):
            pack[:half, :TRIPLE] = dot(ins.normed[:, cols], every, TN).astype(BF16)
            pack[:half, TRIPLE:] = dot(ins.branch[:, cols], ins.mixed[g][...], TN).astype(BF16)
    outs.sums[...] = ins.sums[...]
    for tile in range(length // ROWS):
        rows = pl.ds(tile * ROWS, ROWS)
        for which, cols in enumerate(halves):
            part = dot(ds[0, rows, :], ins.packs[0][which][:half, :TRIPLE], NT)
            for g in range(1, groups):
                part += dot(ds[g, rows, :], ins.packs[g][which][:half, :TRIPLE], NT)
            outs.sums[0:1, cols] += jnp.sum(part * ins.xhat[rows, cols].astype(F32), axis=0, keepdims=True)
            outs.sums[1:2, cols] += jnp.sum(part, axis=0, keepdims=True)
            for before in ins.one:
                part += before[rows, cols]
            outs.one[rows, cols] = part
    for g in range(groups):
        total = jnp.sum(ds[g].astype(F32), axis=0, keepdims=True)
        total = jnp.concatenate([total, jnp.zeros((1, PAIR), F32)], axis=1)
        extra = jnp.broadcast_to(total, (EXTRA, 4 * PAIR)).astype(BF16)
        outs.send[g][half:, :] = extra
        outs.keep[g][half:, :] = extra


def back_scratch(groups, length):
    return [
        pltpu.VMEM((groups, 2 * length, 2 * PAIR), BF16),
        pltpu.VMEM((groups, length, 2 * PAIR), BF16),
        pltpu.VMEM((groups, length, PAIR), BF16),
        pltpu.VMEM((groups, 2 * length, PAIR), BF16),
        pltpu.VMEM((groups, PAIR, length), BF16),
        pltpu.VMEM((groups, length, PAIR), F32),
        pltpu.VMEM((groups, length, PAIR), F32),
        pltpu.VMEM((groups, length, TRIPLE), BF16),
        pltpu.VMEM((2, 2 * BLOCK, 2 * ROWS), BF16),
        pltpu.VMEM((2, 2 * BLOCK, 2 * ROWS), BF16),
    ]


def back_outs(groups, length, width):
    pack = shape((width // 2 + EXTRA, 4 * PAIR), BF16)
    return Bag(
        send=[pack] * groups, keep=[pack] * groups, one=shape((length, width), F32), sums=shape((8, width), F32)
    )


def back(meta, given, one, sums, part, kept):
    length, width = given.normed.shape
    ins = Bag(
        labels=given.labels,
        qkv=[given.qkv[g] for g in part],
        back=[given.back[g] for g in part],
        lse=[given.lse[g] for g in part],
        pulls=given.pulls,
        normed=given.normed,
        xhat=given.xhat,
        branch=given.branch,
        mixed=[given.mixed[g] for g in part],
        packs=[list(given.packs[g]) for g in part],
        one=[one],
        sums=sums,
    )
    outs = back_outs(len(part), length, width)
    body = functools.partial(back_body, [2 * g for g in part])
    return staged(body, meta, ins, outs, back_scratch(len(part), length), 8 * len(part), kept)


def turn_back_body(part, table, ins, outs, sums, *scratch):
    turned = Bag(outs.turned)
    turned.update(sums=sums)
    turn_body(table, ins.turn, turned)
    given = Bag(ins.back)
    given.update(
        back=[outs.turned.back[g] for g in part], pulls=outs.turned.pulls, branch=outs.turned.branch, one=[], sums=sums
    )
    back_body([2 * g for g in part], table, given, outs.back, *scratch)


def turn_back(meta, given, inner, two, out, cot, vectors, part, kept):
    length, width = inner.shape
    ins = Bag(
        turn=Bag(
            inner=inner,
            two=two,
            out=out,
            cot=cot,
            vectors=vectors,
            mixed=list(given.mixed),
            packs=[list(p) for p in given.packs],
        ),
        back=Bag(
            labels=given.labels,
            qkv=[given.qkv[g] for g in part],
            lse=[given.lse[g] for g in part],
            normed=given.normed,
            xhat=given.xhat,
            mixed=[given.mixed[g] for g in part],
            packs=[list(given.packs[g]) for g in part],
        ),
    )
    groups = len(given.mixed)
    outs = Bag(
        turned=Bag(
            layer=shape((length, width), BF16),
            pulls=shape((max(8, 2 * groups), length), F32),
            delta=shape((length, width), F32),
            branch=shape((length, width), BF16),
            back=[shape((length, PAIR), BF16)] * groups,
        ),
        back=back_outs(len(part), length, width),
    )
    scratch = [pltpu.VMEM((8, width), F32)] + back_scratch(len(part), length)
    return staged(functools.partial(turn_back_body, part), meta, ins, outs, scratch, 14, kept)


def close_body(table, ins, outs):
    length, width = ins.frames.shape
    for tile in range(length // ROWS):
        rows = pl.ds(tile * ROWS, ROWS)
        xhat, scale = centred(ins.frames[rows, :].astype(F32))
        e = ins.one[rows, :] * ins.vectors[0:1, :]
        lean = jnp.mean(e, axis=-1, keepdims=True)
        pull = jnp.mean(e * xhat, axis=-1, keepdims=True)
        outs.frames_delta[rows, :] = (ins.delta[rows, :] + scale * (e - lean - xhat * pull)).astype(BF16)


def close(meta, frames, vectors, delta, one, kept):
    ins = Bag(vectors=vectors, frames=frames, delta=delta, one=one)
    outs = Bag(frames_delta=shape(frames.shape, BF16))
    return staged(close_body, meta, ins, outs, [], 3, kept).frames_delta


def cut_body(table, ins, outs):
    size = outs.blocks[0].shape[0] - EXTRA
    rows = size * len(outs.blocks)
    place = table[0, 15]
    end = sum(p[rows:, :].astype(F32) for p in ins.pieces).astype(BF16)
    for j, block in enumerate(outs.blocks):
        at = pl.ds(pl.multiple_of(jnp.bitwise_xor(place, j) * size, size), size)
        block[:size, :] = sum(p[at, :].astype(F32) for p in ins.pieces).astype(BF16)
        block[size:, :] = end


def cut_blocks(meta, pieces, count, kept):
    rows, cols = pieces[0].shape
    block = shape(((rows - EXTRA) // count + EXTRA, cols), BF16)
    return staged(cut_body, meta, Bag(pieces=list(pieces)), Bag(blocks=[block] * count), [], 2, kept).blocks


def sum_body(table, ins, outs):
    total = sum(p[...].astype(F32) for p in ins.parts)
    size = total.shape[0] - EXTRA
    outs.extra[...] = total[size:]
    outs.block[:size, :] = total[:size].astype(BF16)
    if ins.small:
        small = ins.small[0][...]
        high = small.astype(BF16).astype(F32)
        outs.block[size:, :] = jnp.concatenate([high, small - high], axis=0).astype(BF16)


def sum_blocks(meta, parts, small, kept):
    rows, cols = parts[0].shape
    outs = Bag(block=shape((rows if small else rows - EXTRA, cols), BF16), extra=shape((EXTRA, cols), F32))
    return staged(sum_body, meta, Bag(parts=list(parts), small=list(small)), outs, [], 1, kept)


def ordered_into(table, blocks, pack_s):
    size = pack_s.shape[0] // len(blocks)
    for j, block in enumerate(blocks):
        at = pl.ds(pl.multiple_of(jnp.bitwise_xor(table[0, 15], j) * size, size), size)
        pack_s[at, :] = block[:size, :].astype(F32)


def feed_end_body(count, table, ins, outs, pack_s):
    width, hidden = outs.up.shape
    half = width // 2
    for cols, stack in zip(my_half(table, half), (ins.near, ins.far)):
        size = stack.shape[0] // count
        ordered_into(table, [stack.at[pl.ds(j * size, size)] for j in range(count)], pack_s)
        outs.up[cols, :] = pack_s[:half, :]
        for b in range(0, hidden, half):
            outs.down[b : b + half, cols] = pack_s[half:, b : b + half]
    outs.bias[...] = ins.extra[0:1, :].reshape(hidden)


def feed_end(meta, near, far, extra, count, width, hidden):
    ins = Bag(near=near, far=far, extra=extra)
    outs = Bag(up=shape((width, hidden), F32), down=shape((hidden, width), F32), bias=shape((hidden,), F32))
    return staged(
        functools.partial(feed_end_body, count), meta, ins, outs, [pltpu.VMEM((width, hidden), F32)], 3
    )


def out_end_body(table, ins, outs, pack_s):
    half = pack_s.shape[0]
    for cols, blocks in zip(my_half(table, half), (ins.blocks, ins.far)):
        ordered_into(table, blocks, pack_s)
        for i, to in enumerate((outs.query, outs.key, outs.value)):
            to[cols, :] = pack_s[:, i * PAIR : (i + 1) * PAIR]
        outs.out[:, cols] = pack_s[:, TRIPLE:].T
    row = ins.extra[0:1, :]
    outs.query_bias[...] = row[:, :PAIR].reshape(PAIR)
    outs.value_bias[...] = row[:, 2 * PAIR : TRIPLE].reshape(PAIR)
    size = ins.blocks[0].shape[0] - EXTRA
    small = sum(block[size:, :].astype(F32) for block in ins.blocks)
    small = small[:8] + small[8:]
    for i, to in enumerate(outs.small):
        to[...] = small[i : i + 1, :].reshape(to.shape[0])


def out_end(meta, blocks, far, extra, width):
    ins = Bag(blocks=list(blocks), far=list(far), extra=extra)
    outs = Bag(
        query=shape((width, PAIR), F32),
        key=shape((width, PAIR), F32),
        value=shape((width, PAIR), F32),
        out=shape((PAIR, width), F32),
        query_bias=shape((PAIR,), F32),
        value_bias=shape((PAIR,), F32),
        small=[shape((width,), F32)] * 6,
    )
    return staged(out_end_body, meta, ins, outs, [pltpu.VMEM((width // 2, 4 * PAIR), F32)], 2)


def plane_swap(value, step, size):
    return lax.ppermute(value, PLANE, [(i, i ^ step) for i in range(size)])


def dp_swap(value, step, size):
    return lax.ppermute(value, DP, [(i, i ^ step) for i in range(size)])


def to_blocks(value, half):
    rows = value.shape[0]
    if rows >= half:
        return jnp.concatenate(jnp.split(value, rows // half, axis=0), axis=1)
    return jnp.concatenate(jnp.split(value, half // rows, axis=1), axis=0)


def from_blocks(value, half):
    cols = value.shape[1]
    if cols >= half:
        return jnp.concatenate(jnp.split(value, cols // half, axis=1), axis=0)
    return jnp.concatenate(jnp.split(value, half // cols, axis=0), axis=1)


def extra_row(value):
    return jnp.pad(value[None], ((0, EXTRA - 1), (0, 0)))


def qkvo_pack(half_at, half, query, key, value, out, query_bias, value_bias):
    parts = [lax.dynamic_slice_in_dim(w, half_at, half, axis=0) for w in (query, key, value)]
    parts.append(lax.dynamic_slice_in_dim(out, half_at, half, axis=1).T)
    zero = jnp.zeros_like(query_bias)
    bias = jnp.concatenate([query_bias, zero, value_bias, zero])
    return jnp.concatenate([jnp.concatenate(parts, axis=1), extra_row(bias)], axis=0)


def feed_pack(half_at, half, up, up_bias, down):
    top = lax.dynamic_slice_in_dim(up, half_at, half, axis=0)
    low = to_blocks(lax.dynamic_slice_in_dim(down, half_at, half, axis=1), half)
    return jnp.concatenate([top, low, extra_row(up_bias)], axis=0)


def qkvo_join(shards):
    if len(shards) == 1:
        return shards[0]
    quarters = [jnp.split(s, 4, axis=1) for s in shards]
    return jnp.concatenate([q[i] for i in range(4) for q in quarters], axis=1)


def qkvo_cut(pack, count):
    if count == 1:
        return [pack]
    pieces = jnp.split(pack, 4 * count, axis=1)
    return [jnp.concatenate([pieces[i * count + s] for i in range(4)], axis=1) for s in range(count)]


def feed_join(shards, half):
    if len(shards) == 1:
        return shards[0]
    top = jnp.concatenate([s[:half] for s in shards], axis=1)
    low = jnp.concatenate([from_blocks(s[half : 2 * half], half) for s in shards], axis=0)
    end = jnp.concatenate([s[2 * half :] for s in shards], axis=1)
    return jnp.concatenate([top, to_blocks(low, half), end], axis=0)


def feed_cut(pack, count, half):
    if count == 1:
        return [pack]
    tops = jnp.split(pack[:half], count, axis=1)
    lows = jnp.split(from_blocks(pack[half : 2 * half], half), count, axis=0)
    ends = jnp.split(pack[2 * half :], count, axis=1)
    return [jnp.concatenate([t, to_blocks(l, half), e], axis=0) for t, l, e in zip(tops, lows, ends)]


def ordered(mine, other, core, axis):
    low = jnp.where(core == 0, mine, other)
    high = jnp.where(core == 0, other, mine)
    return jnp.concatenate([low, high], axis=axis)


def after(value, other):
    return lax.optimization_barrier((value, other))


def added(pieces):
    total = pieces[0].astype(F32)
    for piece in pieces[1:]:
        total += piece.astype(F32)
    return total.astype(BF16)


def z_swaps(pack, dp_size):
    return [pack] + [dp_swap(pack, k, dp_size) for k in range(2, dp_size, 2)]


def z_blocks(pack, dp_at, dp_size):
    rows, z_size = pack.shape[0] - EXTRA, dp_size // 2
    size = rows // z_size
    z_at = dp_at // 2

    def block(at):
        return jnp.concatenate([lax.dynamic_slice_in_dim(pack, at * size, size, axis=0), pack[rows:]], axis=0)

    return [block(z_at ^ k) for k in range(z_size)]


def from_z(blocks, dp_at, dp_size):
    stack = jnp.stack(blocks)
    z_at, z_size = dp_at // 2, dp_size // 2
    return jnp.concatenate([stack[z_at ^ j] for j in range(z_size)], axis=0)


def shards(
    frames,
    segment_ids,
    cotangent,
    first_gain,
    first_shift,
    query_weight,
    query_bias,
    key_weight,
    value_weight,
    value_bias,
    out_weight,
    out_bias,
    second_gain,
    second_shift,
    up_weight,
    up_bias,
    down_weight,
    down_bias,
):
    length, width = frames.shape[1:]
    half = width // 2
    planes = lax.axis_size(PLANE)
    dp_size = lax.axis_size(DP)
    dp_at = lax.axis_index(DP)
    core = dp_at % 2
    groups = width // PAIR
    per_group = planes // groups
    alone = per_group == 1
    x, dy, labels = frames[0], cotangent[0], segment_ids
    group_of = [range(g * per_group, (g + 1) * per_group) for g in range(groups)]
    last = groups - 1
    middle = list(range(1, last))
    peers = list(range(1, planes))
    late = [r for g in middle for r in group_of[g]]
    soon = list(group_of[last])
    rest = [r for r in group_of[0] if r]
    rows = (first_gain, first_shift, out_bias, second_gain, second_shift, down_bias)

    def far_half(near):
        return {r: dp_swap(v, 1, dp_size) for r, v in near.items()}

    def out_pair(g):
        return qkvo_join([near[r] for r in group_of[g]]), qkvo_join([far[r] for r in group_of[g]])

    def feed_pair(g):
        return feed_join([feed_near[r] for r in group_of[g]], half), feed_join([feed_far[r] for r in group_of[g]], half)

    if alone:
        own, other, vectors, meta = opened(
            labels,
            query_weight,
            key_weight,
            value_weight,
            out_weight,
            query_bias,
            value_bias,
            (*rows, up_bias),
        )
        near = {r: plane_swap(own, r, planes) for r in peers}
        one = first(meta, labels, x, vectors, (own, other), (up_weight, down_weight))
        near, one = after(near, one)
        far = far_half(near)
        feed_own, feed_other = one.feed
    else:
        meta = scalars(core, labels)
        zero = jnp.zeros((width,), F32)
        vectors = jnp.stack([v.astype(F32) for v in rows] + [zero] * 2)
        own, other = (
            qkvo_pack(c * half, half, query_weight, key_weight, value_weight, out_weight, query_bias, value_bias)
            for c in (core, 1 - core)
        )
        near = {r: plane_swap(own, r, planes) for r in peers}
        far = far_half(near)
        feed_own, feed_other = (feed_pack(c * half, half, up_weight, up_bias, down_weight) for c in (core, 1 - core))
    near[0], far[0] = own, other
    qkvo = [out_pair(g) for g in range(groups)]
    if not alone:
        one = first(meta, labels, x, vectors, qkvo[0], ())
    feed_near, feed_far = {0: feed_own}, {0: feed_other}
    feed_soon = {r: plane_swap(feed_own, r, planes) for r in soon + rest}
    two = second(meta, labels, one.normed, qkvo[1:], ())
    feed_soon, two = after(feed_soon, two)
    feed_near.update(feed_soon)
    feed_far.update(far_half(feed_soon))
    mixed, qkv, lse = one.mixed + two.mixed, one.qkv + two.qkv, one.lse + two.lse
    held = [two.qkv, two.lse, one.normed]
    joined = join(meta, x, vectors, mixed, qkvo, dy, held)
    feed_far, joined = after(feed_far, joined)
    feed_own, feed_soon = after(feed_own, feed_soon)
    feed_near.update({r: plane_swap(feed_own, r, planes) for r in late})

    def chip_sum(keep, far_send):
        return (keep.astype(F32) + far_send.astype(F32)).astype(BF16)

    def across(send):
        return dp_swap(send, 1, dp_size)

    def spread(pack, g, cut):
        return [plane_swap(p, r, planes) if r else p for r, p in zip(group_of[g], cut(pack))]

    def cut_feed(pack):
        return feed_cut(pack, per_group, half)

    def cut_qkvo(pack):
        return qkvo_cut(pack, per_group)

    held += [joined.inner, two.mixed, qkvo]
    three = feed(meta, joined.normed, joined.cot, (), [feed_pair(last), feed_pair(0)], held)
    feed_late, three = after({r: feed_near[r] for r in late}, three)
    feed_near.update(feed_late)
    feed_far.update(far_half(feed_late))
    far_send = across(three.send[0])
    middle_packs, far_send = after([feed_pair(g) for g in middle], far_send)
    feed_here = spread(chip_sum(three.keep[0], far_send), last, cut_feed)
    four = feed(meta, joined.normed, joined.cot, [[three.two, three.out]], middle_packs, held)
    four, feed_here = after(four, feed_here)
    three_send, four.send[0] = after(three.send[1], four.send[0])
    far_sends = [across(s) for s in four.send]
    two_sum, far_sends = after(four.two, far_sends)
    for i, g in enumerate(middle):
        feed_here += spread(chip_sum(four.keep[i], far_sends[i]), g, cut_feed)

    def along_z(parts):
        return [dp_swap(p, 2 * k, dp_size) if k else p for k, p in enumerate(parts)]

    def z_cut(pieces, kept):
        if alone:
            return cut_blocks(meta, pieces, dp_size // 2, kept)
        return z_blocks(added(pieces), dp_at, dp_size)

    given = Bag(labels=labels, normed=one.normed, xhat=one.xhat, qkv=qkv, lse=lse, mixed=mixed, packs=qkvo)
    far_send = across(three_send)
    got = turn_back(meta, given, joined.inner, two_sum, four.out, dy, vectors, [last], held)
    turned = got.turned
    given.update(pulls=turned.pulls, branch=turned.branch, back=turned.back)
    held = [two.qkv, two.lse, one.normed, mixed, qkvo, turned.back, turned.branch]
    got = got.back
    (feed_here, far_send), got = after((feed_here, far_send), got)
    if alone:
        feed_here += [three.keep[1], far_send]
    else:
        feed_here += spread(chip_sum(three.keep[1], far_send), 0, cut_feed)
    far_send = across(got.send[0])
    fed_parts = z_cut(feed_here, held + [got.one])
    labels, (fed_parts, far_send) = after(labels, (fed_parts, far_send))
    given.update(labels=labels)
    fed_parts = along_z(fed_parts)
    out_here = spread(chip_sum(got.keep[0], far_send), last, cut_qkvo)

    got = back(meta, given, got.one, got.sums, middle, held)
    (out_here, fed_parts), got = after((out_here, fed_parts), got)
    far_sends = [across(s) for s in got.send]
    fed_sum = sum_blocks(meta, fed_parts, (), held + [got.one])
    labels, (fed_sum, far_sends) = after(labels, (fed_sum, far_sends))
    given.update(labels=labels)
    fed_blocks = z_swaps(fed_sum.block, dp_size)
    for i, g in enumerate(middle):
        out_here += spread(chip_sum(got.keep[i], far_sends[i]), g, cut_qkvo)

    got = back(meta, given, got.one, got.sums, [0], held)
    (out_here, fed_blocks), got = after((out_here, fed_blocks), got)
    far_send, far_sums = after(across(got.send[0]), across(got.sums))
    if alone:
        out_parts = z_cut(out_here + [got.keep[0], far_send], [])
    else:
        out_here += spread(chip_sum(got.keep[0], far_send), 0, cut_qkvo)
        out_parts = z_cut(out_here, [])
    (vectors, fed_blocks), out_parts = after((vectors, fed_blocks), out_parts)
    out_parts = along_z(out_parts)
    frames_delta = close(meta, x, vectors, turned.delta, got.one, [])
    fed_near = jnp.concatenate(fed_blocks, axis=0)
    fed_far = across(fed_near)
    small, steps = got.sums + far_sums, [1 << i for i in range(planes.bit_length() - 1)]
    small += plane_swap(small, steps[0], planes)
    small, frames_delta = after(small, frames_delta)
    if alone:
        small, fed_far = after(small, fed_far)
        fed_far = feed_end(meta, fed_near, fed_far, fed_sum.extra, dp_size // 2, width, up_weight.shape[1])
    for step in steps[1:]:
        small += plane_swap(small, step, planes)
    out_parts, (fed_far, small) = after(out_parts, (fed_far, small))
    out_sum = sum_blocks(meta, out_parts, (small,) if alone else (), [])
    out_blocks = z_swaps(out_sum.block, dp_size)
    total = small
    for step in () if alone else range(1, dp_size.bit_length() - 1):
        total += dp_swap(total, 1 << step, dp_size)
    out_far = [across(b) for b in out_blocks]
    if alone:
        up_change, down_change, upbias_change = fed_far.up, fed_far.down, fed_far.bias
        ended = out_end(meta, out_blocks, out_far, out_sum.extra, width)
        query_change, key_change, value_change, out_change = ended.query, ended.key, ended.value, ended.out
        qbias_change, vbias_change, total = ended.query_bias, ended.value_bias, ended.small
    else:
        fed_near, fed_far = (from_z(jnp.split(f, dp_size // 2), dp_at, dp_size) for f in (fed_near, fed_far))
        up_change = ordered(fed_near[:half], fed_far[:half], core, 0).astype(F32)
        down_change = ordered(from_blocks(fed_near[half:], half), from_blocks(fed_far[half:], half), core, 1)
        down_change = down_change.astype(F32)
        upbias_change = fed_sum.extra[0]
        out_near, out_far = from_z(out_blocks, dp_at, dp_size), from_z(out_far, dp_at, dp_size)
        qkvo_change = ordered(out_near, out_far, core, 0).astype(F32)
        query_change, key_change, value_change, out_change = jnp.split(qkvo_change, 4, axis=1)
        qbias_change, _, vbias_change, _ = jnp.split(out_sum.extra[0], 4)
        out_change = out_change.T
    return (
        turned.layer[None],
        frames_delta[None],
        total[0],
        total[1],
        query_change,
        qbias_change,
        key_change,
        value_change,
        vbias_change,
        out_change,
        total[4],
        total[2],
        total[3],
        up_change,
        upbias_change,
        down_change,
        total[5],
    )


def solution(mesh):
    rows = P((DP, *PLANE), None, None)
    cols = P(None, PLANE)
    flat = P(PLANE)
    down = P(PLANE, None)
    every = P()
    placed = (
        rows, P((DP, *PLANE), None), rows, every, every, cols, flat, cols, cols, flat,
        down, every, every, every, cols, flat, down, every,
    )
    outs = (
        rows, rows, every, every, cols, flat, cols, cols, flat, down, every, every, every, cols, flat, down, every,
    )
    return jax.shard_map(shards, mesh=mesh, in_specs=placed, out_specs=outs, check_vma=False)
```

```python
import functools
import math

import jax
import jax.numpy as jnp
from jax import lax
from jax.experimental import pallas as pl
from jax.experimental.pallas import tpu as pltpu
from jax.sharding import PartitionSpec as P

HEAD_DIM = 64
PAIR = 2 * HEAD_DIM
TRIPLE = 3 * PAIR
BLOCK = 128
ROWS = 256
EXTRA = 16
EPSILON = 1e-05
MASKED = -1e30
SPANS = (3, 5, 6, 8)
DP = "dp"
PLANE = ("aa", "ba")

F32 = jnp.float32
BF16 = jnp.bfloat16
NN = (((1,), (0,)), ((), ()))
NT = (((1,), (1,)), ((), ()))
TN = (((0,), (0,)), ((), ()))
SPARE = 8 * 1024 * 1024
LARGE = 61 * 1024 * 1024
VMEM = pl.BlockSpec(memory_space=pltpu.VMEM)
SMEM = pl.BlockSpec(memory_space=pltpu.SMEM)
PACE = 1e6


def dot(left, right, dims=NN):
    return lax.dot_general(left, right, dims, preferred_element_type=F32)


def shape(dims, dtype):
    return jax.ShapeDtypeStruct(tuple(dims), dtype)


class Bag(dict):
    def __getattr__(self, name):
        if name not in self:
            raise AttributeError(name)
        return self[name]


jax.tree_util.register_pytree_node(
    Bag, lambda bag: (tuple(bag.values()), tuple(bag)), lambda names, values: Bag(zip(names, values))
)


def leaves(tree):
    if isinstance(tree, dict):
        tree = list(tree.values())
    if isinstance(tree, (list, tuple)):
        return [leaf for part in tree for leaf in leaves(part)]
    return [tree]


def rebuilt(tree, values):
    if isinstance(tree, dict):
        return Bag({key: rebuilt(part, values) for key, part in tree.items()})
    if isinstance(tree, (list, tuple)):
        return [rebuilt(part, values) for part in tree]
    return next(values)


def staged(body, meta, ins, outs, scratch, microseconds, kept=(), room=None):
    kept = leaves(list(kept))
    given, made = leaves(ins), leaves(outs)

    def kernel(*refs):
        table, refs = refs[0], refs[1 + len(kept) :]
        ours, refs = refs[: len(given)], refs[len(given) :]
        theirs, rest = refs[: len(made)], refs[len(made) :]
        body(table, rebuilt(ins, iter(ours)), rebuilt(outs, iter(theirs)), *rest)

    if room is None:
        room = sum(math.prod(v.shape) * jnp.dtype(v.dtype).itemsize for v in scratch) + SPARE
    got = pl.pallas_call(
        kernel,
        out_shape=made,
        in_specs=[SMEM] + [VMEM] * (len(kept) + len(given)),
        out_specs=[VMEM] * len(made),
        scratch_shapes=list(scratch),
        compiler_params=pltpu.CompilerParams(vmem_limit_bytes=room),
        cost_estimate=pl.CostEstimate(flops=1000, bytes_accessed=int(microseconds * PACE), transcendentals=0),
    )(meta, *kept, *given)
    return rebuilt(outs, iter(got))


def centred(values):
    centre = jnp.mean(values, axis=-1, keepdims=True)
    offset = values - centre
    spread = jnp.mean(offset * offset, axis=-1, keepdims=True)
    scale = lax.rsqrt(spread + EPSILON)
    return offset * scale, scale


def lane_of(dims):
    return lax.broadcasted_iota(jnp.int32, dims, 1)


def my_half(table, half):
    core = table[0, 0]
    mine = pl.ds(pl.multiple_of(core * half, half), half)
    other = pl.ds(pl.multiple_of((1 - core) * half, half), half)
    return mine, other


def scalars(core, labels):
    length = labels.shape[1]
    first_q, last_q = labels[0, ::ROWS], labels[0, ROWS - 1 :: ROWS]
    first_k, last_k = labels[0, ::BLOCK], labels[0, BLOCK - 1 :: BLOCK]
    low = jnp.sum((last_k[None, :] < first_q[:, None]).astype(jnp.int32), axis=1)
    above = jnp.sum((first_k[None, :] > last_q[:, None]).astype(jnp.int32), axis=1)
    count = length // BLOCK - above - low
    return jnp.concatenate([core.astype(jnp.int32)[None], low, count])[None]


def open_kernel(labels, q, k, v, o, qb, vb, *refs):
    rows, (own, other, vectors, table) = refs[:-4], refs[-4:]
    half = own.shape[0] - EXTRA
    length = labels.shape[1]
    place = lax.axis_index(DP)
    core = lax.rem(place, 2)
    for pack, at in ((own, core), (other, 1 - core)):
        part = pl.ds(pl.multiple_of(at * half, half), half)
        for i, w in enumerate((q, k, v)):
            pack[:half, i * PAIR : (i + 1) * PAIR] = w[part, :]
        pack[:half, TRIPLE:] = o[:, part].T
        pack[half:, :] = jnp.zeros((EXTRA, 4 * PAIR), BF16)
        for i, b in ((0, qb), (2, vb)):
            wide = jnp.broadcast_to(b[...].astype(F32).reshape(1, PAIR), (EXTRA, PAIR))
            pack[half:, i * PAIR : (i + 1) * PAIR] = wide.astype(BF16)
    vectors[...] = jnp.zeros_like(vectors)
    for i, r in enumerate(rows):
        vectors[i : i + 1, :] = r[...].astype(F32).reshape(1, r.shape[0])
    table[0, 0] = core
    table[0, 15] = lax.div(place, 2)
    queries, blocks = length // ROWS, length // BLOCK
    for at in range(queries):
        first, last = labels[0, at * ROWS], labels[0, (at + 1) * ROWS - 1]
        low, high = jnp.int32(0), jnp.int32(blocks)
        for b in range(blocks):
            low += (labels[0, (b + 1) * BLOCK - 1] < first).astype(jnp.int32)
            high -= (labels[0, b * BLOCK] > last).astype(jnp.int32)
        table[0, 1 + at] = low
        table[0, 1 + queries + at] = high - low


def opened(labels, q, k, v, o, qb, vb, rows):
    width = q.shape[0]
    pack = shape((width // 2 + EXTRA, 4 * PAIR), BF16)
    return pl.pallas_call(
        open_kernel,
        out_shape=[pack, pack, shape((8, width), F32), shape((1, 16), jnp.int32)],
        in_specs=[SMEM] + [VMEM] * (6 + len(rows)),
        out_specs=[VMEM, VMEM, VMEM, SMEM],
        compiler_params=pltpu.CompilerParams(vmem_limit_bytes=LARGE),
        cost_estimate=pl.CostEstimate(flops=1000, bytes_accessed=int(2 * PACE), transcendentals=0),
    )(labels, q, k, v, o, qb, vb, *rows)


def each_query_block(table, length, body, spans):
    blocks = length // BLOCK
    queries = length // ROWS

    def step(at, carry):
        low = table[0, 1 + at]
        count = table[0, 1 + queries + at]
        under = 0
        for span in [s for s in spans if s < blocks] + [blocks]:
            base = jnp.minimum(low, blocks - span)

            @pl.when((count > under) & (count <= span))
            def _():
                body(at, base, span)

            under = span
        return carry

    lax.fori_loop(0, queries, step, 0)


def clip_marks(labels, at):
    clip = lax.broadcasted_iota(jnp.int32, (BLOCK, ROWS), 0)
    same = clip == labels[:, pl.ds(at, ROWS)]
    hot = jnp.where(same, 1.0, 0.0).T.astype(BF16)
    cold = jnp.where(same, 0.0, MASKED).T.astype(BF16)
    return hot, cold


def split_heads(wide):
    low = lane_of(wide.shape) < HEAD_DIM
    zero = jnp.zeros_like(wide)
    return jnp.where(low, wide, zero), jnp.where(low, zero, wide)


def attend_scratch(groups, length):
    return [
        pltpu.VMEM((groups, 2 * length, 2 * PAIR), BF16),
        pltpu.VMEM((groups, length, 2 * PAIR), BF16),
        pltpu.VMEM((2 * groups, HEAD_DIM + EXTRA, length), BF16),
        pltpu.VMEM((2 * groups, length, ROWS), BF16),
    ]


def attend(table, labels, norm_tile, packs, qkv, mixed, lse, qm, ke, vt, probs):
    length = qkv[0].shape[0]
    half = packs[0][0].shape[0] - EXTRA
    mine, other = my_half(table, half)
    for tile in range(length // ROWS):
        at = tile * ROWS
        rows = pl.ds(at, ROWS)
        normed = norm_tile(rows)
        hot, cold = clip_marks(labels, at)
        for g, (own, far) in enumerate(packs):
            y = dot(normed[rows, mine], own[:half, :TRIPLE])
            y += dot(normed[rows, other], far[:half, :TRIPLE])
            y += own[half:, :TRIPLE][:1].astype(F32)
            q = (y[:, :PAIR] * HEAD_DIM ** (-0.5)).astype(BF16)
            k = y[:, PAIR : 2 * PAIR].astype(BF16)
            v = y[:, 2 * PAIR :].astype(BF16)
            qkv[g][rows, :PAIR] = q
            qkv[g][rows, PAIR : 2 * PAIR] = k
            qkv[g][rows, 2 * PAIR :] = v
            for head, part in enumerate(split_heads(q)):
                to = pl.ds(2 * at + head * ROWS, ROWS)
                qm[g, to, :PAIR] = part
                qm[g, to, PAIR:] = hot
            ke[g, rows, :PAIR] = k
            ke[g, rows, PAIR:] = cold
            turned = v.T
            for head in range(2):
                vt[2 * g + head, :HEAD_DIM, rows] = turned[head * HEAD_DIM : (head + 1) * HEAD_DIM]
                vt[2 * g + head, HEAD_DIM:, rows] = jnp.ones((EXTRA, ROWS), BF16)
    for out in lse:
        out[...] = jnp.zeros_like(out)

    def body(at, base, span):
        keys = pl.ds(pl.multiple_of(base * BLOCK, BLOCK), span * BLOCK)
        rows = pl.ds(pl.multiple_of(at * ROWS, ROWS), ROWS)
        peaks = []
        for g in range(len(packs)):
            for head in range(2):
                queries = pl.ds(pl.multiple_of((2 * at + head) * ROWS, ROWS), ROWS)
                scores = dot(ke[g, keys, :], qm[g, queries, :], NT)
                peaks.append(jnp.max(scores, axis=0, keepdims=True))
                probs[2 * g + head, : span * BLOCK, :] = jnp.exp(scores - peaks[-1]).astype(BF16)
        for g in range(len(packs)):
            heads = []
            for head in range(2):
                out = dot(vt[2 * g + head, :, keys], probs[2 * g + head, : span * BLOCK, :])
                total = out[HEAD_DIM : HEAD_DIM + 1]
                heads.append(out[:HEAD_DIM] * (1.0 / total))
                lse[g][head : head + 1, rows] = peaks[2 * g + head] + jnp.log(total)
            mixed[g][rows, :] = jnp.concatenate(heads, axis=0).T.astype(BF16)

    each_query_block(table, length, body, SPANS)


def attend_outs(groups, length):
    return Bag(
        qkv=[shape((length, TRIPLE), BF16)] * groups,
        mixed=[shape((length, PAIR), BF16)] * groups,
        lse=[shape((8, length), F32)] * groups,
    )


def feed_pack_into(pack, up, down, bias, rows, half):
    hidden = up.shape[1]
    pack[:half, :] = up[rows, :]
    for b in range(0, hidden, half):
        pack[half : 2 * half, b : b + half] = down[b : b + half, rows]
    pack[2 * half :, :] = jnp.broadcast_to(bias, (EXTRA, hidden)).astype(BF16)


def first_body(table, ins, outs, *scratch):
    vectors = ins.vectors

    def norm_tile(rows):
        xhat, _ = centred(ins.frames[rows, :].astype(F32))
        outs.xhat[rows, :] = xhat.astype(BF16)
        outs.normed[rows, :] = (xhat * vectors[0:1, :] + vectors[1:2, :]).astype(BF16)
        return outs.normed

    attend(table, ins.labels, norm_tile, [ins.pack], outs.qkv, outs.mixed, outs.lse, *scratch)
    if len(ins.feed):
        up, down = ins.feed
        half = up.shape[0] // 2
        for pack, rows in zip(outs.feed, my_half(table, half)):
            feed_pack_into(pack, up, down, vectors[6:7, :], rows, half)


def first(meta, labels, frames, vectors, pack, feed):
    length, width = frames.shape
    outs = attend_outs(1, length)
    outs.update(
        normed=shape((length, width), BF16),
        xhat=shape((length, width), BF16),
        feed=[shape((width + EXTRA, up.shape[1]), BF16) for up in feed],
    )
    ins = Bag(labels=labels, vectors=vectors, pack=list(pack), frames=frames, feed=list(feed))
    return staged(first_body, meta, ins, outs, attend_scratch(1, length), 9, room=LARGE)


def second_body(table, ins, outs, *scratch):
    attend(table, ins.labels, lambda rows: ins.normed, ins.packs, outs.qkv, outs.mixed, outs.lse, *scratch)


def second(meta, labels, normed, packs, kept):
    length, width = normed.shape
    groups = len(packs)
    ins = Bag(labels=labels, packs=[list(pair) for pair in packs], normed=normed)
    scratch = attend_scratch(groups, length)
    return staged(second_body, meta, ins, attend_outs(groups, length), scratch, 13, kept)


def join_body(table, ins, outs, normed_s):
    length, width = ins.frames.shape
    half = width // 2
    vectors, inner = ins.vectors, outs.inner
    for tile in range(length // ROWS):
        rows = pl.ds(tile * ROWS, ROWS)
        for which, cols in enumerate(my_half(table, half)):
            total = ins.frames[rows, cols].astype(F32) + vectors[2:3, cols]
            for m, pack in zip(ins.mixed, ins.packs):
                total += dot(m[rows, :], pack[which][:half, TRIPLE:], NT)
            inner[rows, cols] = total
        xhat, _ = centred(inner[rows, :])
        normed_s[rows, :] = (xhat * vectors[3:4, :] + vectors[4:5, :]).astype(BF16)
        for which, cols in enumerate(my_half(table, half)):
            to = slice(which * half, (which + 1) * half)
            outs.normed[rows, to] = normed_s[rows, cols]
            outs.cot[rows, to] = ins.cot[rows, cols]


def join(meta, frames, vectors, mixed, packs, cot, kept):
    ins = Bag(frames=frames, vectors=vectors, mixed=list(mixed), packs=[list(pair) for pair in packs], cot=cot)
    outs = Bag(inner=shape(frames.shape, F32), normed=shape(frames.shape, BF16), cot=shape(frames.shape, BF16))
    return staged(join_body, meta, ins, outs, [pltpu.VMEM(frames.shape, BF16)], 4, kept)


def gelu_both(u):
    falling = jnp.exp(u * u * -0.5)
    t = 1.0 / (1.0 + jnp.abs(u) * (0.3275911 * 0.5**0.5))
    poly = 0.5 * 1.061405429
    for c in (-1.453152027, 1.421413741, -0.284496736, 0.254829592):
        poly = poly * t + 0.5 * c
    tail = poly * t * falling
    phi = jnp.where(u >= 0.0, 1.0 - tail, tail)
    return u * phi, phi + u * falling * (0.5 / jnp.pi) ** 0.5


def feed_body(count, table, ins, outs, up, down, act, delta):
    length, width = ins.normed.shape
    half = width // 2
    hidden = ins.feed[0][0].shape[1]
    bias = []
    for i, pair in enumerate(ins.feed):
        at = i * hidden
        bias.append(pair[0][2 * half :, :][:1].astype(F32))
        for which, pack in enumerate(pair):
            part = slice(which * half, (which + 1) * half)
            up[part, at : at + hidden] = pack[:half, :]
            for b in range(0, hidden, half):
                down[at + b : at + b + half, part] = pack[half : 2 * half, b : b + half]
    bias = jnp.concatenate(bias, axis=1)

    def outward(rows):
        for i, (grad, to) in enumerate(((True, outs.two), (False, outs.out))):
            total = dot(delta[rows, :], up[...], NT) if grad else dot(act[rows, :], down[...])
            for which, cols in enumerate(my_half(table, half)):
                part = total[:, which * half : (which + 1) * half]
                for before in ins.before:
                    part += before[i][rows, cols]
                to[rows, cols] = part

    late = None
    for rows in [pl.ds(at, ROWS) for at in range(0, length, ROWS)]:
        u = dot(ins.normed[rows, :], up[...]) + bias
        back = dot(ins.cot[rows, :], down[...], NT)
        if late is not None:
            outward(late)
        active, slope = gelu_both(u)
        act[rows, :] = active.astype(BF16)
        delta[rows, :] = (back * slope).astype(BF16)
        late = rows
    outward(late)
    for i, packs in enumerate(zip(outs.keep, outs.send)):
        mine = slice(i * hidden, (i + 1) * hidden)
        up_delta = dot(ins.normed[...], delta[:, mine], TN)
        down_delta = dot(act[:, mine], ins.cot[...], TN)
        total = jnp.sum(delta[:, mine].astype(F32), axis=0, keepdims=True)
        for which, pack in enumerate(packs):
            part = slice(which * half, (which + 1) * half)
            pack[:half, :] = up_delta[part, :].astype(BF16)
            for b in range(0, hidden, half):
                pack[half : 2 * half, b : b + half] = down_delta[b : b + half, part].astype(BF16)
            pack[2 * half :, :] = jnp.broadcast_to(total, (EXTRA, hidden)).astype(BF16)


def feed(meta, normed, cot, before, packs, kept):
    length, width = normed.shape
    hidden = packs[0][0].shape[1]
    count = len(packs)
    ins = Bag(feed=[list(pair) for pair in packs], normed=normed, cot=cot, before=before)
    pack = shape(packs[0][0].shape, BF16)
    outs = Bag(
        keep=[pack] * count, send=[pack] * count, two=shape((length, width), F32), out=shape((length, width), F32)
    )
    scratch = [
        pltpu.VMEM((width, count * hidden), BF16),
        pltpu.VMEM((count * hidden, width), BF16),
        pltpu.VMEM((length, count * hidden), BF16),
        pltpu.VMEM((length, count * hidden), BF16),
    ]
    return staged(functools.partial(feed_body, count), meta, ins, outs, scratch, 4 * count, kept)


def turn_body(table, ins, outs):
    length, width = ins.inner.shape
    half = width // 2
    mine, other = my_half(table, half)
    sums, pulls, packs = outs.sums, outs.pulls, ins.packs
    sums[...] = jnp.zeros_like(sums)
    pulls[...] = jnp.zeros_like(pulls)
    dims = (8, PAIR)
    picks = lax.broadcasted_iota(jnp.int32, dims, 0) == lane_of(dims) // HEAD_DIM
    ones = jnp.where(picks, 1.0, 0.0).astype(BF16)
    for tile in range(length // ROWS):
        rows = pl.ds(tile * ROWS, ROWS)
        inner = ins.inner[rows, :]
        outs.layer[rows, :] = (inner + ins.out[rows, :] + ins.vectors[5:6, :]).astype(BF16)
        xhat, scale = centred(inner)
        two = ins.two[rows, :]
        dy = ins.cot[rows, :].astype(F32)
        e = two * ins.vectors[3:4, :]
        lean = jnp.mean(e, axis=-1, keepdims=True)
        pull = jnp.mean(e * xhat, axis=-1, keepdims=True)
        delta = dy + scale * (e - lean - xhat * pull)
        outs.delta[rows, :] = delta
        branch = delta.astype(BF16)
        outs.branch[rows, :] = branch
        for at, part in enumerate((two * xhat, two, branch.astype(F32), dy)):
            sums[2 + at : 3 + at, :] += jnp.sum(part, axis=0, keepdims=True)
        for g, m in enumerate(ins.mixed):
            back = dot(outs.branch[rows, mine], packs[g][0][:half, TRIPLE:])
            back += dot(outs.branch[rows, other], packs[g][1][:half, TRIPLE:])
            back = back.astype(BF16)
            outs.back[g][rows, :] = back
            product = back.astype(F32) * m[rows, :].astype(F32)
            high = product.astype(BF16)
            low = (product - high.astype(F32)).astype(BF16)
            pulls[2 * g : 2 * g + 2, rows] = (dot(ones, high, NT) + dot(ones, low, NT))[:2]


def prepare_body(table, ins, outs):
    length = ins.qkv[0].shape[0]
    for at in range(0, length, ROWS):
        rows = pl.ds(at, ROWS)
        hot, cold = clip_marks(ins.labels, at)
        for qkv, qm, ke, kt in zip(ins.qkv, outs.qm, outs.ke, outs.kt):
            k = qkv[rows, PAIR : 2 * PAIR]
            for head, part in enumerate(split_heads(qkv[rows, :PAIR])):
                to = pl.ds(2 * at + head * ROWS, ROWS)
                qm[to, :PAIR] = part
                qm[to, PAIR:] = hot
            ke[rows, :PAIR] = k
            ke[rows, PAIR:] = cold
            kt[:, rows] = k.T


def prepare(meta, labels, qkv, kept):
    length, groups = qkv[0].shape[0], len(qkv)
    outs = Bag(
        qm=[shape((2 * length, 2 * PAIR), BF16)] * groups,
        ke=[shape((length, 2 * PAIR), BF16)] * groups,
        kt=[shape((PAIR, length), BF16)] * groups,
    )
    return staged(prepare_body, meta, Bag(labels=labels, qkv=list(qkv)), outs, [], 4, kept)


def back_body(at_rows, table, ins, outs, dmm, dk, dv, ds, probs, tilts):
    groups = len(at_rows)
    length = ins.qkv[0].shape[0]
    blocks = length // BLOCK
    qm, ke, kt = ins.qm, ins.ke, ins.kt
    for at in range(0, length, ROWS):
        rows = pl.ds(at, ROWS)
        for g in range(groups):
            for head, d in enumerate(split_heads(ins.back[g][rows, :])):
                dmm[g, pl.ds(2 * at + head * ROWS, ROWS), :] = d
            dk[g, rows, :] = jnp.zeros((ROWS, PAIR), F32)
            dv[g, rows, :] = jnp.zeros((ROWS, PAIR), F32)

    def body(at, base, span):
        rows = pl.ds(pl.multiple_of(at * ROWS, ROWS), ROWS)
        both = pl.ds(pl.multiple_of(at * 2 * ROWS, 2 * ROWS), 2 * ROWS)
        queries = [qm[g][both, :] for g in range(groups)]
        downs = [dmm[g, both, :] for g in range(groups)]
        dqt = [[jnp.zeros((HEAD_DIM, ROWS), F32)] * 2 for _ in range(groups)]
        items = [(g, done, min(2, span - done)) for g in range(groups) for done in range(0, span, 2)]

        def weigh(slot, g, done, size):
            keys = pl.ds(pl.multiple_of((base + done) * BLOCK, BLOCK), size * BLOCK)
            for head in range(2):
                cut = slice(head * ROWS, (head + 1) * ROWS)
                scores = dot(ke[g][keys, :], queries[g][cut], NT)
                slope = dot(ins.qkv[g][keys, 2 * PAIR :], downs[g][cut], NT)
                p = jnp.exp(scores - ins.lse[g][head : head + 1, rows])
                at_row = at_rows[g] + head
                delta = p * (slope - ins.pulls[at_row : at_row + 1, rows])
                probs[slot, : size * BLOCK, cut] = p.astype(BF16)
                tilts[slot, : size * BLOCK, cut] = delta.astype(BF16)

        def gather(slot, g, done, size):
            keys = pl.ds(pl.multiple_of((base + done) * BLOCK, BLOCK), size * BLOCK)
            part = slice(0, size * BLOCK)
            dv[g, keys, :] += dot(probs[slot, part, :], downs[g])
            dk[g, keys, :] += dot(tilts[slot, part, :], queries[g][:, :PAIR])
            for head in range(2):
                cut = slice(head * ROWS, (head + 1) * ROWS)
                wide = kt[g][head * HEAD_DIM : (head + 1) * HEAD_DIM, keys]
                dqt[g][head] += dot(wide, tilts[slot, part, cut])

        for i, item in enumerate(items):
            weigh(i % 2, *item)
            if i:
                gather((i - 1) % 2, *items[i - 1])
        gather((len(items) - 1) % 2, *items[-1])
        for g in range(groups):
            dq = jnp.concatenate(dqt[g], axis=0).T.astype(BF16).astype(F32) * HEAD_DIM ** (-0.5)
            ds[g, rows, :PAIR] = dq.astype(BF16)

    each_query_block(table, length, body, range(2, blocks))
    half = ins.normed.shape[1] // 2
    halves = my_half(table, half)
    for g in range(groups):
        ds[g, :, PAIR : 2 * PAIR] = dk[g].astype(BF16)
        ds[g, :, 2 * PAIR :] = dv[g].astype(BF16)
        every = ds[g]
        for cols, pack in zip(halves[::-1], (outs.send[g], outs.keep[g])):
            pack[:half, :TRIPLE] = dot(ins.normed[:, cols], every, TN).astype(BF16)
            pack[:half, TRIPLE:] = dot(ins.branch[:, cols], ins.mixed[g][...], TN).astype(BF16)
    outs.sums[...] = ins.sums[...]
    for tile in range(length // ROWS):
        rows = pl.ds(tile * ROWS, ROWS)
        for which, cols in enumerate(halves):
            part = dot(ds[0, rows, :], ins.packs[0][which][:half, :TRIPLE], NT)
            for g in range(1, groups):
                part += dot(ds[g, rows, :], ins.packs[g][which][:half, :TRIPLE], NT)
            outs.sums[0:1, cols] += jnp.sum(part * ins.xhat[rows, cols].astype(F32), axis=0, keepdims=True)
            outs.sums[1:2, cols] += jnp.sum(part, axis=0, keepdims=True)
            for before in ins.one:
                part += before[rows, cols]
            outs.one[rows, cols] = part
    for g in range(groups):
        total = jnp.sum(ds[g].astype(F32), axis=0, keepdims=True)
        total = jnp.concatenate([total, jnp.zeros((1, PAIR), F32)], axis=1)
        extra = jnp.broadcast_to(total, (EXTRA, 4 * PAIR)).astype(BF16)
        outs.send[g][half:, :] = extra
        outs.keep[g][half:, :] = extra


def back_scratch(groups, length):
    return [
        pltpu.VMEM((groups, 2 * length, PAIR), BF16),
        pltpu.VMEM((groups, length, PAIR), F32),
        pltpu.VMEM((groups, length, PAIR), F32),
        pltpu.VMEM((groups, length, TRIPLE), BF16),
        pltpu.VMEM((2, 2 * BLOCK, 2 * ROWS), BF16),
        pltpu.VMEM((2, 2 * BLOCK, 2 * ROWS), BF16),
    ]


def back_outs(groups, length, width):
    pack = shape((width // 2 + EXTRA, 4 * PAIR), BF16)
    return Bag(
        send=[pack] * groups, keep=[pack] * groups, one=shape((length, width), F32), sums=shape((8, width), F32)
    )


def back(meta, given, one, sums, part, kept):
    length, width = given.normed.shape
    ins = Bag(
        labels=given.labels,
        qkv=[given.qkv[g] for g in part],
        qm=[given.qm[g] for g in part],
        ke=[given.ke[g] for g in part],
        kt=[given.kt[g] for g in part],
        back=[given.back[g] for g in part],
        lse=[given.lse[g] for g in part],
        pulls=given.pulls,
        normed=given.normed,
        xhat=given.xhat,
        branch=given.branch,
        mixed=[given.mixed[g] for g in part],
        packs=[list(given.packs[g]) for g in part],
        one=[one],
        sums=sums,
    )
    outs = back_outs(len(part), length, width)
    body = functools.partial(back_body, [2 * g for g in part])
    return staged(body, meta, ins, outs, back_scratch(len(part), length), 8 * len(part), kept)


def turn_back_body(part, table, ins, outs, sums, *scratch):
    turned = Bag(outs.turned)
    turned.update(sums=sums)
    turn_body(table, ins.turn, turned)
    given = Bag(ins.back)
    given.update(
        back=[outs.turned.back[g] for g in part], pulls=outs.turned.pulls, branch=outs.turned.branch, one=[], sums=sums
    )
    back_body([2 * g for g in part], table, given, outs.back, *scratch)


def turn_back(meta, given, inner, two, out, cot, vectors, part, kept):
    length, width = inner.shape
    ins = Bag(
        turn=Bag(
            inner=inner,
            two=two,
            out=out,
            cot=cot,
            vectors=vectors,
            mixed=list(given.mixed),
            packs=[list(p) for p in given.packs],
        ),
        back=Bag(
            labels=given.labels,
            qkv=[given.qkv[g] for g in part],
            qm=[given.qm[g] for g in part],
            ke=[given.ke[g] for g in part],
            kt=[given.kt[g] for g in part],
            lse=[given.lse[g] for g in part],
            normed=given.normed,
            xhat=given.xhat,
            mixed=[given.mixed[g] for g in part],
            packs=[list(given.packs[g]) for g in part],
        ),
    )
    groups = len(given.mixed)
    outs = Bag(
        turned=Bag(
            layer=shape((length, width), BF16),
            pulls=shape((max(8, 2 * groups), length), F32),
            delta=shape((length, width), F32),
            branch=shape((length, width), BF16),
            back=[shape((length, PAIR), BF16)] * groups,
        ),
        back=back_outs(len(part), length, width),
    )
    scratch = [pltpu.VMEM((8, width), F32)] + back_scratch(len(part), length)
    return staged(functools.partial(turn_back_body, part), meta, ins, outs, scratch, 14, kept)


def close_body(table, ins, outs):
    length, width = ins.frames.shape
    for tile in range(length // ROWS):
        rows = pl.ds(tile * ROWS, ROWS)
        xhat, scale = centred(ins.frames[rows, :].astype(F32))
        e = ins.one[rows, :] * ins.vectors[0:1, :]
        lean = jnp.mean(e, axis=-1, keepdims=True)
        pull = jnp.mean(e * xhat, axis=-1, keepdims=True)
        outs.frames_delta[rows, :] = (ins.delta[rows, :] + scale * (e - lean - xhat * pull)).astype(BF16)


def close(meta, frames, vectors, delta, one, kept):
    ins = Bag(vectors=vectors, frames=frames, delta=delta, one=one)
    outs = Bag(frames_delta=shape(frames.shape, BF16))
    return staged(close_body, meta, ins, outs, [], 3, kept).frames_delta


def cut_body(table, ins, outs):
    size = outs.blocks[0].shape[0] - EXTRA
    rows = size * len(outs.blocks)
    place = table[0, 15]
    end = sum(p[rows:, :].astype(F32) for p in ins.pieces).astype(BF16)
    for j, block in enumerate(outs.blocks):
        at = pl.ds(pl.multiple_of(jnp.bitwise_xor(place, j) * size, size), size)
        block[:size, :] = sum(p[at, :].astype(F32) for p in ins.pieces).astype(BF16)
        block[size:, :] = end


def cut_blocks(meta, pieces, count, kept):
    rows, cols = pieces[0].shape
    block = shape(((rows - EXTRA) // count + EXTRA, cols), BF16)
    return staged(cut_body, meta, Bag(pieces=list(pieces)), Bag(blocks=[block] * count), [], 2, kept).blocks


def sum_body(table, ins, outs):
    total = sum(p[...].astype(F32) for p in ins.parts)
    size = total.shape[0] - EXTRA
    outs.extra[...] = total[size:]
    outs.block[:size, :] = total[:size].astype(BF16)
    if ins.small:
        small = ins.small[0][...]
        high = small.astype(BF16).astype(F32)
        outs.block[size:, :] = jnp.concatenate([high, small - high], axis=0).astype(BF16)


def sum_blocks(meta, parts, small, kept):
    rows, cols = parts[0].shape
    outs = Bag(block=shape((rows if small else rows - EXTRA, cols), BF16), extra=shape((EXTRA, cols), F32))
    return staged(sum_body, meta, Bag(parts=list(parts), small=list(small)), outs, [], 1, kept)


def ordered_into(table, blocks, pack_s):
    size = pack_s.shape[0] // len(blocks)
    for j, block in enumerate(blocks):
        at = pl.ds(pl.multiple_of(jnp.bitwise_xor(table[0, 15], j) * size, size), size)
        pack_s[at, :] = block[:size, :].astype(F32)


def feed_end_body(count, table, ins, outs, pack_s):
    width, hidden = outs.up.shape
    half = width // 2
    for cols, stack in zip(my_half(table, half), (ins.near, ins.far)):
        size = stack.shape[0] // count
        ordered_into(table, [stack.at[pl.ds(j * size, size)] for j in range(count)], pack_s)
        outs.up[cols, :] = pack_s[:half, :]
        for b in range(0, hidden, half):
            outs.down[b : b + half, cols] = pack_s[half:, b : b + half]
    outs.bias[...] = ins.extra[0:1, :].reshape(hidden)


def feed_end(meta, near, far, extra, count, width, hidden):
    ins = Bag(near=near, far=far, extra=extra)
    outs = Bag(up=shape((width, hidden), F32), down=shape((hidden, width), F32), bias=shape((hidden,), F32))
    return staged(
        functools.partial(feed_end_body, count), meta, ins, outs, [pltpu.VMEM((width, hidden), F32)], 3
    )


def out_end_body(table, ins, outs, pack_s):
    half = pack_s.shape[0]
    for cols, blocks in zip(my_half(table, half), (ins.blocks, ins.far)):
        ordered_into(table, blocks, pack_s)
        for i, to in enumerate((outs.query, outs.key, outs.value)):
            to[cols, :] = pack_s[:, i * PAIR : (i + 1) * PAIR]
        outs.out[:, cols] = pack_s[:, TRIPLE:].T
    row = ins.extra[0:1, :]
    outs.query_bias[...] = row[:, :PAIR].reshape(PAIR)
    outs.value_bias[...] = row[:, 2 * PAIR : TRIPLE].reshape(PAIR)
    size = ins.blocks[0].shape[0] - EXTRA
    small = sum(block[size:, :].astype(F32) for block in ins.blocks)
    small = small[:8] + small[8:]
    for i, to in enumerate(outs.small):
        to[...] = small[i : i + 1, :].reshape(to.shape[0])


def out_end(meta, blocks, far, extra, width):
    ins = Bag(blocks=list(blocks), far=list(far), extra=extra)
    outs = Bag(
        query=shape((width, PAIR), F32),
        key=shape((width, PAIR), F32),
        value=shape((width, PAIR), F32),
        out=shape((PAIR, width), F32),
        query_bias=shape((PAIR,), F32),
        value_bias=shape((PAIR,), F32),
        small=[shape((width,), F32)] * 6,
    )
    return staged(out_end_body, meta, ins, outs, [pltpu.VMEM((width // 2, 4 * PAIR), F32)], 2)


def plane_swap(value, step, size):
    return lax.ppermute(value, PLANE, [(i, i ^ step) for i in range(size)])


def dp_swap(value, step, size):
    return lax.ppermute(value, DP, [(i, i ^ step) for i in range(size)])


def to_blocks(value, half):
    rows = value.shape[0]
    if rows >= half:
        return jnp.concatenate(jnp.split(value, rows // half, axis=0), axis=1)
    return jnp.concatenate(jnp.split(value, half // rows, axis=1), axis=0)


def from_blocks(value, half):
    cols = value.shape[1]
    if cols >= half:
        return jnp.concatenate(jnp.split(value, cols // half, axis=1), axis=0)
    return jnp.concatenate(jnp.split(value, half // cols, axis=0), axis=1)


def extra_row(value):
    return jnp.pad(value[None], ((0, EXTRA - 1), (0, 0)))


def qkvo_pack(half_at, half, query, key, value, out, query_bias, value_bias):
    parts = [lax.dynamic_slice_in_dim(w, half_at, half, axis=0) for w in (query, key, value)]
    parts.append(lax.dynamic_slice_in_dim(out, half_at, half, axis=1).T)
    zero = jnp.zeros_like(query_bias)
    bias = jnp.concatenate([query_bias, zero, value_bias, zero])
    return jnp.concatenate([jnp.concatenate(parts, axis=1), extra_row(bias)], axis=0)


def feed_pack(half_at, half, up, up_bias, down):
    top = lax.dynamic_slice_in_dim(up, half_at, half, axis=0)
    low = to_blocks(lax.dynamic_slice_in_dim(down, half_at, half, axis=1), half)
    return jnp.concatenate([top, low, extra_row(up_bias)], axis=0)


def qkvo_join(shards):
    if len(shards) == 1:
        return shards[0]
    quarters = [jnp.split(s, 4, axis=1) for s in shards]
    return jnp.concatenate([q[i] for i in range(4) for q in quarters], axis=1)


def qkvo_cut(pack, count):
    if count == 1:
        return [pack]
    pieces = jnp.split(pack, 4 * count, axis=1)
    return [jnp.concatenate([pieces[i * count + s] for i in range(4)], axis=1) for s in range(count)]


def feed_join(shards, half):
    if len(shards) == 1:
        return shards[0]
    top = jnp.concatenate([s[:half] for s in shards], axis=1)
    low = jnp.concatenate([from_blocks(s[half : 2 * half], half) for s in shards], axis=0)
    end = jnp.concatenate([s[2 * half :] for s in shards], axis=1)
    return jnp.concatenate([top, to_blocks(low, half), end], axis=0)


def feed_cut(pack, count, half):
    if count == 1:
        return [pack]
    tops = jnp.split(pack[:half], count, axis=1)
    lows = jnp.split(from_blocks(pack[half : 2 * half], half), count, axis=0)
    ends = jnp.split(pack[2 * half :], count, axis=1)
    return [jnp.concatenate([t, to_blocks(l, half), e], axis=0) for t, l, e in zip(tops, lows, ends)]


def ordered(mine, other, core, axis):
    low = jnp.where(core == 0, mine, other)
    high = jnp.where(core == 0, other, mine)
    return jnp.concatenate([low, high], axis=axis)


def after(value, other):
    return lax.optimization_barrier((value, other))


def added(pieces):
    total = pieces[0].astype(F32)
    for piece in pieces[1:]:
        total += piece.astype(F32)
    return total.astype(BF16)


def z_swaps(pack, dp_size):
    return [pack] + [dp_swap(pack, k, dp_size) for k in range(2, dp_size, 2)]


def z_blocks(pack, dp_at, dp_size):
    rows, z_size = pack.shape[0] - EXTRA, dp_size // 2
    size = rows // z_size
    z_at = dp_at // 2

    def block(at):
        return jnp.concatenate([lax.dynamic_slice_in_dim(pack, at * size, size, axis=0), pack[rows:]], axis=0)

    return [block(z_at ^ k) for k in range(z_size)]


def from_z(blocks, dp_at, dp_size):
    stack = jnp.stack(blocks)
    z_at, z_size = dp_at // 2, dp_size // 2
    return jnp.concatenate([stack[z_at ^ j] for j in range(z_size)], axis=0)


def shards(
    frames,
    segment_ids,
    cotangent,
    first_gain,
    first_shift,
    query_weight,
    query_bias,
    key_weight,
    value_weight,
    value_bias,
    out_weight,
    out_bias,
    second_gain,
    second_shift,
    up_weight,
    up_bias,
    down_weight,
    down_bias,
):
    length, width = frames.shape[1:]
    half = width // 2
    planes = lax.axis_size(PLANE)
    dp_size = lax.axis_size(DP)
    dp_at = lax.axis_index(DP)
    core = dp_at % 2
    groups = width // PAIR
    per_group = planes // groups
    alone = per_group == 1
    x, dy, labels = frames[0], cotangent[0], segment_ids
    group_of = [range(g * per_group, (g + 1) * per_group) for g in range(groups)]
    last = groups - 1
    middle = list(range(1, last))
    peers = list(range(1, planes))
    late = [r for g in middle for r in group_of[g]]
    soon = list(group_of[last])
    rest = [r for r in group_of[0] if r]
    rows = (first_gain, first_shift, out_bias, second_gain, second_shift, down_bias)

    def far_half(near):
        return {r: dp_swap(v, 1, dp_size) for r, v in near.items()}

    def out_pair(g):
        return qkvo_join([near[r] for r in group_of[g]]), qkvo_join([far[r] for r in group_of[g]])

    def feed_pair(g):
        return feed_join([feed_near[r] for r in group_of[g]], half), feed_join([feed_far[r] for r in group_of[g]], half)

    if alone:
        own, other, vectors, meta = opened(
            labels,
            query_weight,
            key_weight,
            value_weight,
            out_weight,
            query_bias,
            value_bias,
            (*rows, up_bias),
        )
        near = {r: plane_swap(own, r, planes) for r in peers}
        one = first(meta, labels, x, vectors, (own, other), (up_weight, down_weight))
        near, one = after(near, one)
        far = far_half(near)
        feed_own, feed_other = one.feed
    else:
        meta = scalars(core, labels)
        zero = jnp.zeros((width,), F32)
        vectors = jnp.stack([v.astype(F32) for v in rows] + [zero] * 2)
        own, other = (
            qkvo_pack(c * half, half, query_weight, key_weight, value_weight, out_weight, query_bias, value_bias)
            for c in (core, 1 - core)
        )
        near = {r: plane_swap(own, r, planes) for r in peers}
        far = far_half(near)
        feed_own, feed_other = (feed_pack(c * half, half, up_weight, up_bias, down_weight) for c in (core, 1 - core))
    near[0], far[0] = own, other
    qkvo = [out_pair(g) for g in range(groups)]
    if not alone:
        one = first(meta, labels, x, vectors, qkvo[0], ())
    feed_near, feed_far = {0: feed_own}, {0: feed_other}
    feed_soon = {r: plane_swap(feed_own, r, planes) for r in soon + rest}
    two = second(meta, labels, one.normed, qkvo[1:], ())
    feed_soon, two = after(feed_soon, two)
    feed_near.update(feed_soon)
    feed_far.update(far_half(feed_soon))
    mixed, qkv, lse = one.mixed + two.mixed, one.qkv + two.qkv, one.lse + two.lse
    held = [two.qkv, two.lse, one.normed]
    joined = join(meta, x, vectors, mixed, qkvo, dy, held)
    feed_far, joined = after(feed_far, joined)
    feed_own, feed_soon = after(feed_own, feed_soon)
    feed_near.update({r: plane_swap(feed_own, r, planes) for r in late})

    def chip_sum(keep, far_send):
        return (keep.astype(F32) + far_send.astype(F32)).astype(BF16)

    def across(send):
        return dp_swap(send, 1, dp_size)

    def spread(pack, g, cut):
        return [plane_swap(p, r, planes) if r else p for r, p in zip(group_of[g], cut(pack))]

    def cut_feed(pack):
        return feed_cut(pack, per_group, half)

    def cut_qkvo(pack):
        return qkvo_cut(pack, per_group)

    held += [joined.inner, two.mixed, qkvo]
    three = feed(meta, joined.normed, joined.cot, (), [feed_pair(last), feed_pair(0)], held)
    feed_late, three = after({r: feed_near[r] for r in late}, three)
    feed_near.update(feed_late)
    feed_far.update(far_half(feed_late))
    far_send = across(three.send[0])
    middle_packs, far_send = after([feed_pair(g) for g in middle], far_send)
    feed_here = spread(chip_sum(three.keep[0], far_send), last, cut_feed)
    four = feed(meta, joined.normed, joined.cot, [[three.two, three.out]], middle_packs, held)
    labels, four = after(labels, four)
    ready = prepare(meta, labels, qkv, held)
    (four, feed_here), ready = after((four, feed_here), ready)
    three_send, four.send[0] = after(three.send[1], four.send[0])
    far_sends = [across(s) for s in four.send]
    two_sum, far_sends = after(four.two, far_sends)
    for i, g in enumerate(middle):
        feed_here += spread(chip_sum(four.keep[i], far_sends[i]), g, cut_feed)

    def along_z(parts):
        return [dp_swap(p, 2 * k, dp_size) if k else p for k, p in enumerate(parts)]

    def z_cut(pieces, kept):
        if alone:
            return cut_blocks(meta, pieces, dp_size // 2, kept)
        return z_blocks(added(pieces), dp_at, dp_size)

    given = Bag(labels=labels, normed=one.normed, xhat=one.xhat, qkv=qkv, lse=lse, mixed=mixed, packs=qkvo)
    far_send = across(three_send)
    given.update(ready)
    got = turn_back(meta, given, joined.inner, two_sum, four.out, dy, vectors, [last], held)
    turned = got.turned
    given.update(pulls=turned.pulls, branch=turned.branch, back=turned.back)
    held = [two.qkv, two.lse, one.normed, mixed, qkvo, turned.back, turned.branch, ready]
    got = got.back
    (feed_here, far_send), got = after((feed_here, far_send), got)
    if alone:
        feed_here += [three.keep[1], far_send]
    else:
        feed_here += spread(chip_sum(three.keep[1], far_send), 0, cut_feed)
    far_send = across(got.send[0])
    fed_parts = z_cut(feed_here, held + [got.one])
    labels, (fed_parts, far_send) = after(labels, (fed_parts, far_send))
    given.update(labels=labels)
    fed_parts = along_z(fed_parts)
    out_here = spread(chip_sum(got.keep[0], far_send), last, cut_qkvo)

    got = back(meta, given, got.one, got.sums, middle, held)
    (out_here, fed_parts), got = after((out_here, fed_parts), got)
    far_sends = [across(s) for s in got.send]
    fed_sum = sum_blocks(meta, fed_parts, (), held + [got.one])
    labels, (fed_sum, far_sends) = after(labels, (fed_sum, far_sends))
    given.update(labels=labels)
    fed_blocks = z_swaps(fed_sum.block, dp_size)
    for i, g in enumerate(middle):
        out_here += spread(chip_sum(got.keep[i], far_sends[i]), g, cut_qkvo)

    got = back(meta, given, got.one, got.sums, [0], held)
    (out_here, fed_blocks), got = after((out_here, fed_blocks), got)
    far_send, far_sums = after(across(got.send[0]), across(got.sums))
    if alone:
        out_parts = z_cut(out_here + [got.keep[0], far_send], [])
    else:
        out_here += spread(chip_sum(got.keep[0], far_send), 0, cut_qkvo)
        out_parts = z_cut(out_here, [])
    (vectors, fed_blocks), out_parts = after((vectors, fed_blocks), out_parts)
    out_parts = along_z(out_parts)
    frames_delta = close(meta, x, vectors, turned.delta, got.one, [])
    fed_near = jnp.concatenate(fed_blocks, axis=0)
    fed_far = across(fed_near)
    small, steps = got.sums + far_sums, [1 << i for i in range(planes.bit_length() - 1)]
    small += plane_swap(small, steps[0], planes)
    small, frames_delta = after(small, frames_delta)
    if alone:
        small, fed_far = after(small, fed_far)
        fed_far = feed_end(meta, fed_near, fed_far, fed_sum.extra, dp_size // 2, width, up_weight.shape[1])
    for step in steps[1:]:
        small += plane_swap(small, step, planes)
    out_parts, (fed_far, small) = after(out_parts, (fed_far, small))
    out_sum = sum_blocks(meta, out_parts, (small,) if alone else (), [])
    out_blocks = z_swaps(out_sum.block, dp_size)
    total = small
    for step in () if alone else range(1, dp_size.bit_length() - 1):
        total += dp_swap(total, 1 << step, dp_size)
    out_far = [across(b) for b in out_blocks]
    if alone:
        up_change, down_change, upbias_change = fed_far.up, fed_far.down, fed_far.bias
        ended = out_end(meta, out_blocks, out_far, out_sum.extra, width)
        query_change, key_change, value_change, out_change = ended.query, ended.key, ended.value, ended.out
        qbias_change, vbias_change, total = ended.query_bias, ended.value_bias, ended.small
    else:
        fed_near, fed_far = (from_z(jnp.split(f, dp_size // 2), dp_at, dp_size) for f in (fed_near, fed_far))
        up_change = ordered(fed_near[:half], fed_far[:half], core, 0).astype(F32)
        down_change = ordered(from_blocks(fed_near[half:], half), from_blocks(fed_far[half:], half), core, 1)
        down_change = down_change.astype(F32)
        upbias_change = fed_sum.extra[0]
        out_near, out_far = from_z(out_blocks, dp_at, dp_size), from_z(out_far, dp_at, dp_size)
        qkvo_change = ordered(out_near, out_far, core, 0).astype(F32)
        query_change, key_change, value_change, out_change = jnp.split(qkvo_change, 4, axis=1)
        qbias_change, _, vbias_change, _ = jnp.split(out_sum.extra[0], 4)
        out_change = out_change.T
    return (
        turned.layer[None],
        frames_delta[None],
        total[0],
        total[1],
        query_change,
        qbias_change,
        key_change,
        value_change,
        vbias_change,
        out_change,
        total[4],
        total[2],
        total[3],
        up_change,
        upbias_change,
        down_change,
        total[5],
    )


def solution(mesh):
    rows = P((DP, *PLANE), None, None)
    cols = P(None, PLANE)
    flat = P(PLANE)
    down = P(PLANE, None)
    every = P()
    placed = (
        rows, P((DP, *PLANE), None), rows, every, every, cols, flat, cols, cols, flat,
        down, every, every, every, cols, flat, down, every,
    )
    outs = (
        rows, rows, every, every, cols, flat, cols, cols, flat, down, every, every, every, cols, flat, down, every,
    )
    return jax.shard_map(shards, mesh=mesh, in_specs=placed, out_specs=outs, check_vma=False)
```

```python
import functools
import math

import jax
import jax.numpy as jnp
from jax import lax
from jax.experimental import pallas as pl
from jax.experimental.pallas import tpu as pltpu
from jax.sharding import PartitionSpec as P

HEAD_DIM = 64
PAIR = 2 * HEAD_DIM
TRIPLE = 3 * PAIR
BLOCK = 128
ROWS = 256
EXTRA = 16
EPSILON = 1e-05
MASKED = -1e30
SPANS = (3, 5, 6, 8)
DP = "dp"
PLANE = ("aa", "ba")

F32 = jnp.float32
BF16 = jnp.bfloat16
NN = (((1,), (0,)), ((), ()))
NT = (((1,), (1,)), ((), ()))
TN = (((0,), (0,)), ((), ()))
SPARE = 8 * 1024 * 1024
LARGE = 61 * 1024 * 1024
VMEM = pl.BlockSpec(memory_space=pltpu.VMEM)
SMEM = pl.BlockSpec(memory_space=pltpu.SMEM)
PACE = 1e6


def dot(left, right, dims=NN):
    return lax.dot_general(left, right, dims, preferred_element_type=F32)


def shape(dims, dtype):
    return jax.ShapeDtypeStruct(tuple(dims), dtype)


class Bag(dict):
    def __getattr__(self, name):
        if name not in self:
            raise AttributeError(name)
        return self[name]


jax.tree_util.register_pytree_node(
    Bag, lambda bag: (tuple(bag.values()), tuple(bag)), lambda names, values: Bag(zip(names, values))
)


def leaves(tree):
    if isinstance(tree, dict):
        tree = list(tree.values())
    if isinstance(tree, (list, tuple)):
        return [leaf for part in tree for leaf in leaves(part)]
    return [tree]


def rebuilt(tree, values):
    if isinstance(tree, dict):
        return Bag({key: rebuilt(part, values) for key, part in tree.items()})
    if isinstance(tree, (list, tuple)):
        return [rebuilt(part, values) for part in tree]
    return next(values)


def staged(body, meta, ins, outs, scratch, microseconds, kept=(), room=None):
    kept = leaves(list(kept))
    given, made = leaves(ins), leaves(outs)

    def kernel(*refs):
        table, refs = refs[0], refs[1 + len(kept) :]
        ours, refs = refs[: len(given)], refs[len(given) :]
        theirs, rest = refs[: len(made)], refs[len(made) :]
        body(table, rebuilt(ins, iter(ours)), rebuilt(outs, iter(theirs)), *rest)

    if room is None:
        room = sum(math.prod(v.shape) * jnp.dtype(v.dtype).itemsize for v in scratch) + SPARE
    got = pl.pallas_call(
        kernel,
        out_shape=made,
        in_specs=[SMEM] + [VMEM] * (len(kept) + len(given)),
        out_specs=[VMEM] * len(made),
        scratch_shapes=list(scratch),
        compiler_params=pltpu.CompilerParams(vmem_limit_bytes=room),
        cost_estimate=pl.CostEstimate(flops=1000, bytes_accessed=int(microseconds * PACE), transcendentals=0),
    )(meta, *kept, *given)
    return rebuilt(outs, iter(got))


def centred(values):
    centre = jnp.mean(values, axis=-1, keepdims=True)
    offset = values - centre
    spread = jnp.mean(offset * offset, axis=-1, keepdims=True)
    scale = lax.rsqrt(spread + EPSILON)
    return offset * scale, scale


def lane_of(dims):
    return lax.broadcasted_iota(jnp.int32, dims, 1)


def my_half(table, half):
    core = table[0, 0]
    mine = pl.ds(pl.multiple_of(core * half, half), half)
    other = pl.ds(pl.multiple_of((1 - core) * half, half), half)
    return mine, other


def scalars(core, labels):
    length = labels.shape[1]
    first_q, last_q = labels[0, ::ROWS], labels[0, ROWS - 1 :: ROWS]
    first_k, last_k = labels[0, ::BLOCK], labels[0, BLOCK - 1 :: BLOCK]
    low = jnp.sum((last_k[None, :] < first_q[:, None]).astype(jnp.int32), axis=1)
    above = jnp.sum((first_k[None, :] > last_q[:, None]).astype(jnp.int32), axis=1)
    count = length // BLOCK - above - low
    return jnp.concatenate([core.astype(jnp.int32)[None], low, count])[None]


def open_kernel(labels, q, k, v, o, qb, vb, *refs):
    rows, (own, other, vectors, table) = refs[:-4], refs[-4:]
    half = own.shape[0] - EXTRA
    length = labels.shape[1]
    place = lax.axis_index(DP)
    core = lax.rem(place, 2)
    for pack, at in ((own, core), (other, 1 - core)):
        part = pl.ds(pl.multiple_of(at * half, half), half)
        for i, w in enumerate((q, k, v)):
            pack[:half, i * PAIR : (i + 1) * PAIR] = w[part, :]
        pack[:half, TRIPLE:] = o[:, part].T
        pack[half:, :] = jnp.zeros((EXTRA, 4 * PAIR), BF16)
        for i, b in ((0, qb), (2, vb)):
            wide = jnp.broadcast_to(b[...].astype(F32).reshape(1, PAIR), (EXTRA, PAIR))
            pack[half:, i * PAIR : (i + 1) * PAIR] = wide.astype(BF16)
    vectors[...] = jnp.zeros_like(vectors)
    for i, r in enumerate(rows):
        vectors[i : i + 1, :] = r[...].astype(F32).reshape(1, r.shape[0])
    table[0, 0] = core
    table[0, 15] = lax.div(place, 2)
    queries, blocks = length // ROWS, length // BLOCK
    for at in range(queries):
        first, last = labels[0, at * ROWS], labels[0, (at + 1) * ROWS - 1]
        low, high = jnp.int32(0), jnp.int32(blocks)
        for b in range(blocks):
            low += (labels[0, (b + 1) * BLOCK - 1] < first).astype(jnp.int32)
            high -= (labels[0, b * BLOCK] > last).astype(jnp.int32)
        table[0, 1 + at] = low
        table[0, 1 + queries + at] = high - low


def opened(labels, q, k, v, o, qb, vb, rows):
    width = q.shape[0]
    pack = shape((width // 2 + EXTRA, 4 * PAIR), BF16)
    return pl.pallas_call(
        open_kernel,
        out_shape=[pack, pack, shape((8, width), F32), shape((1, 16), jnp.int32)],
        in_specs=[SMEM] + [VMEM] * (6 + len(rows)),
        out_specs=[VMEM, VMEM, VMEM, SMEM],
        compiler_params=pltpu.CompilerParams(vmem_limit_bytes=LARGE),
        cost_estimate=pl.CostEstimate(flops=1000, bytes_accessed=int(2 * PACE), transcendentals=0),
    )(labels, q, k, v, o, qb, vb, *rows)


def each_query_block(table, length, body, spans):
    blocks = length // BLOCK
    queries = length // ROWS

    def step(at, carry):
        low = table[0, 1 + at]
        count = table[0, 1 + queries + at]
        under = 0
        for span in [s for s in spans if s < blocks] + [blocks]:
            base = jnp.minimum(low, blocks - span)

            @pl.when((count > under) & (count <= span))
            def _():
                body(at, base, span)

            under = span
        return carry

    lax.fori_loop(0, queries, step, 0)


def clip_marks(labels, at):
    clip = lax.broadcasted_iota(jnp.int32, (BLOCK, ROWS), 0)
    same = clip == labels[:, pl.ds(at, ROWS)]
    hot = jnp.where(same, 1.0, 0.0).T.astype(BF16)
    cold = jnp.where(same, 0.0, MASKED).T.astype(BF16)
    return hot, cold


def split_heads(wide):
    low = lane_of(wide.shape) < HEAD_DIM
    zero = jnp.zeros_like(wide)
    return jnp.where(low, wide, zero), jnp.where(low, zero, wide)


def attend_scratch(groups, length):
    return [
        pltpu.VMEM((groups, 2 * length, 2 * PAIR), BF16),
        pltpu.VMEM((groups, length, 2 * PAIR), BF16),
        pltpu.VMEM((2 * groups, HEAD_DIM + EXTRA, length), BF16),
        pltpu.VMEM((2 * groups, length, ROWS), BF16),
    ]


def attend(table, labels, norm_tile, packs, outs, qm, ke, vt, probs):
    qkv, mixed, rest, lse = outs.qkv, outs.mixed, outs.rest, outs.lse
    length = qkv[0].shape[0]
    half = packs[0][0].shape[0] - EXTRA
    mine, other = my_half(table, half)
    for tile in range(length // ROWS):
        at = tile * ROWS
        rows = pl.ds(at, ROWS)
        normed = norm_tile(rows)
        hot, cold = clip_marks(labels, at)
        for g, (own, far) in enumerate(packs):
            y = dot(normed[rows, mine], own[:half, :TRIPLE])
            y += dot(normed[rows, other], far[:half, :TRIPLE])
            y += own[half:, :TRIPLE][:1].astype(F32)
            q = (y[:, :PAIR] * HEAD_DIM ** (-0.5)).astype(BF16)
            k = y[:, PAIR : 2 * PAIR].astype(BF16)
            v = y[:, 2 * PAIR :].astype(BF16)
            qkv[g][rows, :PAIR] = q
            qkv[g][rows, PAIR : 2 * PAIR] = k
            qkv[g][rows, 2 * PAIR :] = v
            for head, part in enumerate(split_heads(q)):
                to = pl.ds(2 * at + head * ROWS, ROWS)
                qm[g, to, :PAIR] = part
                qm[g, to, PAIR:] = hot
            ke[g, rows, :PAIR] = k
            ke[g, rows, PAIR:] = cold
            turned = v.T
            for head in range(2):
                vt[2 * g + head, :HEAD_DIM, rows] = turned[head * HEAD_DIM : (head + 1) * HEAD_DIM]
                vt[2 * g + head, HEAD_DIM:, rows] = jnp.ones((EXTRA, ROWS), BF16)
    for out in lse:
        out[...] = jnp.zeros_like(out)

    def body(at, base, span):
        keys = pl.ds(pl.multiple_of(base * BLOCK, BLOCK), span * BLOCK)
        rows = pl.ds(pl.multiple_of(at * ROWS, ROWS), ROWS)
        peaks = []
        for g in range(len(packs)):
            for head in range(2):
                queries = pl.ds(pl.multiple_of((2 * at + head) * ROWS, ROWS), ROWS)
                scores = dot(ke[g, keys, :], qm[g, queries, :], NT)
                peaks.append(jnp.max(scores, axis=0, keepdims=True))
                probs[2 * g + head, : span * BLOCK, :] = jnp.exp(scores - peaks[-1]).astype(BF16)
        for g in range(len(packs)):
            heads = []
            for head in range(2):
                out = dot(vt[2 * g + head, :, keys], probs[2 * g + head, : span * BLOCK, :])
                total = out[HEAD_DIM : HEAD_DIM + 1]
                heads.append(out[:HEAD_DIM] * (1.0 / total))
                lse[g][head : head + 1, rows] = peaks[2 * g + head] + jnp.log(total)
            out = jnp.concatenate(heads, axis=0).T
            high = out.astype(BF16)
            mixed[g][rows, :] = high
            rest[g][rows, :] = (out - high.astype(F32)).astype(BF16)

    each_query_block(table, length, body, SPANS)


def attend_outs(groups, length):
    return Bag(
        qkv=[shape((length, TRIPLE), BF16)] * groups,
        mixed=[shape((length, PAIR), BF16)] * groups,
        rest=[shape((length, PAIR), BF16)] * groups,
        lse=[shape((8, length), F32)] * groups,
    )


def feed_pack_into(pack, up, down, bias, rows, half):
    hidden = up.shape[1]
    pack[:half, :] = up[rows, :]
    for b in range(0, hidden, half):
        pack[half : 2 * half, b : b + half] = down[b : b + half, rows]
    pack[2 * half :, :] = jnp.broadcast_to(bias, (EXTRA, hidden)).astype(BF16)


def first_body(table, ins, outs, *scratch):
    vectors = ins.vectors

    def norm_tile(rows):
        xhat, _ = centred(ins.frames[rows, :].astype(F32))
        outs.xhat[rows, :] = xhat.astype(BF16)
        outs.normed[rows, :] = (xhat * vectors[0:1, :] + vectors[1:2, :]).astype(BF16)
        return outs.normed

    attend(table, ins.labels, norm_tile, [ins.pack], outs, *scratch)
    if len(ins.feed):
        up, down = ins.feed
        half = up.shape[0] // 2
        for pack, rows in zip(outs.feed, my_half(table, half)):
            feed_pack_into(pack, up, down, vectors[6:7, :], rows, half)


def first(meta, labels, frames, vectors, pack, feed):
    length, width = frames.shape
    outs = attend_outs(1, length)
    outs.update(
        normed=shape((length, width), BF16),
        xhat=shape((length, width), BF16),
        feed=[shape((width + EXTRA, up.shape[1]), BF16) for up in feed],
    )
    ins = Bag(labels=labels, vectors=vectors, pack=list(pack), frames=frames, feed=list(feed))
    return staged(first_body, meta, ins, outs, attend_scratch(1, length), 9, room=LARGE)


def second_body(table, ins, outs, *scratch):
    attend(table, ins.labels, lambda rows: ins.normed, ins.packs, outs, *scratch)


def second(meta, labels, normed, packs, kept):
    length, width = normed.shape
    groups = len(packs)
    ins = Bag(labels=labels, packs=[list(pair) for pair in packs], normed=normed)
    scratch = attend_scratch(groups, length)
    return staged(second_body, meta, ins, attend_outs(groups, length), scratch, 13, kept)


def join_body(table, ins, outs, normed_s):
    length, width = ins.frames.shape
    half = width // 2
    vectors, inner = ins.vectors, outs.inner
    for tile in range(length // ROWS):
        rows = pl.ds(tile * ROWS, ROWS)
        for which, cols in enumerate(my_half(table, half)):
            total = ins.frames[rows, cols].astype(F32) + vectors[2:3, cols]
            for m, pack in zip(ins.mixed, ins.packs):
                total += dot(m[rows, :], pack[which][:half, TRIPLE:], NT)
            inner[rows, cols] = total
        xhat, _ = centred(inner[rows, :])
        normed_s[rows, :] = (xhat * vectors[3:4, :] + vectors[4:5, :]).astype(BF16)
        for which, cols in enumerate(my_half(table, half)):
            to = slice(which * half, (which + 1) * half)
            outs.normed[rows, to] = normed_s[rows, cols]
            outs.cot[rows, to] = ins.cot[rows, cols]


def join(meta, frames, vectors, mixed, packs, cot, kept):
    ins = Bag(frames=frames, vectors=vectors, mixed=list(mixed), packs=[list(pair) for pair in packs], cot=cot)
    outs = Bag(inner=shape(frames.shape, F32), normed=shape(frames.shape, BF16), cot=shape(frames.shape, BF16))
    return staged(join_body, meta, ins, outs, [pltpu.VMEM(frames.shape, BF16)], 4, kept)


def gelu_both(u):
    falling = jnp.exp(u * u * -0.5)
    t = 1.0 / (1.0 + jnp.abs(u) * (0.3275911 * 0.5**0.5))
    poly = 0.5 * 1.061405429
    for c in (-1.453152027, 1.421413741, -0.284496736, 0.254829592):
        poly = poly * t + 0.5 * c
    tail = poly * t * falling
    phi = jnp.where(u >= 0.0, 1.0 - tail, tail)
    return u * phi, phi + u * falling * (0.5 / jnp.pi) ** 0.5


def feed_body(count, table, ins, outs, up, down, act, delta):
    length, width = ins.normed.shape
    half = width // 2
    hidden = ins.feed[0][0].shape[1]
    bias = []
    for i, pair in enumerate(ins.feed):
        at = i * hidden
        bias.append(pair[0][2 * half :, :][:1].astype(F32))
        for which, pack in enumerate(pair):
            part = slice(which * half, (which + 1) * half)
            up[part, at : at + hidden] = pack[:half, :]
            for b in range(0, hidden, half):
                down[at + b : at + b + half, part] = pack[half : 2 * half, b : b + half]
    bias = jnp.concatenate(bias, axis=1)

    def outward(rows):
        for i, (grad, to) in enumerate(((True, outs.two), (False, outs.out))):
            total = dot(delta[rows, :], up[...], NT) if grad else dot(act[rows, :], down[...])
            for which, cols in enumerate(my_half(table, half)):
                part = total[:, which * half : (which + 1) * half]
                for before in ins.before:
                    part += before[i][rows, cols]
                to[rows, cols] = part

    late = None
    for rows in [pl.ds(at, ROWS) for at in range(0, length, ROWS)]:
        u = dot(ins.normed[rows, :], up[...]) + bias
        back = dot(ins.cot[rows, :], down[...], NT)
        if late is not None:
            outward(late)
        active, slope = gelu_both(u)
        act[rows, :] = active.astype(BF16)
        delta[rows, :] = (back * slope).astype(BF16)
        late = rows
    outward(late)
    for i, packs in enumerate(zip(outs.keep, outs.send)):
        mine = slice(i * hidden, (i + 1) * hidden)
        up_delta = dot(ins.normed[...], delta[:, mine], TN)
        down_delta = dot(act[:, mine], ins.cot[...], TN)
        total = jnp.sum(delta[:, mine].astype(F32), axis=0, keepdims=True)
        for which, pack in enumerate(packs):
            part = slice(which * half, (which + 1) * half)
            pack[:half, :] = up_delta[part, :].astype(BF16)
            for b in range(0, hidden, half):
                pack[half : 2 * half, b : b + half] = down_delta[b : b + half, part].astype(BF16)
            pack[2 * half :, :] = jnp.broadcast_to(total, (EXTRA, hidden)).astype(BF16)


def feed(meta, normed, cot, before, packs, kept):
    length, width = normed.shape
    hidden = packs[0][0].shape[1]
    count = len(packs)
    ins = Bag(feed=[list(pair) for pair in packs], normed=normed, cot=cot, before=before)
    pack = shape(packs[0][0].shape, BF16)
    outs = Bag(
        keep=[pack] * count, send=[pack] * count, two=shape((length, width), F32), out=shape((length, width), F32)
    )
    scratch = [
        pltpu.VMEM((width, count * hidden), BF16),
        pltpu.VMEM((count * hidden, width), BF16),
        pltpu.VMEM((length, count * hidden), BF16),
        pltpu.VMEM((length, count * hidden), BF16),
    ]
    return staged(functools.partial(feed_body, count), meta, ins, outs, scratch, 4 * count, kept)


def turn_body(table, ins, outs):
    length, width = ins.inner.shape
    half = width // 2
    mine, other = my_half(table, half)
    sums, pulls, packs = outs.sums, outs.pulls, ins.packs
    sums[...] = jnp.zeros_like(sums)
    pulls[...] = jnp.zeros_like(pulls)
    dims = (8, PAIR)
    picks = lax.broadcasted_iota(jnp.int32, dims, 0) == lane_of(dims) // HEAD_DIM
    ones = jnp.where(picks, 1.0, 0.0).astype(BF16)
    for tile in range(length // ROWS):
        rows = pl.ds(tile * ROWS, ROWS)
        inner = ins.inner[rows, :]
        outs.layer[rows, :] = (inner + ins.out[rows, :] + ins.vectors[5:6, :]).astype(BF16)
        xhat, scale = centred(inner)
        two = ins.two[rows, :]
        dy = ins.cot[rows, :].astype(F32)
        e = two * ins.vectors[3:4, :]
        lean = jnp.mean(e, axis=-1, keepdims=True)
        pull = jnp.mean(e * xhat, axis=-1, keepdims=True)
        delta = dy + scale * (e - lean - xhat * pull)
        outs.delta[rows, :] = delta
        branch = delta.astype(BF16)
        outs.branch[rows, :] = branch
        for at, part in enumerate((two * xhat, two, branch.astype(F32), dy)):
            sums[2 + at : 3 + at, :] += jnp.sum(part, axis=0, keepdims=True)
        for g, (m, r) in enumerate(zip(ins.mixed, ins.rest)):
            back = dot(outs.branch[rows, mine], packs[g][0][:half, TRIPLE:])
            back += dot(outs.branch[rows, other], packs[g][1][:half, TRIPLE:])
            back = back.astype(BF16)
            outs.back[g][rows, :] = back
            product = back.astype(F32) * (m[rows, :].astype(F32) + r[rows, :].astype(F32))
            high = product.astype(BF16)
            low = (product - high.astype(F32)).astype(BF16)
            pulls[2 * g : 2 * g + 2, rows] = (dot(ones, high, NT) + dot(ones, low, NT))[:2]


def prepare_body(table, ins, outs):
    length = ins.qkv[0].shape[0]
    for at in range(0, length, ROWS):
        rows = pl.ds(at, ROWS)
        hot, cold = clip_marks(ins.labels, at)
        for qkv, qm, ke, kt in zip(ins.qkv, outs.qm, outs.ke, outs.kt):
            k = qkv[rows, PAIR : 2 * PAIR]
            for head, part in enumerate(split_heads(qkv[rows, :PAIR])):
                to = pl.ds(2 * at + head * ROWS, ROWS)
                qm[to, :PAIR] = part
                qm[to, PAIR:] = hot
            ke[rows, :PAIR] = k
            ke[rows, PAIR:] = cold
            kt[:, rows] = k.T


def prepare(meta, labels, qkv, kept):
    length, groups = qkv[0].shape[0], len(qkv)
    outs = Bag(
        qm=[shape((2 * length, 2 * PAIR), BF16)] * groups,
        ke=[shape((length, 2 * PAIR), BF16)] * groups,
        kt=[shape((PAIR, length), BF16)] * groups,
    )
    return staged(prepare_body, meta, Bag(labels=labels, qkv=list(qkv)), outs, [], 4, kept)


def back_body(at_rows, table, ins, outs, dmm, dk, dv, ds, probs, tilts):
    groups = len(at_rows)
    length = ins.qkv[0].shape[0]
    blocks = length // BLOCK
    qm, ke, kt = ins.qm, ins.ke, ins.kt
    for at in range(0, length, ROWS):
        rows = pl.ds(at, ROWS)
        for g in range(groups):
            for head, d in enumerate(split_heads(ins.back[g][rows, :])):
                dmm[g, pl.ds(2 * at + head * ROWS, ROWS), :] = d
            dk[g, rows, :] = jnp.zeros((ROWS, PAIR), F32)
            dv[g, rows, :] = jnp.zeros((ROWS, PAIR), F32)

    def body(at, base, span):
        rows = pl.ds(pl.multiple_of(at * ROWS, ROWS), ROWS)
        both = pl.ds(pl.multiple_of(at * 2 * ROWS, 2 * ROWS), 2 * ROWS)
        queries = [qm[g][both, :] for g in range(groups)]
        downs = [dmm[g, both, :] for g in range(groups)]
        dqt = [[jnp.zeros((HEAD_DIM, ROWS), F32)] * 2 for _ in range(groups)]
        items = [(g, done, min(2, span - done)) for g in range(groups) for done in range(0, span, 2)]

        def weigh(slot, g, done, size):
            keys = pl.ds(pl.multiple_of((base + done) * BLOCK, BLOCK), size * BLOCK)
            for head in range(2):
                cut = slice(head * ROWS, (head + 1) * ROWS)
                scores = dot(ke[g][keys, :], queries[g][cut], NT)
                slope = dot(ins.qkv[g][keys, 2 * PAIR :], downs[g][cut], NT)
                p = jnp.exp(scores - ins.lse[g][head : head + 1, rows])
                at_row = at_rows[g] + head
                delta = p * (slope - ins.pulls[at_row : at_row + 1, rows])
                probs[slot, : size * BLOCK, cut] = p.astype(BF16)
                tilts[slot, : size * BLOCK, cut] = delta.astype(BF16)

        def gather(slot, g, done, size):
            keys = pl.ds(pl.multiple_of((base + done) * BLOCK, BLOCK), size * BLOCK)
            part = slice(0, size * BLOCK)
            dv[g, keys, :] += dot(probs[slot, part, :], downs[g])
            dk[g, keys, :] += dot(tilts[slot, part, :], queries[g][:, :PAIR])
            for head in range(2):
                cut = slice(head * ROWS, (head + 1) * ROWS)
                wide = kt[g][head * HEAD_DIM : (head + 1) * HEAD_DIM, keys]
                dqt[g][head] += dot(wide, tilts[slot, part, cut])

        for i, item in enumerate(items):
            weigh(i % 2, *item)
            if i:
                gather((i - 1) % 2, *items[i - 1])
        gather((len(items) - 1) % 2, *items[-1])
        for g in range(groups):
            dq = jnp.concatenate(dqt[g], axis=0).T.astype(BF16).astype(F32) * HEAD_DIM ** (-0.5)
            ds[g, rows, :PAIR] = dq.astype(BF16)

    each_query_block(table, length, body, range(2, blocks))
    half = ins.normed.shape[1] // 2
    halves = my_half(table, half)
    for g in range(groups):
        ds[g, :, PAIR : 2 * PAIR] = dk[g].astype(BF16)
        ds[g, :, 2 * PAIR :] = dv[g].astype(BF16)
        every = ds[g]
        for cols, pack in zip(halves[::-1], (outs.send[g], outs.keep[g])):
            pack[:half, :TRIPLE] = dot(ins.normed[:, cols], every, TN).astype(BF16)
            pack[:half, TRIPLE:] = dot(ins.branch[:, cols], ins.mixed[g][...], TN).astype(BF16)
    outs.sums[...] = ins.sums[...]
    for tile in range(length // ROWS):
        rows = pl.ds(tile * ROWS, ROWS)
        for which, cols in enumerate(halves):
            part = dot(ds[0, rows, :], ins.packs[0][which][:half, :TRIPLE], NT)
            for g in range(1, groups):
                part += dot(ds[g, rows, :], ins.packs[g][which][:half, :TRIPLE], NT)
            outs.sums[0:1, cols] += jnp.sum(part * ins.xhat[rows, cols].astype(F32), axis=0, keepdims=True)
            outs.sums[1:2, cols] += jnp.sum(part, axis=0, keepdims=True)
            for before in ins.one:
                part += before[rows, cols]
            outs.one[rows, cols] = part
    for g in range(groups):
        total = jnp.sum(ds[g].astype(F32), axis=0, keepdims=True)
        total = jnp.concatenate([total, jnp.zeros((1, PAIR), F32)], axis=1)
        extra = jnp.broadcast_to(total, (EXTRA, 4 * PAIR)).astype(BF16)
        outs.send[g][half:, :] = extra
        outs.keep[g][half:, :] = extra


def back_scratch(groups, length):
    return [
        pltpu.VMEM((groups, 2 * length, PAIR), BF16),
        pltpu.VMEM((groups, length, PAIR), F32),
        pltpu.VMEM((groups, length, PAIR), F32),
        pltpu.VMEM((groups, length, TRIPLE), BF16),
        pltpu.VMEM((2, 2 * BLOCK, 2 * ROWS), BF16),
        pltpu.VMEM((2, 2 * BLOCK, 2 * ROWS), BF16),
    ]


def back_outs(groups, length, width):
    pack = shape((width // 2 + EXTRA, 4 * PAIR), BF16)
    return Bag(
        send=[pack] * groups, keep=[pack] * groups, one=shape((length, width), F32), sums=shape((8, width), F32)
    )


def back(meta, given, one, sums, part, kept):
    length, width = given.normed.shape
    ins = Bag(
        labels=given.labels,
        qkv=[given.qkv[g] for g in part],
        qm=[given.qm[g] for g in part],
        ke=[given.ke[g] for g in part],
        kt=[given.kt[g] for g in part],
        back=[given.back[g] for g in part],
        lse=[given.lse[g] for g in part],
        pulls=given.pulls,
        normed=given.normed,
        xhat=given.xhat,
        branch=given.branch,
        mixed=[given.mixed[g] for g in part],
        packs=[list(given.packs[g]) for g in part],
        one=[one],
        sums=sums,
    )
    outs = back_outs(len(part), length, width)
    body = functools.partial(back_body, [2 * g for g in part])
    return staged(body, meta, ins, outs, back_scratch(len(part), length), 8 * len(part), kept)


def turn_back_body(part, table, ins, outs, sums, *scratch):
    turned = Bag(outs.turned)
    turned.update(sums=sums)
    turn_body(table, ins.turn, turned)
    given = Bag(ins.back)
    given.update(
        back=[outs.turned.back[g] for g in part], pulls=outs.turned.pulls, branch=outs.turned.branch, one=[], sums=sums
    )
    back_body([2 * g for g in part], table, given, outs.back, *scratch)


def turn_back(meta, given, inner, two, out, cot, vectors, part, kept):
    length, width = inner.shape
    ins = Bag(
        turn=Bag(
            inner=inner,
            two=two,
            out=out,
            cot=cot,
            vectors=vectors,
            mixed=list(given.mixed),
            rest=list(given.rest),
            packs=[list(p) for p in given.packs],
        ),
        back=Bag(
            labels=given.labels,
            qkv=[given.qkv[g] for g in part],
            qm=[given.qm[g] for g in part],
            ke=[given.ke[g] for g in part],
            kt=[given.kt[g] for g in part],
            lse=[given.lse[g] for g in part],
            normed=given.normed,
            xhat=given.xhat,
            mixed=[given.mixed[g] for g in part],
            packs=[list(given.packs[g]) for g in part],
        ),
    )
    groups = len(given.mixed)
    outs = Bag(
        turned=Bag(
            layer=shape((length, width), BF16),
            pulls=shape((max(8, 2 * groups), length), F32),
            delta=shape((length, width), F32),
            branch=shape((length, width), BF16),
            back=[shape((length, PAIR), BF16)] * groups,
        ),
        back=back_outs(len(part), length, width),
    )
    scratch = [pltpu.VMEM((8, width), F32)] + back_scratch(len(part), length)
    return staged(functools.partial(turn_back_body, part), meta, ins, outs, scratch, 14, kept)


def close_body(table, ins, outs):
    length, width = ins.frames.shape
    for tile in range(length // ROWS):
        rows = pl.ds(tile * ROWS, ROWS)
        xhat, scale = centred(ins.frames[rows, :].astype(F32))
        e = ins.one[rows, :] * ins.vectors[0:1, :]
        lean = jnp.mean(e, axis=-1, keepdims=True)
        pull = jnp.mean(e * xhat, axis=-1, keepdims=True)
        outs.frames_delta[rows, :] = (ins.delta[rows, :] + scale * (e - lean - xhat * pull)).astype(BF16)


def close(meta, frames, vectors, delta, one, kept):
    ins = Bag(vectors=vectors, frames=frames, delta=delta, one=one)
    outs = Bag(frames_delta=shape(frames.shape, BF16))
    return staged(close_body, meta, ins, outs, [], 3, kept).frames_delta


def cut_body(table, ins, outs):
    size = outs.blocks[0].shape[0] - EXTRA
    rows = size * len(outs.blocks)
    place = table[0, 15]
    end = sum(p[rows:, :].astype(F32) for p in ins.pieces).astype(BF16)
    for j, block in enumerate(outs.blocks):
        at = pl.ds(pl.multiple_of(jnp.bitwise_xor(place, j) * size, size), size)
        block[:size, :] = sum(p[at, :].astype(F32) for p in ins.pieces).astype(BF16)
        block[size:, :] = end


def cut_blocks(meta, pieces, count, kept):
    rows, cols = pieces[0].shape
    block = shape(((rows - EXTRA) // count + EXTRA, cols), BF16)
    return staged(cut_body, meta, Bag(pieces=list(pieces)), Bag(blocks=[block] * count), [], 2, kept).blocks


def sum_body(table, ins, outs):
    total = sum(p[...].astype(F32) for p in ins.parts)
    size = total.shape[0] - EXTRA
    outs.extra[...] = total[size:]
    outs.block[:size, :] = total[:size].astype(BF16)
    if ins.small:
        small = ins.small[0][...]
        high = small.astype(BF16).astype(F32)
        outs.block[size:, :] = jnp.concatenate([high, small - high], axis=0).astype(BF16)


def sum_blocks(meta, parts, small, kept):
    rows, cols = parts[0].shape
    outs = Bag(block=shape((rows if small else rows - EXTRA, cols), BF16), extra=shape((EXTRA, cols), F32))
    return staged(sum_body, meta, Bag(parts=list(parts), small=list(small)), outs, [], 1, kept)


def ordered_into(table, blocks, pack_s):
    size = pack_s.shape[0] // len(blocks)
    for j, block in enumerate(blocks):
        at = pl.ds(pl.multiple_of(jnp.bitwise_xor(table[0, 15], j) * size, size), size)
        pack_s[at, :] = block[:size, :].astype(F32)


def feed_end_body(count, table, ins, outs, pack_s):
    width, hidden = outs.up.shape
    half = width // 2
    for cols, stack in zip(my_half(table, half), (ins.near, ins.far)):
        size = stack.shape[0] // count
        ordered_into(table, [stack.at[pl.ds(j * size, size)] for j in range(count)], pack_s)
        outs.up[cols, :] = pack_s[:half, :]
        for b in range(0, hidden, half):
            outs.down[b : b + half, cols] = pack_s[half:, b : b + half]
    outs.bias[...] = ins.extra[0:1, :].reshape(hidden)


def feed_end(meta, near, far, extra, count, width, hidden):
    ins = Bag(near=near, far=far, extra=extra)
    outs = Bag(up=shape((width, hidden), F32), down=shape((hidden, width), F32), bias=shape((hidden,), F32))
    return staged(
        functools.partial(feed_end_body, count), meta, ins, outs, [pltpu.VMEM((width, hidden), F32)], 3
    )


def out_end_body(table, ins, outs, pack_s):
    half = pack_s.shape[0]
    for cols, blocks in zip(my_half(table, half), (ins.blocks, ins.far)):
        ordered_into(table, blocks, pack_s)
        for i, to in enumerate((outs.query, outs.key, outs.value)):
            to[cols, :] = pack_s[:, i * PAIR : (i + 1) * PAIR]
        outs.out[:, cols] = pack_s[:, TRIPLE:].T
    row = ins.extra[0:1, :]
    outs.query_bias[...] = row[:, :PAIR].reshape(PAIR)
    outs.value_bias[...] = row[:, 2 * PAIR : TRIPLE].reshape(PAIR)
    size = ins.blocks[0].shape[0] - EXTRA
    small = sum(block[size:, :].astype(F32) for block in ins.blocks)
    small = small[:8] + small[8:]
    for i, to in enumerate(outs.small):
        to[...] = small[i : i + 1, :].reshape(to.shape[0])


def out_end(meta, blocks, far, extra, width):
    ins = Bag(blocks=list(blocks), far=list(far), extra=extra)
    outs = Bag(
        query=shape((width, PAIR), F32),
        key=shape((width, PAIR), F32),
        value=shape((width, PAIR), F32),
        out=shape((PAIR, width), F32),
        query_bias=shape((PAIR,), F32),
        value_bias=shape((PAIR,), F32),
        small=[shape((width,), F32)] * 6,
    )
    return staged(out_end_body, meta, ins, outs, [pltpu.VMEM((width // 2, 4 * PAIR), F32)], 2)


def plane_swap(value, step, size):
    return lax.ppermute(value, PLANE, [(i, i ^ step) for i in range(size)])


def dp_swap(value, step, size):
    return lax.ppermute(value, DP, [(i, i ^ step) for i in range(size)])


def to_blocks(value, half):
    rows = value.shape[0]
    if rows >= half:
        return jnp.concatenate(jnp.split(value, rows // half, axis=0), axis=1)
    return jnp.concatenate(jnp.split(value, half // rows, axis=1), axis=0)


def from_blocks(value, half):
    cols = value.shape[1]
    if cols >= half:
        return jnp.concatenate(jnp.split(value, cols // half, axis=1), axis=0)
    return jnp.concatenate(jnp.split(value, half // cols, axis=0), axis=1)


def extra_row(value):
    return jnp.pad(value[None], ((0, EXTRA - 1), (0, 0)))


def qkvo_pack(half_at, half, query, key, value, out, query_bias, value_bias):
    parts = [lax.dynamic_slice_in_dim(w, half_at, half, axis=0) for w in (query, key, value)]
    parts.append(lax.dynamic_slice_in_dim(out, half_at, half, axis=1).T)
    zero = jnp.zeros_like(query_bias)
    bias = jnp.concatenate([query_bias, zero, value_bias, zero])
    return jnp.concatenate([jnp.concatenate(parts, axis=1), extra_row(bias)], axis=0)


def feed_pack(half_at, half, up, up_bias, down):
    top = lax.dynamic_slice_in_dim(up, half_at, half, axis=0)
    low = to_blocks(lax.dynamic_slice_in_dim(down, half_at, half, axis=1), half)
    return jnp.concatenate([top, low, extra_row(up_bias)], axis=0)


def qkvo_join(shards):
    if len(shards) == 1:
        return shards[0]
    quarters = [jnp.split(s, 4, axis=1) for s in shards]
    return jnp.concatenate([q[i] for i in range(4) for q in quarters], axis=1)


def qkvo_cut(pack, count):
    if count == 1:
        return [pack]
    pieces = jnp.split(pack, 4 * count, axis=1)
    return [jnp.concatenate([pieces[i * count + s] for i in range(4)], axis=1) for s in range(count)]


def feed_join(shards, half):
    if len(shards) == 1:
        return shards[0]
    top = jnp.concatenate([s[:half] for s in shards], axis=1)
    low = jnp.concatenate([from_blocks(s[half : 2 * half], half) for s in shards], axis=0)
    end = jnp.concatenate([s[2 * half :] for s in shards], axis=1)
    return jnp.concatenate([top, to_blocks(low, half), end], axis=0)


def feed_cut(pack, count, half):
    if count == 1:
        return [pack]
    tops = jnp.split(pack[:half], count, axis=1)
    lows = jnp.split(from_blocks(pack[half : 2 * half], half), count, axis=0)
    ends = jnp.split(pack[2 * half :], count, axis=1)
    return [jnp.concatenate([t, to_blocks(l, half), e], axis=0) for t, l, e in zip(tops, lows, ends)]


def ordered(mine, other, core, axis):
    low = jnp.where(core == 0, mine, other)
    high = jnp.where(core == 0, other, mine)
    return jnp.concatenate([low, high], axis=axis)


def after(value, other):
    return lax.optimization_barrier((value, other))


def added(pieces):
    total = pieces[0].astype(F32)
    for piece in pieces[1:]:
        total += piece.astype(F32)
    return total.astype(BF16)


def z_swaps(pack, dp_size):
    return [pack] + [dp_swap(pack, k, dp_size) for k in range(2, dp_size, 2)]


def z_blocks(pack, dp_at, dp_size):
    rows, z_size = pack.shape[0] - EXTRA, dp_size // 2
    size = rows // z_size
    z_at = dp_at // 2

    def block(at):
        return jnp.concatenate([lax.dynamic_slice_in_dim(pack, at * size, size, axis=0), pack[rows:]], axis=0)

    return [block(z_at ^ k) for k in range(z_size)]


def from_z(blocks, dp_at, dp_size):
    stack = jnp.stack(blocks)
    z_at, z_size = dp_at // 2, dp_size // 2
    return jnp.concatenate([stack[z_at ^ j] for j in range(z_size)], axis=0)


def shards(
    frames,
    segment_ids,
    cotangent,
    first_gain,
    first_shift,
    query_weight,
    query_bias,
    key_weight,
    value_weight,
    value_bias,
    out_weight,
    out_bias,
    second_gain,
    second_shift,
    up_weight,
    up_bias,
    down_weight,
    down_bias,
):
    length, width = frames.shape[1:]
    half = width // 2
    planes = lax.axis_size(PLANE)
    dp_size = lax.axis_size(DP)
    dp_at = lax.axis_index(DP)
    core = dp_at % 2
    groups = width // PAIR
    per_group = planes // groups
    alone = per_group == 1
    x, dy, labels = frames[0], cotangent[0], segment_ids
    group_of = [range(g * per_group, (g + 1) * per_group) for g in range(groups)]
    last = groups - 1
    middle = list(range(1, last))
    peers = list(range(1, planes))
    late = [r for g in middle for r in group_of[g]]
    soon = list(group_of[last])
    rest = [r for r in group_of[0] if r]
    rows = (first_gain, first_shift, out_bias, second_gain, second_shift, down_bias)

    def far_half(near):
        return {r: dp_swap(v, 1, dp_size) for r, v in near.items()}

    def out_pair(g):
        return qkvo_join([near[r] for r in group_of[g]]), qkvo_join([far[r] for r in group_of[g]])

    def feed_pair(g):
        return feed_join([feed_near[r] for r in group_of[g]], half), feed_join([feed_far[r] for r in group_of[g]], half)

    if alone:
        own, other, vectors, meta = opened(
            labels,
            query_weight,
            key_weight,
            value_weight,
            out_weight,
            query_bias,
            value_bias,
            (*rows, up_bias),
        )
        near = {r: plane_swap(own, r, planes) for r in peers}
        one = first(meta, labels, x, vectors, (own, other), (up_weight, down_weight))
        near, one = after(near, one)
        far = far_half(near)
        feed_own, feed_other = one.feed
    else:
        meta = scalars(core, labels)
        zero = jnp.zeros((width,), F32)
        vectors = jnp.stack([v.astype(F32) for v in rows] + [zero] * 2)
        own, other = (
            qkvo_pack(c * half, half, query_weight, key_weight, value_weight, out_weight, query_bias, value_bias)
            for c in (core, 1 - core)
        )
        near = {r: plane_swap(own, r, planes) for r in peers}
        far = far_half(near)
        feed_own, feed_other = (feed_pack(c * half, half, up_weight, up_bias, down_weight) for c in (core, 1 - core))
    near[0], far[0] = own, other
    qkvo = [out_pair(g) for g in range(groups)]
    if not alone:
        one = first(meta, labels, x, vectors, qkvo[0], ())
    feed_near, feed_far = {0: feed_own}, {0: feed_other}
    feed_soon = {r: plane_swap(feed_own, r, planes) for r in soon + rest}
    two = second(meta, labels, one.normed, qkvo[1:], ())
    feed_soon, two = after(feed_soon, two)
    feed_near.update(feed_soon)
    feed_far.update(far_half(feed_soon))
    mixed, qkv, lse = one.mixed + two.mixed, one.qkv + two.qkv, one.lse + two.lse
    held = [two.qkv, two.lse, two.rest, one.normed]
    joined = join(meta, x, vectors, mixed, qkvo, dy, held)
    feed_far, joined = after(feed_far, joined)
    feed_own, feed_soon = after(feed_own, feed_soon)
    feed_near.update({r: plane_swap(feed_own, r, planes) for r in late})

    def chip_sum(keep, far_send):
        return (keep.astype(F32) + far_send.astype(F32)).astype(BF16)

    def across(send):
        return dp_swap(send, 1, dp_size)

    def spread(pack, g, cut):
        return [plane_swap(p, r, planes) if r else p for r, p in zip(group_of[g], cut(pack))]

    def cut_feed(pack):
        return feed_cut(pack, per_group, half)

    def cut_qkvo(pack):
        return qkvo_cut(pack, per_group)

    held += [joined.inner, two.mixed, qkvo]
    three = feed(meta, joined.normed, joined.cot, (), [feed_pair(last), feed_pair(0)], held)
    feed_late, three = after({r: feed_near[r] for r in late}, three)
    feed_near.update(feed_late)
    feed_far.update(far_half(feed_late))
    far_send = across(three.send[0])
    middle_packs, far_send = after([feed_pair(g) for g in middle], far_send)
    feed_here = spread(chip_sum(three.keep[0], far_send), last, cut_feed)
    four = feed(meta, joined.normed, joined.cot, [[three.two, three.out]], middle_packs, held)
    labels, four = after(labels, four)
    ready = prepare(meta, labels, qkv, held)
    (four, feed_here), ready = after((four, feed_here), ready)
    three_send, four.send[0] = after(three.send[1], four.send[0])
    far_sends = [across(s) for s in four.send]
    two_sum, far_sends = after(four.two, far_sends)
    for i, g in enumerate(middle):
        feed_here += spread(chip_sum(four.keep[i], far_sends[i]), g, cut_feed)

    def along_z(parts):
        return [dp_swap(p, 2 * k, dp_size) if k else p for k, p in enumerate(parts)]

    def z_cut(pieces, kept):
        if alone:
            return cut_blocks(meta, pieces, dp_size // 2, kept)
        return z_blocks(added(pieces), dp_at, dp_size)

    given = Bag(labels=labels, normed=one.normed, xhat=one.xhat, qkv=qkv, lse=lse, mixed=mixed, packs=qkvo)
    given.update(rest=one.rest + two.rest)
    far_send = across(three_send)
    given.update(ready)
    got = turn_back(meta, given, joined.inner, two_sum, four.out, dy, vectors, [last], held)
    turned = got.turned
    given.update(pulls=turned.pulls, branch=turned.branch, back=turned.back)
    held = [two.qkv, two.lse, one.normed, mixed, qkvo, turned.back, turned.branch, ready]
    got = got.back
    (feed_here, far_send), got = after((feed_here, far_send), got)
    if alone:
        feed_here += [three.keep[1], far_send]
    else:
        feed_here += spread(chip_sum(three.keep[1], far_send), 0, cut_feed)
    far_send = across(got.send[0])
    fed_parts = z_cut(feed_here, held + [got.one])
    labels, (fed_parts, far_send) = after(labels, (fed_parts, far_send))
    given.update(labels=labels)
    fed_parts = along_z(fed_parts)
    out_here = spread(chip_sum(got.keep[0], far_send), last, cut_qkvo)

    got = back(meta, given, got.one, got.sums, middle, held)
    (out_here, fed_parts), got = after((out_here, fed_parts), got)
    far_sends = [across(s) for s in got.send]
    fed_sum = sum_blocks(meta, fed_parts, (), held + [got.one])
    labels, (fed_sum, far_sends) = after(labels, (fed_sum, far_sends))
    given.update(labels=labels)
    fed_blocks = z_swaps(fed_sum.block, dp_size)
    for i, g in enumerate(middle):
        out_here += spread(chip_sum(got.keep[i], far_sends[i]), g, cut_qkvo)

    got = back(meta, given, got.one, got.sums, [0], held)
    (out_here, fed_blocks), got = after((out_here, fed_blocks), got)
    far_send, far_sums = after(across(got.send[0]), across(got.sums))
    if alone:
        out_parts = z_cut(out_here + [got.keep[0], far_send], [])
    else:
        out_here += spread(chip_sum(got.keep[0], far_send), 0, cut_qkvo)
        out_parts = z_cut(out_here, [])
    (vectors, fed_blocks), out_parts = after((vectors, fed_blocks), out_parts)
    out_parts = along_z(out_parts)
    frames_delta = close(meta, x, vectors, turned.delta, got.one, [])
    fed_near = jnp.concatenate(fed_blocks, axis=0)
    fed_far = across(fed_near)
    small, steps = got.sums + far_sums, [1 << i for i in range(planes.bit_length() - 1)]
    small += plane_swap(small, steps[0], planes)
    small, frames_delta = after(small, frames_delta)
    if alone:
        small, fed_far = after(small, fed_far)
        fed_far = feed_end(meta, fed_near, fed_far, fed_sum.extra, dp_size // 2, width, up_weight.shape[1])
    for step in steps[1:]:
        small += plane_swap(small, step, planes)
    out_parts, (fed_far, small) = after(out_parts, (fed_far, small))
    out_sum = sum_blocks(meta, out_parts, (small,) if alone else (), [])
    out_blocks = z_swaps(out_sum.block, dp_size)
    total = small
    for step in () if alone else range(1, dp_size.bit_length() - 1):
        total += dp_swap(total, 1 << step, dp_size)
    out_far = [across(b) for b in out_blocks]
    if alone:
        up_change, down_change, upbias_change = fed_far.up, fed_far.down, fed_far.bias
        ended = out_end(meta, out_blocks, out_far, out_sum.extra, width)
        query_change, key_change, value_change, out_change = ended.query, ended.key, ended.value, ended.out
        qbias_change, vbias_change, total = ended.query_bias, ended.value_bias, ended.small
    else:
        fed_near, fed_far = (from_z(jnp.split(f, dp_size // 2), dp_at, dp_size) for f in (fed_near, fed_far))
        up_change = ordered(fed_near[:half], fed_far[:half], core, 0).astype(F32)
        down_change = ordered(from_blocks(fed_near[half:], half), from_blocks(fed_far[half:], half), core, 1)
        down_change = down_change.astype(F32)
        upbias_change = fed_sum.extra[0]
        out_near, out_far = from_z(out_blocks, dp_at, dp_size), from_z(out_far, dp_at, dp_size)
        qkvo_change = ordered(out_near, out_far, core, 0).astype(F32)
        query_change, key_change, value_change, out_change = jnp.split(qkvo_change, 4, axis=1)
        qbias_change, _, vbias_change, _ = jnp.split(out_sum.extra[0], 4)
        out_change = out_change.T
    return (
        turned.layer[None],
        frames_delta[None],
        total[0],
        total[1],
        query_change,
        qbias_change,
        key_change,
        value_change,
        vbias_change,
        out_change,
        total[4],
        total[2],
        total[3],
        up_change,
        upbias_change,
        down_change,
        total[5],
    )


def solution(mesh):
    rows = P((DP, *PLANE), None, None)
    cols = P(None, PLANE)
    flat = P(PLANE)
    down = P(PLANE, None)
    every = P()
    placed = (
        rows, P((DP, *PLANE), None), rows, every, every, cols, flat, cols, cols, flat,
        down, every, every, every, cols, flat, down, every,
    )
    outs = (
        rows, rows, every, every, cols, flat, cols, cols, flat, down, every, every, every, cols, flat, down, every,
    )
    return jax.shard_map(shards, mesh=mesh, in_specs=placed, out_specs=outs, check_vma=False)
```

```python
import functools
import math

import jax
import jax.numpy as jnp
from jax import lax
from jax.experimental import pallas as pl
from jax.experimental.pallas import tpu as pltpu
from jax.sharding import PartitionSpec as P

HEAD_DIM = 64
PAIR = 2 * HEAD_DIM
TRIPLE = 3 * PAIR
BLOCK = 128
ROWS = 256
EXTRA = 16
EPSILON = 1e-05
MASKED = -1e30
SPANS = (3, 5, 6, 8)
DP = "dp"
PLANE = ("aa", "ba")

F32 = jnp.float32
BF16 = jnp.bfloat16
NN = (((1,), (0,)), ((), ()))
NT = (((1,), (1,)), ((), ()))
TN = (((0,), (0,)), ((), ()))
SPARE = 8 * 1024 * 1024
LARGE = 61 * 1024 * 1024
VMEM = pl.BlockSpec(memory_space=pltpu.VMEM)
SMEM = pl.BlockSpec(memory_space=pltpu.SMEM)
PACE = 1e6


def dot(left, right, dims=NN):
    return lax.dot_general(left, right, dims, preferred_element_type=F32)


def shape(dims, dtype):
    return jax.ShapeDtypeStruct(tuple(dims), dtype)


class Bag(dict):
    def __getattr__(self, name):
        if name not in self:
            raise AttributeError(name)
        return self[name]


jax.tree_util.register_pytree_node(
    Bag, lambda bag: (tuple(bag.values()), tuple(bag)), lambda names, values: Bag(zip(names, values))
)


def leaves(tree):
    if isinstance(tree, dict):
        tree = list(tree.values())
    if isinstance(tree, (list, tuple)):
        return [leaf for part in tree for leaf in leaves(part)]
    return [tree]


def rebuilt(tree, values):
    if isinstance(tree, dict):
        return Bag({key: rebuilt(part, values) for key, part in tree.items()})
    if isinstance(tree, (list, tuple)):
        return [rebuilt(part, values) for part in tree]
    return next(values)


def staged(body, meta, ins, outs, scratch, microseconds, kept=(), room=None):
    kept = leaves(list(kept))
    given, made = leaves(ins), leaves(outs)

    def kernel(*refs):
        table, refs = refs[0], refs[1 + len(kept) :]
        ours, refs = refs[: len(given)], refs[len(given) :]
        theirs, rest = refs[: len(made)], refs[len(made) :]
        body(table, rebuilt(ins, iter(ours)), rebuilt(outs, iter(theirs)), *rest)

    if room is None:
        room = sum(math.prod(v.shape) * jnp.dtype(v.dtype).itemsize for v in scratch) + SPARE
    got = pl.pallas_call(
        kernel,
        out_shape=made,
        in_specs=[SMEM] + [VMEM] * (len(kept) + len(given)),
        out_specs=[VMEM] * len(made),
        scratch_shapes=list(scratch),
        compiler_params=pltpu.CompilerParams(vmem_limit_bytes=room),
        cost_estimate=pl.CostEstimate(flops=1000, bytes_accessed=int(microseconds * PACE), transcendentals=0),
    )(meta, *kept, *given)
    return rebuilt(outs, iter(got))


def centred(values):
    centre = jnp.mean(values, axis=-1, keepdims=True)
    offset = values - centre
    spread = jnp.mean(offset * offset, axis=-1, keepdims=True)
    scale = lax.rsqrt(spread + EPSILON)
    return offset * scale, scale


def lane_of(dims):
    return lax.broadcasted_iota(jnp.int32, dims, 1)


def my_half(table, half):
    core = table[0, 0]
    mine = pl.ds(pl.multiple_of(core * half, half), half)
    other = pl.ds(pl.multiple_of((1 - core) * half, half), half)
    return mine, other


def scalars(core, labels):
    length = labels.shape[1]
    first_q, last_q = labels[0, ::ROWS], labels[0, ROWS - 1 :: ROWS]
    first_k, last_k = labels[0, ::BLOCK], labels[0, BLOCK - 1 :: BLOCK]
    low = jnp.sum((last_k[None, :] < first_q[:, None]).astype(jnp.int32), axis=1)
    above = jnp.sum((first_k[None, :] > last_q[:, None]).astype(jnp.int32), axis=1)
    count = length // BLOCK - above - low
    return jnp.concatenate([core.astype(jnp.int32)[None], low, count])[None]


def open_kernel(labels, q, k, v, o, qb, vb, *refs):
    rows, (own, other, vectors, table) = refs[:-4], refs[-4:]
    half = own.shape[0] - EXTRA
    length = labels.shape[1]
    place = lax.axis_index(DP)
    core = lax.rem(place, 2)
    for pack, at in ((own, core), (other, 1 - core)):
        part = pl.ds(pl.multiple_of(at * half, half), half)
        for i, w in enumerate((q, k, v)):
            pack[:half, i * PAIR : (i + 1) * PAIR] = w[part, :]
        pack[:half, TRIPLE:] = o[:, part].T
        pack[half:, :] = jnp.zeros((EXTRA, 4 * PAIR), BF16)
        for i, b in ((0, qb), (2, vb)):
            wide = jnp.broadcast_to(b[...].astype(F32).reshape(1, PAIR), (EXTRA, PAIR))
            pack[half:, i * PAIR : (i + 1) * PAIR] = wide.astype(BF16)
    vectors[...] = jnp.zeros_like(vectors)
    for i, r in enumerate(rows):
        vectors[i : i + 1, :] = r[...].astype(F32).reshape(1, r.shape[0])
    table[0, 0] = core
    table[0, 15] = lax.div(place, 2)
    queries, blocks = length // ROWS, length // BLOCK
    for at in range(queries):
        first, last = labels[0, at * ROWS], labels[0, (at + 1) * ROWS - 1]
        low, high = jnp.int32(0), jnp.int32(blocks)
        for b in range(blocks):
            low += (labels[0, (b + 1) * BLOCK - 1] < first).astype(jnp.int32)
            high -= (labels[0, b * BLOCK] > last).astype(jnp.int32)
        table[0, 1 + at] = low
        table[0, 1 + queries + at] = high - low


def opened(labels, q, k, v, o, qb, vb, rows):
    width = q.shape[0]
    pack = shape((width // 2 + EXTRA, 4 * PAIR), BF16)
    return pl.pallas_call(
        open_kernel,
        out_shape=[pack, pack, shape((8, width), F32), shape((1, 16), jnp.int32)],
        in_specs=[SMEM] + [VMEM] * (6 + len(rows)),
        out_specs=[VMEM, VMEM, VMEM, SMEM],
        compiler_params=pltpu.CompilerParams(vmem_limit_bytes=LARGE),
        cost_estimate=pl.CostEstimate(flops=1000, bytes_accessed=int(2 * PACE), transcendentals=0),
    )(labels, q, k, v, o, qb, vb, *rows)


def each_query_block(table, length, body, spans):
    blocks = length // BLOCK
    queries = length // ROWS

    def step(at, carry):
        low = table[0, 1 + at]
        count = table[0, 1 + queries + at]
        under = 0
        for span in [s for s in spans if s < blocks] + [blocks]:
            base = jnp.minimum(low, blocks - span)

            @pl.when((count > under) & (count <= span))
            def _():
                body(at, base, span)

            under = span
        return carry

    lax.fori_loop(0, queries, step, 0)


def clip_marks(labels, at):
    clip = lax.broadcasted_iota(jnp.int32, (BLOCK, ROWS), 0)
    same = clip == labels[:, pl.ds(at, ROWS)]
    hot = jnp.where(same, 1.0, 0.0).T.astype(BF16)
    cold = jnp.where(same, 0.0, MASKED).T.astype(BF16)
    return hot, cold


def split_heads(wide):
    low = lane_of(wide.shape) < HEAD_DIM
    zero = jnp.zeros_like(wide)
    return jnp.where(low, wide, zero), jnp.where(low, zero, wide)


def attend_scratch(groups, length):
    return [
        pltpu.VMEM((groups, 2 * length, 2 * PAIR), BF16),
        pltpu.VMEM((groups, length, 2 * PAIR), BF16),
        pltpu.VMEM((2 * groups, HEAD_DIM + EXTRA, length), BF16),
        pltpu.VMEM((2 * groups, length, ROWS), BF16),
    ]


def attend(table, labels, norm_tile, packs, outs, qm, ke, vt, probs):
    qkv, mixed, rest, lse = outs.qkv, outs.mixed, outs.rest, outs.lse
    length = qkv[0].shape[0]
    half = packs[0][0].shape[0] - EXTRA
    mine, other = my_half(table, half)
    for tile in range(length // ROWS):
        at = tile * ROWS
        rows = pl.ds(at, ROWS)
        normed = norm_tile(rows)
        hot, cold = clip_marks(labels, at)
        for g, (own, far) in enumerate(packs):
            y = dot(normed[rows, mine], own[:half, :TRIPLE])
            y += dot(normed[rows, other], far[:half, :TRIPLE])
            y += own[half:, :TRIPLE][:1].astype(F32)
            q = (y[:, :PAIR] * HEAD_DIM ** (-0.5)).astype(BF16)
            k = y[:, PAIR : 2 * PAIR].astype(BF16)
            v = y[:, 2 * PAIR :].astype(BF16)
            qkv[g][rows, :PAIR] = q
            qkv[g][rows, PAIR : 2 * PAIR] = k
            qkv[g][rows, 2 * PAIR :] = v
            for head, part in enumerate(split_heads(q)):
                to = pl.ds(2 * at + head * ROWS, ROWS)
                qm[g, to, :PAIR] = part
                qm[g, to, PAIR:] = hot
            ke[g, rows, :PAIR] = k
            ke[g, rows, PAIR:] = cold
            turned = v.T
            for head in range(2):
                vt[2 * g + head, :HEAD_DIM, rows] = turned[head * HEAD_DIM : (head + 1) * HEAD_DIM]
                vt[2 * g + head, HEAD_DIM:, rows] = jnp.ones((EXTRA, ROWS), BF16)
    for out in lse:
        out[...] = jnp.zeros_like(out)

    def body(at, base, span):
        keys = pl.ds(pl.multiple_of(base * BLOCK, BLOCK), span * BLOCK)
        rows = pl.ds(pl.multiple_of(at * ROWS, ROWS), ROWS)
        peaks = []
        for g in range(len(packs)):
            for head in range(2):
                queries = pl.ds(pl.multiple_of((2 * at + head) * ROWS, ROWS), ROWS)
                scores = dot(ke[g, keys, :], qm[g, queries, :], NT)
                peaks.append(jnp.max(scores, axis=0, keepdims=True))
                probs[2 * g + head, : span * BLOCK, :] = jnp.exp(scores - peaks[-1]).astype(BF16)
        for g in range(len(packs)):
            heads = []
            for head in range(2):
                out = dot(vt[2 * g + head, :, keys], probs[2 * g + head, : span * BLOCK, :])
                total = out[HEAD_DIM : HEAD_DIM + 1]
                heads.append(out[:HEAD_DIM] * (1.0 / total))
                lse[g][head : head + 1, rows] = peaks[2 * g + head] + jnp.log(total)
            out = jnp.concatenate(heads, axis=0).T
            high = out.astype(BF16)
            mixed[g][rows, :] = high
            rest[g][rows, :] = (out - high.astype(F32)).astype(BF16)

    each_query_block(table, length, body, SPANS)


def attend_outs(groups, length):
    return Bag(
        qkv=[shape((length, TRIPLE), BF16)] * groups,
        mixed=[shape((length, PAIR), BF16)] * groups,
        rest=[shape((length, PAIR), BF16)] * groups,
        lse=[shape((8, length), F32)] * groups,
    )


def feed_pack_into(pack, up, down, bias, rows, half):
    hidden = up.shape[1]
    pack[:half, :] = up[rows, :]
    for b in range(0, hidden, half):
        pack[half : 2 * half, b : b + half] = down[b : b + half, rows]
    pack[2 * half :, :] = jnp.broadcast_to(bias, (EXTRA, hidden)).astype(BF16)


def first_body(table, ins, outs, *scratch):
    vectors = ins.vectors

    def norm_tile(rows):
        xhat, _ = centred(ins.frames[rows, :].astype(F32))
        outs.xhat[rows, :] = xhat.astype(BF16)
        outs.normed[rows, :] = (xhat * vectors[0:1, :] + vectors[1:2, :]).astype(BF16)
        return outs.normed

    attend(table, ins.labels, norm_tile, [ins.pack], outs, *scratch)
    if len(ins.feed):
        up, down = ins.feed
        half = up.shape[0] // 2
        for pack, rows in zip(outs.feed, my_half(table, half)):
            feed_pack_into(pack, up, down, vectors[6:7, :], rows, half)


def first(meta, labels, frames, vectors, pack, feed):
    length, width = frames.shape
    outs = attend_outs(1, length)
    outs.update(
        normed=shape((length, width), BF16),
        xhat=shape((length, width), BF16),
        feed=[shape((width + EXTRA, up.shape[1]), BF16) for up in feed],
    )
    ins = Bag(labels=labels, vectors=vectors, pack=list(pack), frames=frames, feed=list(feed))
    return staged(first_body, meta, ins, outs, attend_scratch(1, length), 9, room=LARGE)


def second_body(table, ins, outs, *scratch):
    attend(table, ins.labels, lambda rows: ins.normed, ins.packs, outs, *scratch)


def second(meta, labels, normed, packs, kept):
    length, width = normed.shape
    groups = len(packs)
    ins = Bag(labels=labels, packs=[list(pair) for pair in packs], normed=normed)
    scratch = attend_scratch(groups, length)
    return staged(second_body, meta, ins, attend_outs(groups, length), scratch, 13, kept)


def join_body(table, ins, outs, normed_s):
    length, width = ins.frames.shape
    half = width // 2
    vectors, inner = ins.vectors, outs.inner
    for tile in range(length // ROWS):
        rows = pl.ds(tile * ROWS, ROWS)
        for which, cols in enumerate(my_half(table, half)):
            total = ins.frames[rows, cols].astype(F32) + vectors[2:3, cols]
            for m, pack in zip(ins.mixed, ins.packs):
                total += dot(m[rows, :], pack[which][:half, TRIPLE:], NT)
            inner[rows, cols] = total
        xhat, _ = centred(inner[rows, :])
        normed_s[rows, :] = (xhat * vectors[3:4, :] + vectors[4:5, :]).astype(BF16)
        for which, cols in enumerate(my_half(table, half)):
            to = slice(which * half, (which + 1) * half)
            outs.normed[rows, to] = normed_s[rows, cols]
            outs.cot[rows, to] = ins.cot[rows, cols]


def join(meta, frames, vectors, mixed, packs, cot, kept):
    ins = Bag(frames=frames, vectors=vectors, mixed=list(mixed), packs=[list(pair) for pair in packs], cot=cot)
    outs = Bag(inner=shape(frames.shape, F32), normed=shape(frames.shape, BF16), cot=shape(frames.shape, BF16))
    return staged(join_body, meta, ins, outs, [pltpu.VMEM(frames.shape, BF16)], 4, kept)


def gelu_both(u):
    falling = jnp.exp(u * u * -0.5)
    t = 1.0 / (1.0 + jnp.abs(u) * (0.3275911 * 0.5**0.5))
    poly = 0.5 * 1.061405429
    for c in (-1.453152027, 1.421413741, -0.284496736, 0.254829592):
        poly = poly * t + 0.5 * c
    tail = poly * t * falling
    phi = jnp.where(u >= 0.0, 1.0 - tail, tail)
    return u * phi, phi + u * falling * (0.5 / jnp.pi) ** 0.5


def feed_body(count, table, ins, outs, up, down, act, delta):
    length, width = ins.normed.shape
    half = width // 2
    hidden = ins.feed[0][0].shape[1]
    bias = []
    for i, pair in enumerate(ins.feed):
        at = i * hidden
        bias.append(pair[0][2 * half :, :][:1].astype(F32))
        for which, pack in enumerate(pair):
            part = slice(which * half, (which + 1) * half)
            up[part, at : at + hidden] = pack[:half, :]
            for b in range(0, hidden, half):
                down[at + b : at + b + half, part] = pack[half : 2 * half, b : b + half]
    bias = jnp.concatenate(bias, axis=1)

    def outward(rows):
        for i, (grad, to) in enumerate(((True, outs.two), (False, outs.out))):
            total = dot(delta[rows, :], up[...], NT) if grad else dot(act[rows, :], down[...])
            for which, cols in enumerate(my_half(table, half)):
                part = total[:, which * half : (which + 1) * half]
                for before in ins.before:
                    part += before[i][rows, cols]
                to[rows, cols] = part

    late = None
    for rows in [pl.ds(at, ROWS) for at in range(0, length, ROWS)]:
        u = dot(ins.normed[rows, :], up[...]) + bias
        back = dot(ins.cot[rows, :], down[...], NT)
        if late is not None:
            outward(late)
        active, slope = gelu_both(u)
        act[rows, :] = active.astype(BF16)
        delta[rows, :] = (back * slope).astype(BF16)
        late = rows
    outward(late)
    for i, packs in enumerate(zip(outs.keep, outs.send)):
        mine = slice(i * hidden, (i + 1) * hidden)
        up_delta = dot(ins.normed[...], delta[:, mine], TN)
        down_delta = dot(act[:, mine], ins.cot[...], TN)
        total = jnp.sum(delta[:, mine].astype(F32), axis=0, keepdims=True)
        for which, pack in enumerate(packs):
            part = slice(which * half, (which + 1) * half)
            pack[:half, :] = up_delta[part, :].astype(BF16)
            for b in range(0, hidden, half):
                pack[half : 2 * half, b : b + half] = down_delta[b : b + half, part].astype(BF16)
            pack[2 * half :, :] = jnp.broadcast_to(total, (EXTRA, hidden)).astype(BF16)


def feed(meta, normed, cot, before, packs, kept):
    length, width = normed.shape
    hidden = packs[0][0].shape[1]
    count = len(packs)
    ins = Bag(feed=[list(pair) for pair in packs], normed=normed, cot=cot, before=before)
    pack = shape(packs[0][0].shape, BF16)
    outs = Bag(
        keep=[pack] * count, send=[pack] * count, two=shape((length, width), F32), out=shape((length, width), F32)
    )
    scratch = [
        pltpu.VMEM((width, count * hidden), BF16),
        pltpu.VMEM((count * hidden, width), BF16),
        pltpu.VMEM((length, count * hidden), BF16),
        pltpu.VMEM((length, count * hidden), BF16),
    ]
    return staged(functools.partial(feed_body, count), meta, ins, outs, scratch, 4 * count, kept)


def turn_body(table, ins, outs):
    length, width = ins.inner.shape
    half = width // 2
    mine, other = my_half(table, half)
    sums, pulls, packs = outs.sums, outs.pulls, ins.packs
    sums[...] = jnp.zeros_like(sums)
    pulls[...] = jnp.zeros_like(pulls)
    dims = (8, 2 * PAIR)
    picks = lax.broadcasted_iota(jnp.int32, dims, 0) == lax.rem(lane_of(dims), PAIR) // HEAD_DIM
    ones = jnp.where(picks, 1.0, 0.0).astype(BF16)
    for tile in range(length // ROWS):
        rows = pl.ds(tile * ROWS, ROWS)
        inner = ins.inner[rows, :]
        outs.layer[rows, :] = (inner + ins.out[rows, :] + ins.vectors[5:6, :]).astype(BF16)
        xhat, scale = centred(inner)
        two = ins.two[rows, :]
        dy = ins.cot[rows, :].astype(F32)
        e = two * ins.vectors[3:4, :]
        lean = jnp.mean(e, axis=-1, keepdims=True)
        pull = jnp.mean(e * xhat, axis=-1, keepdims=True)
        delta = dy + scale * (e - lean - xhat * pull)
        outs.delta[rows, :] = delta
        branch = delta.astype(BF16)
        outs.branch[rows, :] = branch
        for at, part in enumerate((two * xhat, two, branch.astype(F32), dy)):
            sums[2 + at : 3 + at, :] += jnp.sum(part, axis=0, keepdims=True)
        for g, (m, r) in enumerate(zip(ins.mixed, ins.rest)):
            back = dot(outs.branch[rows, mine], packs[g][0][:half, TRIPLE:])
            back += dot(outs.branch[rows, other], packs[g][1][:half, TRIPLE:])
            back = back.astype(BF16)
            outs.back[g][rows, :] = back
            product = back.astype(F32) * (m[rows, :].astype(F32) + r[rows, :].astype(F32))
            high = product.astype(BF16)
            low = (product - high.astype(F32)).astype(BF16)
            pulls[2 * g : 2 * g + 2, rows] = dot(ones, jnp.concatenate([high, low], axis=1), NT)[:2]


def prepare_body(table, ins, outs):
    length = ins.qkv[0].shape[0]
    for at in range(0, length, ROWS):
        rows = pl.ds(at, ROWS)
        hot, cold = clip_marks(ins.labels, at)
        for qkv, qm, ke, kt in zip(ins.qkv, outs.qm, outs.ke, outs.kt):
            k = qkv[rows, PAIR : 2 * PAIR]
            for head, part in enumerate(split_heads(qkv[rows, :PAIR])):
                to = pl.ds(2 * at + head * ROWS, ROWS)
                qm[to, :PAIR] = part
                qm[to, PAIR:] = hot
            ke[rows, :PAIR] = k
            ke[rows, PAIR:] = cold
            kt[:, rows] = k.T


def prepare(meta, labels, qkv, kept):
    length, groups = qkv[0].shape[0], len(qkv)
    outs = Bag(
        qm=[shape((2 * length, 2 * PAIR), BF16)] * groups,
        ke=[shape((length, 2 * PAIR), BF16)] * groups,
        kt=[shape((PAIR, length), BF16)] * groups,
    )
    return staged(prepare_body, meta, Bag(labels=labels, qkv=list(qkv)), outs, [], 4, kept)


def back_body(at_rows, table, ins, outs, dmm, dk, dv, ds, probs, tilts):
    groups = len(at_rows)
    length = ins.qkv[0].shape[0]
    blocks = length // BLOCK
    qm, ke, kt = ins.qm, ins.ke, ins.kt
    for at in range(0, length, ROWS):
        rows = pl.ds(at, ROWS)
        for g in range(groups):
            for head, d in enumerate(split_heads(ins.back[g][rows, :])):
                dmm[g, pl.ds(2 * at + head * ROWS, ROWS), :] = d
            dk[g, rows, :] = jnp.zeros((ROWS, PAIR), F32)
            dv[g, rows, :] = jnp.zeros((ROWS, PAIR), F32)

    def body(at, base, span):
        rows = pl.ds(pl.multiple_of(at * ROWS, ROWS), ROWS)
        both = pl.ds(pl.multiple_of(at * 2 * ROWS, 2 * ROWS), 2 * ROWS)
        queries = [qm[g][both, :] for g in range(groups)]
        downs = [dmm[g, both, :] for g in range(groups)]
        dqt = [[jnp.zeros((HEAD_DIM, ROWS), F32)] * 2 for _ in range(groups)]
        cut_at = -(-span // 2) if span > 3 else span
        items = [(g, done, min(cut_at, span - done)) for g in range(groups) for done in range(0, span, cut_at)]

        def weigh(slot, g, done, size):
            keys = pl.ds(pl.multiple_of((base + done) * BLOCK, BLOCK), size * BLOCK)
            for head in range(2):
                cut = slice(head * ROWS, (head + 1) * ROWS)
                scores = dot(ke[g][keys, :], queries[g][cut], NT)
                slope = dot(ins.qkv[g][keys, 2 * PAIR :], downs[g][cut], NT)
                p = jnp.exp(scores - ins.lse[g][head : head + 1, rows])
                at_row = at_rows[g] + head
                delta = p * (slope - ins.pulls[at_row : at_row + 1, rows])
                probs[slot, : size * BLOCK, cut] = p.astype(BF16)
                tilts[slot, : size * BLOCK, cut] = delta.astype(BF16)

        def gather(slot, g, done, size):
            keys = pl.ds(pl.multiple_of((base + done) * BLOCK, BLOCK), size * BLOCK)
            part = slice(0, size * BLOCK)
            dv[g, keys, :] += dot(probs[slot, part, :], downs[g])
            dk[g, keys, :] += dot(tilts[slot, part, :], queries[g][:, :PAIR])
            for head in range(2):
                cut = slice(head * ROWS, (head + 1) * ROWS)
                wide = kt[g][head * HEAD_DIM : (head + 1) * HEAD_DIM, keys]
                dqt[g][head] += dot(wide, tilts[slot, part, cut])

        for i, item in enumerate(items):
            weigh(i % 2, *item)
            if i:
                gather((i - 1) % 2, *items[i - 1])
        gather((len(items) - 1) % 2, *items[-1])
        for g in range(groups):
            dq = jnp.concatenate(dqt[g], axis=0).T.astype(BF16).astype(F32) * HEAD_DIM ** (-0.5)
            ds[g, rows, :PAIR] = dq.astype(BF16)

    each_query_block(table, length, body, range(2, blocks))
    half = ins.normed.shape[1] // 2
    halves = my_half(table, half)
    for g in range(groups):
        ds[g, :, PAIR : 2 * PAIR] = dk[g].astype(BF16)
        ds[g, :, 2 * PAIR :] = dv[g].astype(BF16)
        every = ds[g]
        for cols, pack in zip(halves[::-1], (outs.send[g], outs.keep[g])):
            pack[:half, :TRIPLE] = dot(ins.normed[:, cols], every, TN).astype(BF16)
            pack[:half, TRIPLE:] = dot(ins.branch[:, cols], ins.mixed[g][...], TN).astype(BF16)
    outs.sums[...] = ins.sums[...]
    for tile in range(length // ROWS):
        rows = pl.ds(tile * ROWS, ROWS)
        for which, cols in enumerate(halves):
            part = dot(ds[0, rows, :], ins.packs[0][which][:half, :TRIPLE], NT)
            for g in range(1, groups):
                part += dot(ds[g, rows, :], ins.packs[g][which][:half, :TRIPLE], NT)
            outs.sums[0:1, cols] += jnp.sum(part * ins.xhat[rows, cols].astype(F32), axis=0, keepdims=True)
            outs.sums[1:2, cols] += jnp.sum(part, axis=0, keepdims=True)
            for before in ins.one:
                part += before[rows, cols]
            outs.one[rows, cols] = part
    for g in range(groups):
        total = jnp.sum(ds[g].astype(F32), axis=0, keepdims=True)
        total = jnp.concatenate([total, jnp.zeros((1, PAIR), F32)], axis=1)
        extra = jnp.broadcast_to(total, (EXTRA, 4 * PAIR)).astype(BF16)
        outs.send[g][half:, :] = extra
        outs.keep[g][half:, :] = extra


def back_scratch(groups, length):
    return [
        pltpu.VMEM((groups, 2 * length, PAIR), BF16),
        pltpu.VMEM((groups, length, PAIR), F32),
        pltpu.VMEM((groups, length, PAIR), F32),
        pltpu.VMEM((groups, length, TRIPLE), BF16),
        pltpu.VMEM((2, length // 2, 2 * ROWS), BF16),
        pltpu.VMEM((2, length // 2, 2 * ROWS), BF16),
    ]


def back_outs(groups, length, width):
    pack = shape((width // 2 + EXTRA, 4 * PAIR), BF16)
    return Bag(
        send=[pack] * groups, keep=[pack] * groups, one=shape((length, width), F32), sums=shape((8, width), F32)
    )


def back(meta, given, one, sums, part, kept):
    length, width = given.normed.shape
    ins = Bag(
        labels=given.labels,
        qkv=[given.qkv[g] for g in part],
        qm=[given.qm[g] for g in part],
        ke=[given.ke[g] for g in part],
        kt=[given.kt[g] for g in part],
        back=[given.back[g] for g in part],
        lse=[given.lse[g] for g in part],
        pulls=given.pulls,
        normed=given.normed,
        xhat=given.xhat,
        branch=given.branch,
        mixed=[given.mixed[g] for g in part],
        packs=[list(given.packs[g]) for g in part],
        one=[one],
        sums=sums,
    )
    outs = back_outs(len(part), length, width)
    body = functools.partial(back_body, [2 * g for g in part])
    return staged(body, meta, ins, outs, back_scratch(len(part), length), 8 * len(part), kept)


def turn_back_body(part, table, ins, outs, sums, *scratch):
    turned = Bag(outs.turned)
    turned.update(sums=sums)
    turn_body(table, ins.turn, turned)
    given = Bag(ins.back)
    given.update(
        back=[outs.turned.back[g] for g in part], pulls=outs.turned.pulls, branch=outs.turned.branch, one=[], sums=sums
    )
    back_body([2 * g for g in part], table, given, outs.back, *scratch)


def turn_back(meta, given, inner, two, out, cot, vectors, part, kept):
    length, width = inner.shape
    ins = Bag(
        turn=Bag(
            inner=inner,
            two=two,
            out=out,
            cot=cot,
            vectors=vectors,
            mixed=list(given.mixed),
            rest=list(given.rest),
            packs=[list(p) for p in given.packs],
        ),
        back=Bag(
            labels=given.labels,
            qkv=[given.qkv[g] for g in part],
            qm=[given.qm[g] for g in part],
            ke=[given.ke[g] for g in part],
            kt=[given.kt[g] for g in part],
            lse=[given.lse[g] for g in part],
            normed=given.normed,
            xhat=given.xhat,
            mixed=[given.mixed[g] for g in part],
            packs=[list(given.packs[g]) for g in part],
        ),
    )
    groups = len(given.mixed)
    outs = Bag(
        turned=Bag(
            layer=shape((length, width), BF16),
            pulls=shape((max(8, 2 * groups), length), F32),
            delta=shape((length, width), F32),
            branch=shape((length, width), BF16),
            back=[shape((length, PAIR), BF16)] * groups,
        ),
        back=back_outs(len(part), length, width),
    )
    scratch = [pltpu.VMEM((8, width), F32)] + back_scratch(len(part), length)
    return staged(functools.partial(turn_back_body, part), meta, ins, outs, scratch, 14, kept)


def close_body(table, ins, outs):
    length, width = ins.frames.shape
    for tile in range(length // ROWS):
        rows = pl.ds(tile * ROWS, ROWS)
        xhat, scale = centred(ins.frames[rows, :].astype(F32))
        e = ins.one[rows, :] * ins.vectors[0:1, :]
        lean = jnp.mean(e, axis=-1, keepdims=True)
        pull = jnp.mean(e * xhat, axis=-1, keepdims=True)
        outs.frames_delta[rows, :] = (ins.delta[rows, :] + scale * (e - lean - xhat * pull)).astype(BF16)


def close(meta, frames, vectors, delta, one, kept):
    ins = Bag(vectors=vectors, frames=frames, delta=delta, one=one)
    outs = Bag(frames_delta=shape(frames.shape, BF16))
    return staged(close_body, meta, ins, outs, [], 3, kept).frames_delta


def cut_body(table, ins, outs):
    size = outs.blocks[0].shape[0] - EXTRA
    rows = size * len(outs.blocks)
    place = table[0, 15]
    end = sum(p[rows:, :].astype(F32) for p in ins.pieces).astype(BF16)
    for j, block in enumerate(outs.blocks):
        at = pl.ds(pl.multiple_of(jnp.bitwise_xor(place, j) * size, size), size)
        block[:size, :] = sum(p[at, :].astype(F32) for p in ins.pieces).astype(BF16)
        block[size:, :] = end


def cut_blocks(meta, pieces, count, kept):
    rows, cols = pieces[0].shape
    block = shape(((rows - EXTRA) // count + EXTRA, cols), BF16)
    return staged(cut_body, meta, Bag(pieces=list(pieces)), Bag(blocks=[block] * count), [], 2, kept).blocks


def sum_body(table, ins, outs):
    total = sum(p[...].astype(F32) for p in ins.parts)
    size = total.shape[0] - EXTRA
    outs.extra[...] = total[size:]
    outs.block[:size, :] = total[:size].astype(BF16)
    if ins.small:
        small = ins.small[0][...]
        high = small.astype(BF16).astype(F32)
        outs.block[size:, :] = jnp.concatenate([high, small - high], axis=0).astype(BF16)


def sum_blocks(meta, parts, small, kept):
    rows, cols = parts[0].shape
    outs = Bag(block=shape((rows if small else rows - EXTRA, cols), BF16), extra=shape((EXTRA, cols), F32))
    return staged(sum_body, meta, Bag(parts=list(parts), small=list(small)), outs, [], 1, kept)


def ordered_into(table, blocks, pack_s):
    size = pack_s.shape[0] // len(blocks)
    for j, block in enumerate(blocks):
        at = pl.ds(pl.multiple_of(jnp.bitwise_xor(table[0, 15], j) * size, size), size)
        pack_s[at, :] = block[:size, :].astype(F32)


def feed_end_body(count, table, ins, outs, pack_s):
    width, hidden = outs.up.shape
    half = width // 2
    for cols, stack in zip(my_half(table, half), (ins.near, ins.far)):
        size = stack.shape[0] // count
        ordered_into(table, [stack.at[pl.ds(j * size, size)] for j in range(count)], pack_s)
        outs.up[cols, :] = pack_s[:half, :]
        for b in range(0, hidden, half):
            outs.down[b : b + half, cols] = pack_s[half:, b : b + half]
    outs.bias[...] = ins.extra[0:1, :].reshape(hidden)


def feed_end(meta, near, far, extra, count, width, hidden):
    ins = Bag(near=near, far=far, extra=extra)
    outs = Bag(up=shape((width, hidden), F32), down=shape((hidden, width), F32), bias=shape((hidden,), F32))
    return staged(
        functools.partial(feed_end_body, count), meta, ins, outs, [pltpu.VMEM((width, hidden), F32)], 3
    )


def out_end_body(table, ins, outs, pack_s):
    half = pack_s.shape[0]
    for cols, blocks in zip(my_half(table, half), (ins.blocks, ins.far)):
        ordered_into(table, blocks, pack_s)
        for i, to in enumerate((outs.query, outs.key, outs.value)):
            to[cols, :] = pack_s[:, i * PAIR : (i + 1) * PAIR]
        outs.out[:, cols] = pack_s[:, TRIPLE:].T
    row = ins.extra[0:1, :]
    outs.query_bias[...] = row[:, :PAIR].reshape(PAIR)
    outs.value_bias[...] = row[:, 2 * PAIR : TRIPLE].reshape(PAIR)
    size = ins.blocks[0].shape[0] - EXTRA
    small = sum(block[size:, :].astype(F32) for block in ins.blocks)
    small = small[:8] + small[8:]
    for i, to in enumerate(outs.small):
        to[...] = small[i : i + 1, :].reshape(to.shape[0])


def out_end(meta, blocks, far, extra, width):
    ins = Bag(blocks=list(blocks), far=list(far), extra=extra)
    outs = Bag(
        query=shape((width, PAIR), F32),
        key=shape((width, PAIR), F32),
        value=shape((width, PAIR), F32),
        out=shape((PAIR, width), F32),
        query_bias=shape((PAIR,), F32),
        value_bias=shape((PAIR,), F32),
        small=[shape((width,), F32)] * 6,
    )
    return staged(out_end_body, meta, ins, outs, [pltpu.VMEM((width // 2, 4 * PAIR), F32)], 2)


def plane_swap(value, step, size):
    return lax.ppermute(value, PLANE, [(i, i ^ step) for i in range(size)])


def dp_swap(value, step, size):
    return lax.ppermute(value, DP, [(i, i ^ step) for i in range(size)])


def to_blocks(value, half):
    rows = value.shape[0]
    if rows >= half:
        return jnp.concatenate(jnp.split(value, rows // half, axis=0), axis=1)
    return jnp.concatenate(jnp.split(value, half // rows, axis=1), axis=0)


def from_blocks(value, half):
    cols = value.shape[1]
    if cols >= half:
        return jnp.concatenate(jnp.split(value, cols // half, axis=1), axis=0)
    return jnp.concatenate(jnp.split(value, half // cols, axis=0), axis=1)


def extra_row(value):
    return jnp.pad(value[None], ((0, EXTRA - 1), (0, 0)))


def qkvo_pack(half_at, half, query, key, value, out, query_bias, value_bias):
    parts = [lax.dynamic_slice_in_dim(w, half_at, half, axis=0) for w in (query, key, value)]
    parts.append(lax.dynamic_slice_in_dim(out, half_at, half, axis=1).T)
    zero = jnp.zeros_like(query_bias)
    bias = jnp.concatenate([query_bias, zero, value_bias, zero])
    return jnp.concatenate([jnp.concatenate(parts, axis=1), extra_row(bias)], axis=0)


def feed_pack(half_at, half, up, up_bias, down):
    top = lax.dynamic_slice_in_dim(up, half_at, half, axis=0)
    low = to_blocks(lax.dynamic_slice_in_dim(down, half_at, half, axis=1), half)
    return jnp.concatenate([top, low, extra_row(up_bias)], axis=0)


def qkvo_join(shards):
    if len(shards) == 1:
        return shards[0]
    quarters = [jnp.split(s, 4, axis=1) for s in shards]
    return jnp.concatenate([q[i] for i in range(4) for q in quarters], axis=1)


def qkvo_cut(pack, count):
    if count == 1:
        return [pack]
    pieces = jnp.split(pack, 4 * count, axis=1)
    return [jnp.concatenate([pieces[i * count + s] for i in range(4)], axis=1) for s in range(count)]


def feed_join(shards, half):
    if len(shards) == 1:
        return shards[0]
    top = jnp.concatenate([s[:half] for s in shards], axis=1)
    low = jnp.concatenate([from_blocks(s[half : 2 * half], half) for s in shards], axis=0)
    end = jnp.concatenate([s[2 * half :] for s in shards], axis=1)
    return jnp.concatenate([top, to_blocks(low, half), end], axis=0)


def feed_cut(pack, count, half):
    if count == 1:
        return [pack]
    tops = jnp.split(pack[:half], count, axis=1)
    lows = jnp.split(from_blocks(pack[half : 2 * half], half), count, axis=0)
    ends = jnp.split(pack[2 * half :], count, axis=1)
    return [jnp.concatenate([t, to_blocks(l, half), e], axis=0) for t, l, e in zip(tops, lows, ends)]


def ordered(mine, other, core, axis):
    low = jnp.where(core == 0, mine, other)
    high = jnp.where(core == 0, other, mine)
    return jnp.concatenate([low, high], axis=axis)


def after(value, other):
    return lax.optimization_barrier((value, other))


def added(pieces):
    total = pieces[0].astype(F32)
    for piece in pieces[1:]:
        total += piece.astype(F32)
    return total.astype(BF16)


def z_swaps(pack, dp_size):
    return [pack] + [dp_swap(pack, k, dp_size) for k in range(2, dp_size, 2)]


def z_blocks(pack, dp_at, dp_size):
    rows, z_size = pack.shape[0] - EXTRA, dp_size // 2
    size = rows // z_size
    z_at = dp_at // 2

    def block(at):
        return jnp.concatenate([lax.dynamic_slice_in_dim(pack, at * size, size, axis=0), pack[rows:]], axis=0)

    return [block(z_at ^ k) for k in range(z_size)]


def from_z(blocks, dp_at, dp_size):
    stack = jnp.stack(blocks)
    z_at, z_size = dp_at // 2, dp_size // 2
    return jnp.concatenate([stack[z_at ^ j] for j in range(z_size)], axis=0)


def shards(
    frames,
    segment_ids,
    cotangent,
    first_gain,
    first_shift,
    query_weight,
    query_bias,
    key_weight,
    value_weight,
    value_bias,
    out_weight,
    out_bias,
    second_gain,
    second_shift,
    up_weight,
    up_bias,
    down_weight,
    down_bias,
):
    length, width = frames.shape[1:]
    half = width // 2
    planes = lax.axis_size(PLANE)
    dp_size = lax.axis_size(DP)
    dp_at = lax.axis_index(DP)
    core = dp_at % 2
    groups = width // PAIR
    per_group = planes // groups
    alone = per_group == 1
    x, dy, labels = frames[0], cotangent[0], segment_ids
    group_of = [range(g * per_group, (g + 1) * per_group) for g in range(groups)]
    last = groups - 1
    middle = list(range(1, last))
    peers = list(range(1, planes))
    late = [r for g in middle for r in group_of[g]]
    soon = list(group_of[last])
    rest = [r for r in group_of[0] if r]
    rows = (first_gain, first_shift, out_bias, second_gain, second_shift, down_bias)

    def far_half(near):
        return {r: dp_swap(v, 1, dp_size) for r, v in near.items()}

    def out_pair(g):
        return qkvo_join([near[r] for r in group_of[g]]), qkvo_join([far[r] for r in group_of[g]])

    def feed_pair(g):
        return feed_join([feed_near[r] for r in group_of[g]], half), feed_join([feed_far[r] for r in group_of[g]], half)

    if alone:
        own, other, vectors, meta = opened(
            labels,
            query_weight,
            key_weight,
            value_weight,
            out_weight,
            query_bias,
            value_bias,
            (*rows, up_bias),
        )
        near = {r: plane_swap(own, r, planes) for r in peers}
        one = first(meta, labels, x, vectors, (own, other), (up_weight, down_weight))
        near, one = after(near, one)
        far = far_half(near)
        feed_own, feed_other = one.feed
    else:
        meta = scalars(core, labels)
        zero = jnp.zeros((width,), F32)
        vectors = jnp.stack([v.astype(F32) for v in rows] + [zero] * 2)
        own, other = (
            qkvo_pack(c * half, half, query_weight, key_weight, value_weight, out_weight, query_bias, value_bias)
            for c in (core, 1 - core)
        )
        near = {r: plane_swap(own, r, planes) for r in peers}
        far = far_half(near)
        feed_own, feed_other = (feed_pack(c * half, half, up_weight, up_bias, down_weight) for c in (core, 1 - core))
    near[0], far[0] = own, other
    qkvo = [out_pair(g) for g in range(groups)]
    if not alone:
        one = first(meta, labels, x, vectors, qkvo[0], ())
    feed_near, feed_far = {0: feed_own}, {0: feed_other}
    feed_soon = {r: plane_swap(feed_own, r, planes) for r in soon + rest}
    two = second(meta, labels, one.normed, qkvo[1:], ())
    feed_soon, two = after(feed_soon, two)
    feed_near.update(feed_soon)
    feed_far.update(far_half(feed_soon))
    mixed, qkv, lse = one.mixed + two.mixed, one.qkv + two.qkv, one.lse + two.lse
    held = [two.qkv, two.lse, two.rest, one.normed]
    joined = join(meta, x, vectors, mixed, qkvo, dy, held)
    feed_far, joined = after(feed_far, joined)
    feed_own, feed_soon = after(feed_own, feed_soon)
    feed_near.update({r: plane_swap(feed_own, r, planes) for r in late})

    def chip_sum(keep, far_send):
        return (keep.astype(F32) + far_send.astype(F32)).astype(BF16)

    def across(send):
        return dp_swap(send, 1, dp_size)

    def spread(pack, g, cut):
        return [plane_swap(p, r, planes) if r else p for r, p in zip(group_of[g], cut(pack))]

    def cut_feed(pack):
        return feed_cut(pack, per_group, half)

    def cut_qkvo(pack):
        return qkvo_cut(pack, per_group)

    held += [joined.inner, two.mixed, qkvo]
    three = feed(meta, joined.normed, joined.cot, (), [feed_pair(last), feed_pair(0)], held)
    feed_late, three = after({r: feed_near[r] for r in late}, three)
    feed_near.update(feed_late)
    feed_far.update(far_half(feed_late))
    far_send = across(three.send[0])
    middle_packs, far_send = after([feed_pair(g) for g in middle], far_send)
    feed_here = spread(chip_sum(three.keep[0], far_send), last, cut_feed)
    four = feed(meta, joined.normed, joined.cot, [[three.two, three.out]], middle_packs, held)
    labels, four = after(labels, four)
    ready = prepare(meta, labels, qkv, held)
    (four, feed_here), ready = after((four, feed_here), ready)
    three_send, four.send[0] = after(three.send[1], four.send[0])
    far_sends = [across(s) for s in four.send]
    two_sum, far_sends = after(four.two, far_sends)
    for i, g in enumerate(middle):
        feed_here += spread(chip_sum(four.keep[i], far_sends[i]), g, cut_feed)

    def along_z(parts):
        return [dp_swap(p, 2 * k, dp_size) if k else p for k, p in enumerate(parts)]

    def z_cut(pieces, kept):
        if alone:
            return cut_blocks(meta, pieces, dp_size // 2, kept)
        return z_blocks(added(pieces), dp_at, dp_size)

    given = Bag(labels=labels, normed=one.normed, xhat=one.xhat, qkv=qkv, lse=lse, mixed=mixed, packs=qkvo)
    given.update(rest=one.rest + two.rest)
    far_send = across(three_send)
    given.update(ready)
    got = turn_back(meta, given, joined.inner, two_sum, four.out, dy, vectors, [last], held)
    turned = got.turned
    given.update(pulls=turned.pulls, branch=turned.branch, back=turned.back)
    held = [two.qkv, two.lse, one.normed, mixed, qkvo, turned.back, turned.branch, ready]
    got = got.back
    (feed_here, far_send), got = after((feed_here, far_send), got)
    if alone:
        feed_here += [three.keep[1], far_send]
    else:
        feed_here += spread(chip_sum(three.keep[1], far_send), 0, cut_feed)
    far_send = across(got.send[0])
    fed_parts = z_cut(feed_here, held + [got.one])
    labels, (fed_parts, far_send) = after(labels, (fed_parts, far_send))
    given.update(labels=labels)
    fed_parts = along_z(fed_parts)
    out_here = spread(chip_sum(got.keep[0], far_send), last, cut_qkvo)

    got = back(meta, given, got.one, got.sums, middle, held)
    (out_here, fed_parts), got = after((out_here, fed_parts), got)
    far_sends = [across(s) for s in got.send]
    fed_sum = sum_blocks(meta, fed_parts, (), held + [got.one])
    labels, (fed_sum, far_sends) = after(labels, (fed_sum, far_sends))
    given.update(labels=labels)
    fed_blocks = z_swaps(fed_sum.block, dp_size)
    for i, g in enumerate(middle):
        out_here += spread(chip_sum(got.keep[i], far_sends[i]), g, cut_qkvo)

    got = back(meta, given, got.one, got.sums, [0], held)
    (out_here, fed_blocks), got = after((out_here, fed_blocks), got)
    far_send, far_sums = after(across(got.send[0]), across(got.sums))
    if alone:
        out_parts = z_cut(out_here + [got.keep[0], far_send], [])
    else:
        out_here += spread(chip_sum(got.keep[0], far_send), 0, cut_qkvo)
        out_parts = z_cut(out_here, [])
    (vectors, fed_blocks), out_parts = after((vectors, fed_blocks), out_parts)
    out_parts = along_z(out_parts)
    frames_delta = close(meta, x, vectors, turned.delta, got.one, [])
    fed_near = jnp.concatenate(fed_blocks, axis=0)
    fed_far = across(fed_near)
    small, steps = got.sums + far_sums, [1 << i for i in range(planes.bit_length() - 1)]
    small += plane_swap(small, steps[0], planes)
    small, frames_delta = after(small, frames_delta)
    if alone:
        small, fed_far = after(small, fed_far)
        fed_far = feed_end(meta, fed_near, fed_far, fed_sum.extra, dp_size // 2, width, up_weight.shape[1])
    for step in steps[1:]:
        small += plane_swap(small, step, planes)
    out_parts, (fed_far, small) = after(out_parts, (fed_far, small))
    out_sum = sum_blocks(meta, out_parts, (small,) if alone else (), [])
    out_blocks = z_swaps(out_sum.block, dp_size)
    total = small
    for step in () if alone else range(1, dp_size.bit_length() - 1):
        total += dp_swap(total, 1 << step, dp_size)
    out_far = [across(b) for b in out_blocks]
    if alone:
        up_change, down_change, upbias_change = fed_far.up, fed_far.down, fed_far.bias
        ended = out_end(meta, out_blocks, out_far, out_sum.extra, width)
        query_change, key_change, value_change, out_change = ended.query, ended.key, ended.value, ended.out
        qbias_change, vbias_change, total = ended.query_bias, ended.value_bias, ended.small
    else:
        fed_near, fed_far = (from_z(jnp.split(f, dp_size // 2), dp_at, dp_size) for f in (fed_near, fed_far))
        up_change = ordered(fed_near[:half], fed_far[:half], core, 0).astype(F32)
        down_change = ordered(from_blocks(fed_near[half:], half), from_blocks(fed_far[half:], half), core, 1)
        down_change = down_change.astype(F32)
        upbias_change = fed_sum.extra[0]
        out_near, out_far = from_z(out_blocks, dp_at, dp_size), from_z(out_far, dp_at, dp_size)
        qkvo_change = ordered(out_near, out_far, core, 0).astype(F32)
        query_change, key_change, value_change, out_change = jnp.split(qkvo_change, 4, axis=1)
        qbias_change, _, vbias_change, _ = jnp.split(out_sum.extra[0], 4)
        out_change = out_change.T
    return (
        turned.layer[None],
        frames_delta[None],
        total[0],
        total[1],
        query_change,
        qbias_change,
        key_change,
        value_change,
        vbias_change,
        out_change,
        total[4],
        total[2],
        total[3],
        up_change,
        upbias_change,
        down_change,
        total[5],
    )


def solution(mesh):
    rows = P((DP, *PLANE), None, None)
    cols = P(None, PLANE)
    flat = P(PLANE)
    down = P(PLANE, None)
    every = P()
    placed = (
        rows, P((DP, *PLANE), None), rows, every, every, cols, flat, cols, cols, flat,
        down, every, every, every, cols, flat, down, every,
    )
    outs = (
        rows, rows, every, every, cols, flat, cols, cols, flat, down, every, every, every, cols, flat, down, every,
    )
    return jax.shard_map(shards, mesh=mesh, in_specs=placed, out_specs=outs, check_vma=False)
```
